32 devices in a mesh: wide: 8 (over z, x), narrow: 4 (over y, core).
Axes of the slice: x: 2, y: 2, z: 4, core: 2. Of those that a mesh axis runs over, the one named last changes fastest.
Arguments:
- projected: bfloat16 [3, 32768, 768], P(None, ('wide', 'narrow')), may hold values from -2.390625 to 2.390625
- layer_input: bfloat16 [32768, 768], P(('wide', 'narrow')), may hold values from -6 to 6
- segment_ids: int32 [32768], P(('wide', 'narrow')), may hold values from 0 to 2, as said below
- pad_mask: int32 [32768], P(('wide', 'narrow')), may hold values from 0 to 1, as said below
- roles: int32 [256, 3], P(('wide', 'narrow')), may hold values from 0 to 2, each once within a row
- labelled: int32 [256], P(('wide', 'narrow')), may hold values from 0 to 1, as said below
- out_weight: float32 [768, 768], replicated, may hold values from -1.75 to 1.75
- out_momentum: float32 [768, 768], replicated, may hold values from -7.6293945e-05 to 7.6293945e-05
- errors: float32 [32, 768, 768], P(('wide', 'narrow')), may hold values from -0.009765625 to 0.009765625
- factors: float32 [8, 768], replicated, may hold values from -6 to 6
- norm_gain: float32 [768], replicated, may hold values from 0.5 to 1.5
- position_bias: float32 [32, 12], replicated, may hold values from -3 to 3
- log_scale: float32 [1], replicated, may hold values from 3 to 3.6
- gain_momentum: float32 [768], replicated, may hold values from -0.0007324219 to 0.0007324219
- bias_momentum: float32 [32, 12], replicated, may hold values from -0.0014648438 to 0.0014648438
- scale_momentum: float32 [1], replicated, may hold values from -0.02 to 0.02
Outputs:
- updated_weight: float32 [768, 768], replicated
- weight_momentum: float32 [768, 768], replicated
- updated_errors: float32 [32, 768, 768], P(('wide', 'narrow'))
- updated_factors: float32 [8, 768], replicated
- updated_vectors: float32 [1153], replicated
- vector_momentum: float32 [1153], replicated
- loss_sum: float32 [1], replicated
- live_total: float32 [1], replicated
- grad_norm: float32 [1], replicated
The draws below stay inside these ranges and needn't reach their ends.
Inputs may be any that keep to these rules, and one draw needn't show every extreme that they name: `segment_ids`: each row holds three sentences numbered 0, 1, 2 in order, each of 8 to 40 tokens, then padding that carries number 2. `pad_mask`: 1 up to the end of the row's third sentence, 0 after it. The last triple is always labelled. `roles`: each row is a permutation of 0, 1, 2.
All inputs are finite; a program needn't handle non-finite values.
Results may differ from the reference program's by a relative error of at most 0.0011.
Values may be sent and summed in bfloat16 or wider, within the bound.
A program may use at most 128 MiB of HBM per device.

```python
import jax
import jax.numpy as jnp
import numpy as np
from jax import lax

D = 768
HEADS = 12
HEAD_DIM = 64
BUCKETS = 32
LEN = 128
RANK = 8
ROWS_DEV = 8
TRIPLES = 256
TOKENS = 32768
N_WIDE = 8
N_NARROW = 4


def sentence_layout(key):
    key = jax.random.fold_in(key, 11)
    lengths = jax.random.randint(key, (TRIPLES, 3), LEN // 16, 5 * LEN // 16 + 1)
    first_end = lengths[:, 0:1]
    second_end = first_end + lengths[:, 1:2]
    third_end = second_end + lengths[:, 2:3]
    position = jnp.arange(LEN)[None, :]
    segments = (position >= first_end).astype(jnp.int32) + (position >= second_end).astype(jnp.int32)
    present = (position < third_end).astype(jnp.int32)
    return (segments.reshape(-1), present.reshape(-1))


def draw_segment_ids(key, part):
    segments, present = sentence_layout(key)
    return segments


def draw_pad_mask(key, part):
    segments, present = sentence_layout(key)
    return present


def draw_labelled(key, part):
    key = jax.random.fold_in(key, 23)
    ticket = jax.random.randint(key, (TRIPLES,), 0, 3 * TRIPLES)
    position = jnp.arange(TRIPLES)
    chosen = (ticket < TRIPLES + 2 * position) | (position == TRIPLES - 1)
    return chosen.astype(jnp.int32)


def level_of(rng, dims, split, low, high):
    def one(axis_at, blocks):
        steps = jax.random.uniform(jax.random.fold_in(jax.random.fold_in(rng, 6), axis_at), (blocks,), jnp.float32, low / len(split), high / len(split))
        return jnp.repeat(jnp.exp(steps), dims[axis_at] // blocks).reshape((-1,) + (1,) * (len(dims) - axis_at - 1))

    level = one(*split[0])
    for cut in split[1:]:
        level = level * one(*cut)
    return level


def gaussian(own_key, dims, width, limit, cuts=(), kind=jnp.bfloat16):
    loudness = level_of(own_key, dims, cuts, -0.22, 0.18) if cuts else 1.0
    drawn = jax.random.normal(own_key, dims, jnp.float32) * width * loudness
    return jnp.minimum(jnp.maximum(drawn, -limit), limit).astype(kind)


def setup_inputs(seed: int = 0) -> dict:
    seeds = jax.random.split(jax.random.key(seed), 17)
    return {
        "projected": gaussian(seeds[0], (3, TOKENS, D), 0.4, 2.390625, ((1, 32),)),
        "layer_input": gaussian(seeds[1], (TOKENS, D), 1.0, 6.0, ((0, 32),)),
        "segment_ids": draw_segment_ids(jax.random.fold_in(seeds[16], 71), 0),
        "pad_mask": draw_pad_mask(jax.random.fold_in(seeds[16], 71), 0),
        "roles": jax.vmap(lambda own: jax.random.permutation(own, 3))(jax.random.split(seeds[4], TRIPLES)).reshape((TRIPLES, 3)).astype(jnp.int32),
        "labelled": draw_labelled(jax.random.fold_in(seeds[16], 71), 0),
        "out_weight": gaussian(seeds[6], (D, D), (D // 64) ** -0.5, 1.75, (), jnp.float32),
        "out_momentum": gaussian(seeds[7], (D, D), (0.004 / D), 7.62939453125e-05, (), jnp.float32),
        "errors": gaussian(seeds[8], (N_WIDE * N_NARROW, D, D), (0.0056 * (ROWS_DEV * LEN) ** 0.5 / TRIPLES), 0.009765625, ((0, 32),), jnp.float32),
        "factors": gaussian(seeds[9], (RANK, D), 1.0, 6.0, (), jnp.float32),
        "norm_gain": jnp.clip(1.0 + 0.1 * jax.random.normal(seeds[10], (D,), jnp.float32), 0.5, 1.5),
        "position_bias": gaussian(seeds[11], (BUCKETS, HEADS), 0.5, 3.0, (), jnp.float32),
        "log_scale": jnp.clip(jax.random.uniform(seeds[12], (1,), jnp.float32, 3.0, 3.6), 3.0, 3.6),
        "gain_momentum": gaussian(seeds[13], (D,), 0.00005, 0.0007324219, (), jnp.float32),
        "bias_momentum": gaussian(seeds[14], (BUCKETS, HEADS), 0.0001, 0.0014648438, (), jnp.float32),
        "scale_momentum": jnp.clip(jax.random.uniform(seeds[15], (1,), jnp.float32, -0.02, 0.02), -0.02, 0.02),
    }


@jax.custom_vjp
def low(v):
    return lax.optimization_barrier(v.astype(jnp.bfloat16)).astype(jnp.float32)

@jax.custom_vjp
def low_back(v):
    return v

def low_keep(v):
    return (low(v), None)

def low_pass(kept, grad):
    return (grad,)

def back_keep(v):
    return (v, None)

def back_low(kept, grad):
    return (low(grad),)
low.defvjp(low_keep, low_pass)
low_back.defvjp(back_keep, back_low)
EPSILON = 1e-06
MOMENTUM_DECAY = 0.9
CLIP_NORM = 0.01
RATE_MATRIX = 50000.0
RATE_GAIN = 4000.0
RATE_BIAS = 2000.0
RATE_SCALE = 10.0
HIGHEST_PREC = lax.Precision.HIGHEST

def bucket_onehot(length, buckets):
    relative = np.arange(length)[None, :] - np.arange(length)[:, None]
    half_count = buckets // 2
    exact_count = half_count // 2
    base_part = (relative > 0).astype(np.int64) * half_count
    distance = np.abs(relative)
    larger = exact_count + (np.log(np.maximum(distance, 1) / exact_count) / np.log(128.0 / exact_count) * (half_count - exact_count)).astype(np.int64)
    larger = np.minimum(larger, half_count - 1)
    table = base_part + np.where(distance < exact_count, distance, larger)
    return np.eye(buckets, dtype=np.float32)[table.reshape(-1)]

def orthonormal_rows(matrix):
    result_rows = []
    for index in range(matrix.shape[0]):
        vector = matrix[index]
        for earlier in result_rows:
            vector = vector - jnp.sum(vector * earlier) * earlier
        vector = vector * lax.rsqrt(jnp.sum(vector * vector) + EPSILON)
        result_rows.append(vector)
    return jnp.stack(result_rows)

def sentence_forward(proj, resid, segments, present_mask, role_rows, weight, gain, bias_full):
    query = proj[0].reshape(ROWS_DEV, LEN, HEADS, HEAD_DIM)
    keys = proj[1].reshape(ROWS_DEV, LEN, HEADS, HEAD_DIM)
    values = proj[2].reshape(ROWS_DEV, LEN, HEADS, HEAD_DIM)
    present = present_mask == 1
    allowed = (segments[:, :, None] == segments[:, None, :]) & present[:, None, :]
    scores = jnp.einsum('rihd,rjhd->rhij', query, keys, precision=HIGHEST_PREC) + bias_full[None]
    scores = jnp.where(allowed[:, None], scores, -1000000000.0)
    row_top = lax.optimization_barrier(jnp.max(scores, axis=-1, keepdims=True))
    expon = jnp.exp(scores - row_top)
    attn_probs = expon / lax.optimization_barrier(jnp.sum(expon, axis=-1, keepdims=True))
    mixed = jnp.einsum('rhij,rjhd->rihd', low(attn_probs), values, precision=HIGHEST_PREC).reshape(ROWS_DEV * LEN, D)
    mixed = low(low_back(mixed))
    branch = low_back(jnp.dot(mixed, low(weight), precision=HIGHEST_PREC))
    hidden = resid.reshape(ROWS_DEV * LEN, D) + branch
    rms_inv = lax.rsqrt(lax.optimization_barrier(jnp.mean(hidden * hidden, axis=-1, keepdims=True)) + EPSILON)
    normed = (hidden * rms_inv * gain).reshape(ROWS_DEV, LEN, D)
    member = ((segments[:, None, :] == jnp.arange(3)[None, :, None]) & present[:, None, :]).astype(jnp.float32)
    counts = lax.optimization_barrier(jnp.sum(member, axis=-1, keepdims=True))
    means = jnp.einsum('rst,rtd->rsd', member, normed, precision=HIGHEST_PREC) / counts
    unit_vec = means * lax.rsqrt(lax.optimization_barrier(jnp.sum(means * means, axis=-1, keepdims=True)) + EPSILON)
    role_pick = (role_rows[:, :, None] == jnp.arange(3)[None, None, :]).astype(jnp.float32)
    return jnp.einsum('rks,rsd->krd', role_pick, unit_vec, precision=HIGHEST_PREC)

def reference(projected, layer_input, segment_ids, pad_mask, roles, labelled, out_weight, out_momentum, errors, factors, norm_gain, position_bias, log_scale, gain_momentum, bias_momentum, scale_momentum):
    device_count = N_WIDE * N_NARROW
    proj = projected.astype(jnp.float32).reshape(3, device_count, ROWS_DEV, LEN, D).transpose(1, 0, 2, 3, 4)
    resid = layer_input.astype(jnp.float32).reshape(device_count, ROWS_DEV, LEN, D)
    segments = segment_ids.reshape(device_count, ROWS_DEV, LEN)
    present = pad_mask.reshape(device_count, ROWS_DEV, LEN)
    role_rows = roles.reshape(device_count, ROWS_DEV, 3)
    live_rows = labelled.astype(jnp.float32)
    live_total = jnp.sum(live_rows)
    table = jnp.asarray(bucket_onehot(LEN, BUCKETS))
    stacked = jnp.broadcast_to(out_weight, (device_count, D, D))

    def objective(weights, gain, bias, scale):
        bias_full = jnp.dot(table, bias, precision=HIGHEST_PREC).reshape(LEN, LEN, HEADS).transpose(2, 0, 1)

        def one_device(block):
            return sentence_forward(*block, gain, bias_full)
        picked = lax.map(jax.checkpoint(one_device), (proj, resid, segments, present, role_rows, weights))
        anchors = low(picked[:, 0].reshape(TRIPLES, D))
        cands = low(jnp.concatenate([picked[:, 1].reshape(TRIPLES, D), picked[:, 2].reshape(TRIPLES, D)], axis=0))
        raw_scores = low_back(jnp.dot(anchors, cands.T, precision=HIGHEST_PREC))
        logits = jnp.exp(scale[0]) * raw_scores
        row_top = lax.optimization_barrier(jnp.max(logits, axis=1, keepdims=True))
        log_total = row_top[:, 0] + jnp.log(lax.optimization_barrier(jnp.sum(jnp.exp(logits - row_top), axis=1)))
        own_logit = jnp.diagonal(logits)
        total = jnp.sum(live_rows * (log_total - own_logit))
        return (total / live_total, total)
    value_out, pullback, loss_sum = jax.vjp(objective, stacked, norm_gain, position_bias, log_scale, has_aux=True)
    grad_stack, gain_grad, bias_grad, scale_grad = pullback(jnp.ones((), jnp.float32))
    matrices = grad_stack + errors
    matrix_total = lax.optimization_barrier(jnp.sum(matrices, axis=0))
    factor_rows = jnp.dot(factors, matrix_total.T, precision=HIGHEST_PREC)
    ortho = orthonormal_rows(factor_rows)
    factors_new = jnp.dot(ortho, matrix_total, precision=HIGHEST_PREC)
    approx = jnp.dot(ortho.T, factors_new, precision=HIGHEST_PREC)
    vector_grad = jnp.concatenate([gain_grad, bias_grad.reshape(-1), scale_grad])
    grad_norm = jnp.sqrt(jnp.sum(approx * approx) + jnp.sum(vector_grad * vector_grad))
    clip = CLIP_NORM / jnp.maximum(grad_norm, CLIP_NORM)
    weight_mom = MOMENTUM_DECAY * out_momentum + clip * approx
    weight_new = out_weight - RATE_MATRIX * weight_mom
    errors_new = matrices - approx[None] / device_count
    vector_old = jnp.concatenate([norm_gain, position_bias.reshape(-1), log_scale])
    vector_mom_old = jnp.concatenate([gain_momentum, bias_momentum.reshape(-1), scale_momentum])
    vector_mom = MOMENTUM_DECAY * vector_mom_old + clip * vector_grad
    rates = jnp.concatenate([jnp.full((D,), RATE_GAIN, jnp.float32), jnp.full((BUCKETS * HEADS,), RATE_BIAS, jnp.float32), jnp.full((1,), RATE_SCALE, jnp.float32)])
    vector_new = vector_old - rates * vector_mom
    return (weight_new, weight_mom, errors_new, factors_new, vector_new, vector_mom, loss_sum[None], live_total[None], grad_norm[None])
```

```python
import functools

import jax
import jax.numpy as jnp
import numpy as np
from jax import lax
from jax.experimental import pallas as pl
from jax.experimental.pallas import tpu as pltpu
from jax.sharding import PartitionSpec as P

D = 768
HEADS = 12
HEAD_DIM = 64
BUCKETS = 32
LEN = 128
ROWS_DEV = 8
RANK = 8
TOK = ROWS_DEV * LEN
PAIRS = HEADS // 2
HALF = D // 2
FLAT = BUCKETS * HEADS
PACK = D + HALF
GROUP = 32
WIDTH = D + 128

EPSILON = 1e-06
MOMENTUM_DECAY = 0.9
CLIP_NORM = 0.01
RATE_MATRIX = 50000.0
RATE_GAIN = 4000.0
RATE_BIAS = 2000.0
RATE_SCALE = 10.0
MASKED = -float(2**30)
UNLABELLED = 2.0
F32 = jnp.float32
BF16 = jnp.bfloat16
MESH = pl.DeviceIdType.MESH


def diagonal_buckets():
    half_count = BUCKETS // 2
    exact_count = half_count // 2
    table = np.full((2 * LEN,), -1, np.int64)
    for k in range(2 * LEN):
        if k == LEN:
            continue
        relative = -k if k < LEN else 2 * LEN - k
        distance = abs(relative)
        larger = exact_count + int(
            np.log(np.maximum(distance, 1) / exact_count)
            / np.log(128.0 / exact_count)
            * (half_count - exact_count)
        )
        larger = min(larger, half_count - 1)
        table[k] = (half_count if relative > 0 else 0) + (
            distance if distance < exact_count else larger
        )
    return table


def diagonal_onehot():
    table = diagonal_buckets()
    return (table[:, None] == (np.arange(FLAT) // HEADS)[None, :]).astype(np.float32)


def head_mask():
    return (np.arange(16)[:, None] == (np.arange(FLAT) % HEADS)[None, :]).astype(np.float32)


def nn(left, right):
    return lax.dot_general(
        left, right, (((1,), (0,)), ((), ())), preferred_element_type=F32
    )


def nt(left, right):
    return lax.dot_general(
        left, right, (((1,), (1,)), ((), ())), preferred_element_type=F32
    )


def tn(left, right):
    return lax.dot_general(
        left, right, (((0,), (0,)), ((), ())), preferred_element_type=F32
    )


def parts_of(x):
    high = x.astype(BF16).astype(F32)
    rest = x - high
    middle = rest.astype(BF16).astype(F32)
    return high, middle, rest - middle


def stacked_parts(x):
    high, middle, low = parts_of(x)
    return jnp.concatenate([high, middle, low, jnp.zeros_like(x)], axis=0).astype(BF16)


def folded(y, rows):
    return y[0:rows] + y[rows : 2 * rows] + y[2 * rows : 3 * rows]


def looped(count, body, carry):
    if count == 1:
        return body(0, carry)
    return lax.fori_loop(0, count, body, carry)


def step_kernel(
    n_wide,
    n_narrow,
    proj_hbm,
    resid_hbm,
    weight_hbm,
    error_hbm,
    seg_ref,
    pad_ref,
    roles_ref,
    label_ref,
    factor_ref,
    gain_ref,
    bias_flat_ref,
    scale_ref,
    onehot_ref,
    head_mask_ref,
    ortho_ref,
    fnew_ref,
    vec_ref,
    live_ref,
    matrix_hbm,
    proj,
    resid,
    weight,
    error,
    weight_low,
    bias_table,
    key_extra,
    query_extra,
    member,
    member_t,
    probs,
    mixed_t,
    zed,
    rms_inv,
    branch,
    mixed_grad,
    matrix,
    matrix_high,
    matrix_low,
    gather,
    anchors_all,
    own_scores,
    diagonals,
    plane1,
    line1,
    plane2,
    line2,
    row_sem,
    resid_sem,
    load_sem,
    out_sem,
    gather_send,
    gather_recv,
    plane_send,
    plane_recv,
    line_send,
    line_recv,
):
    count = n_wide * n_narrow
    lines = n_wide // 2
    spots = 2 * n_narrow
    cross = n_narrow
    wide = lax.axis_index("wide")
    narrow = lax.axis_index("narrow")
    me = wide * n_narrow + narrow
    line = wide // 2
    side = wide % 2
    spot = side * n_narrow + narrow
    cell = side * (n_narrow // 2) + narrow // 2

    def spot_device(k):
        other = (spot + k) % spots
        return other, (line * 2 + other // n_narrow, other % n_narrow)

    def line_device(k):
        other = (line + k) % lines
        return other, (other * 2 + side, narrow)

    def cell_device(k):
        other = (cell + k) % cross
        return other // (n_narrow // 2), (other % (n_narrow // 2)) * 2 + narrow % 2

    sibling = (wide, narrow + 1 - 2 * (narrow % 2))

    row_copies = []
    for r in range(ROWS_DEV):
        rows = pl.ds(r * LEN, LEN)
        pltpu.make_async_copy(proj_hbm.at[:, rows, :], proj.at[:, rows, :], row_sem.at[r]).start()
    weight_copy = pltpu.make_async_copy(weight_hbm, weight, load_sem.at[0])
    weight_copy.start()
    resid_copy = pltpu.make_async_copy(resid_hbm, resid, resid_sem)
    resid_copy.start()
    error_copy = pltpu.make_async_copy(error_hbm.at[0], error, load_sem.at[1])
    error_copy.start()
    barrier = pltpu.get_barrier_semaphore()
    for k in range(1, spots):
        pl.semaphore_signal(barrier, inc=1, device_id=spot_device(k)[1], device_id_type=MESH)
    for k in range(1, lines):
        pl.semaphore_signal(barrier, inc=1, device_id=line_device(k)[1], device_id_type=MESH)

    onehot = onehot_ref[...]
    spread_bias = bias_flat_ref[...] * head_mask_ref[...]
    high, middle, low = parts_of(spread_bias)
    diag_bias = folded(
        nt(jnp.concatenate([high, middle, low], axis=0).astype(BF16), onehot), 16
    )
    for h in range(HEADS):
        wide_row = jnp.broadcast_to(diag_bias[h : h + 1, :], (LEN, 2 * LEN))
        bias_table[h] = pltpu.roll(wide_row, 0, 1, stride=1, stride_axis=0)[:, :LEN]

    code = jnp.where(pad_ref[...] == 1, seg_ref[...], 3).astype(F32)
    seg_f = seg_ref[...].astype(F32)
    fill = jnp.zeros((LEN - 16, LEN), F32)
    code_t = jnp.concatenate([code, seg_f, fill], axis=0).T
    roles_f = roles_ref[...].astype(F32)
    lane = lax.broadcasted_iota(jnp.int32, (1, LEN), 1)
    slot = lane % 32
    row_of = lax.broadcasted_iota(jnp.int32, (32, 1), 0)
    role_col = jnp.concatenate(
        [roles_f[:, 0:1], roles_f[:, 1:2], roles_f[:, 2:3], jnp.full((8, 1), 9.0, F32)], axis=0
    )
    sentence = lax.broadcasted_iota(jnp.int32, (1, LEN), 1).astype(F32)
    for r in range(ROWS_DEV):
        code_col = code_t[:, r : r + 1]
        seg_col = code_t[:, 8 + r : 9 + r]
        key_extra[r] = jnp.where(
            (sentence < 3.0) & (sentence != code_col), MASKED, 0.0
        ).astype(BF16)
        query_extra[r] = jnp.where(sentence == seg_col, 1.0, 0.0).astype(BF16)
        role_lane = jnp.where(
            slot < 8,
            roles_f[r : r + 1, 0:1],
            jnp.where(slot < 16, roles_f[r : r + 1, 1:2], roles_f[r : r + 1, 2:3]),
        )
        role_lane = jnp.where((slot < 24) & (slot % 8 == r), role_lane, 9.0)
        member_t[r * LEN : (r + 1) * LEN, :] = jnp.where(role_lane == code_col, 1.0, 0.0).astype(
            BF16
        )
        member[:, r * LEN : (r + 1) * LEN] = jnp.where(
            (role_col == code[r : r + 1, :]) & (row_of % 8 == r), 1.0, 0.0
        ).astype(BF16)
    counts = jnp.sum(member[...].astype(F32), axis=1, keepdims=True)[0:24]

    first = jnp.where(lane < HEAD_DIM, 1.0, 0.0).astype(BF16)
    second = jnp.where(lane < HEAD_DIM, 0.0, 1.0).astype(BF16)
    nothing = jnp.zeros((HEAD_DIM, LEN), BF16)

    def attend(r, carry):
        offset = pl.multiple_of(r * LEN, LEN)
        rows = pl.ds(offset, LEN)
        pltpu.make_async_copy(proj_hbm.at[:, rows, :], proj.at[:, rows, :], row_sem.at[r]).wait()
        key_more = key_extra[r]
        query_more = query_extra[r]
        for p in range(PAIRS):
            cols = slice(p * LEN, (p + 1) * LEN)
            query = proj[0, rows, cols]
            left = jnp.concatenate([proj[1, rows, cols], key_more], axis=1)
            right = jnp.concatenate(
                [
                    jnp.concatenate([query * first, query_more], axis=1),
                    jnp.concatenate([query * second, query_more], axis=1),
                ],
                axis=0,
            )
            scores = nt(left, right)
            low_probs = []
            for half in range(2):
                head = 2 * p + half
                part = scores[:, half * LEN : (half + 1) * LEN] + bias_table[head]
                part = jnp.exp(part - jnp.max(part, axis=0, keepdims=True))
                part = part * (1.0 / jnp.sum(part, axis=0, keepdims=True))
                probs[r * HEADS + head] = part
                low_probs.append(part.astype(BF16))
            value_t = proj[2, rows, cols].T
            left = jnp.concatenate(
                [
                    jnp.concatenate([value_t[:HEAD_DIM], nothing], axis=1),
                    jnp.concatenate([nothing, value_t[HEAD_DIM:]], axis=1),
                ],
                axis=0,
            )
            mixed_t[cols, rows] = nn(left, jnp.concatenate(low_probs, axis=0)).astype(BF16)
        return carry

    lax.fori_loop(0, ROWS_DEV, attend, 0)

    weight_copy.wait()
    weight_low[...] = weight[...].astype(BF16)
    resid_copy.wait()
    sums = jnp.zeros((32, D), F32)
    for c in range(4):
        rows = slice(c * 256, (c + 1) * 256)
        hidden = resid[rows, :].astype(F32) + tn(mixed_t[:, rows], weight_low[...])
        inv = lax.rsqrt(jnp.sum(hidden * hidden, axis=1, keepdims=True) * (1.0 / D) + EPSILON)
        zed_rows = hidden * inv
        zed[rows, :] = zed_rows
        rms_inv[rows, :] = inv
        high = zed_rows.astype(BF16)
        low = (zed_rows - high.astype(F32)).astype(BF16)
        picked = member[:, rows]
        sums = sums + (nn(picked, high) + nn(picked, low))
    gain = gain_ref[...]
    zed_mean = sums[0:24] / counts
    means = zed_mean * gain
    inverse = lax.rsqrt(jnp.sum(means * means, axis=1, keepdims=True) + EPSILON)
    unit = means * inverse

    same = lax.broadcasted_iota(jnp.int32, (8, 8), 0) == lax.broadcasted_iota(jnp.int32, (8, 8), 1)
    live_own = jnp.sum(
        jnp.where(same, label_ref[...].astype(F32), 0.0), axis=1, keepdims=True
    )
    wide_lane = lax.broadcasted_iota(jnp.int32, (8, D), 1)
    marked = jnp.where(
        live_own > 0.5, unit[0:8], jnp.where(wide_lane == 0, UNLABELLED, 0.0)
    )
    own_cands = unit[8:24].astype(BF16)
    gather[me, :, 0:D] = own_cands
    gather[me, :, D:PACK] = jnp.concatenate([marked[:, :HALF], marked[:, HALF:]], axis=0).astype(
        BF16
    )
    own_anchors = jnp.concatenate([marked, jnp.zeros_like(marked)], axis=0).astype(BF16)

    pl.semaphore_wait(barrier, spots + lines - 2)
    sends = []

    def send_block(block, device):
        copy = pltpu.make_async_remote_copy(
            src_ref=gather.at[block],
            dst_ref=gather.at[block],
            send_sem=gather_send.at[len(sends)],
            recv_sem=gather_recv.at[block],
            device_id=device,
            device_id_type=MESH,
        )
        copy.start()
        sends.append(copy)

    def await_block(block):
        pltpu.make_async_remote_copy(
            src_ref=gather.at[block],
            dst_ref=gather.at[block],
            send_sem=gather_send.at[0],
            recv_sem=gather_recv.at[block],
            device_id=sibling,
            device_id_type=MESH,
        ).wait_recv()

    for k in range(1, lines):
        send_block(me, line_device(k)[1])
    for k in range(lines):
        block_line, (block_wide, _) = line_device(k)
        block = block_wide * n_narrow + narrow
        if k:
            await_block(block)
        for j in range(1, cross):
            other_side, other_narrow = cell_device(j)
            send_block(block, (line * 2 + other_side, other_narrow))
        send_block(block, sibling)
    for k in range(lines):
        for j in range(1, cross):
            other_side, other_narrow = cell_device(j)
            block = ((line + k) % lines * 2 + other_side) * n_narrow + other_narrow
            await_block(block)
            send_block(block, sibling)

    error_copy.wait()
    factor_parts = stacked_parts(factor_ref[...])
    error_rows = error[...]
    error_high = error_rows.astype(BF16)
    error_low = (error_rows - error_high.astype(F32)).astype(BF16)
    row_part = folded(nt(factor_parts, error_high) + nt(factor_parts, error_low), RANK)

    for k in range(lines):
        for j in range(cross):
            other_side, other_narrow = cell_device(j)
            block = (
                ((line + k) % lines * 2 + other_side) * n_narrow
                + other_narrow
                + 1
                - 2 * (narrow % 2)
            )
            await_block(block)
    for copy in sends:
        copy.wait_send()

    blocks = count // GROUP
    temper = jnp.exp(scale_ref[...])

    def unpack(b, total):
        picked = gather[pl.ds(b * GROUP, GROUP), :, D:PACK].astype(F32)
        left = picked[:, 0:8, :].reshape(GROUP * 8, HALF)
        right = picked[:, 8:16, :].reshape(GROUP * 8, HALF)
        anchors_all[b] = jnp.concatenate([left, right], axis=1).astype(BF16)
        live = jnp.where(left[:, 0:1] < 1.5, 1.0, 0.0)
        return total + jnp.sum(live, axis=0, keepdims=True)

    live_total = looped(blocks, unpack, jnp.zeros((1, 1), F32))

    def cands_of(b):
        return gather[pl.ds(b * GROUP, GROUP), :, 0:D].reshape(GROUP * 16, D)

    first_lane = jnp.where(lax.broadcasted_iota(jnp.int32, (16, D), 1) == 0, 1.0, 0.0).astype(BF16)
    row16 = lax.broadcasted_iota(jnp.int32, (16, GROUP * 8), 0)
    lane16 = lax.broadcasted_iota(jnp.int32, (16, GROUP * 8), 1)
    per_live = 1.0 / live_total

    def columns(b, cand_grad):
        anchors = anchors_all[b]

        def part(c, state):
            top, total = state
            logits = temper * nt(cands_of(c), anchors)
            new_top = jnp.maximum(top, jnp.max(logits, axis=0, keepdims=True))
            total = total * jnp.exp(top - new_top) + jnp.sum(
                jnp.exp(logits - new_top), axis=0, keepdims=True
            )
            return new_top, total

        start = (jnp.full((1, GROUP * 8), -1e30, F32), jnp.zeros((1, GROUP * 8), F32))
        top, total = looped(blocks, part, start)
        log_total = top + jnp.log(total)
        live = jnp.where(nt(first_lane, anchors) < 1.5, per_live, 0.0)
        logits = temper * nt(own_cands, anchors)
        target = jnp.where(
            (row16 < 8) & (lane16 + b * (GROUP * 8) == row16 + me * ROWS_DEV), 1.0, 0.0
        )
        grad = (jnp.exp(logits - log_total) - target) * live
        return cand_grad + nn((temper * grad).astype(BF16), anchors)

    cand_grad = looped(blocks, columns, jnp.zeros((16, D), F32))

    def own_part(b, state):
        top, total = state
        logits = temper * nt(own_anchors, cands_of(b))
        own_scores[b] = logits
        new_top = jnp.maximum(top, jnp.max(logits, axis=1, keepdims=True))
        total = total * jnp.exp(top - new_top) + jnp.sum(
            jnp.exp(logits - new_top), axis=1, keepdims=True
        )
        return new_top, total

    start = (jnp.full((16, 1), -1e30, F32), jnp.zeros((16, 1), F32))
    top, total = looped(blocks, own_part, start)
    log_total = top + jnp.log(total)
    live16 = jnp.concatenate([live_own, jnp.zeros_like(live_own)], axis=0)
    row32 = lax.broadcasted_iota(jnp.int32, (16, GROUP * 16), 0)
    lane32 = lax.broadcasted_iota(jnp.int32, (16, GROUP * 16), 1)

    def own_grad(b, state):
        anchor_grad, positive, scale_grad = state
        logits = own_scores[b]
        target = jnp.where(
            (row32 < 8) & (lane32 + b * (GROUP * 16) == row32 + me * 2 * ROWS_DEV), 1.0, 0.0
        )
        positive = positive + jnp.sum(logits * target, axis=1, keepdims=True)
        grad = (jnp.exp(logits - log_total) - target) * (live16 * per_live)
        scale_grad = scale_grad + jnp.sum(grad * logits, axis=1, keepdims=True)
        anchor_grad = anchor_grad + nn((temper * grad).astype(BF16), cands_of(b))
        return anchor_grad, positive, scale_grad

    column = jnp.zeros((16, 1), F32)
    anchor_grad, positive, scale_grad = looped(
        blocks, own_grad, (jnp.zeros((16, D), F32), column, column)
    )
    loss_own = jnp.sum(live16 * (log_total - positive), axis=0, keepdims=True)
    scale_grad = jnp.sum(scale_grad, axis=0, keepdims=True)

    unit_grad = jnp.concatenate([anchor_grad[0:8], cand_grad], axis=0)
    mean_grad = inverse * (unit_grad - unit * jnp.sum(unit * unit_grad, axis=1, keepdims=True))
    gain_grad = jnp.sum(mean_grad * zed_mean, axis=0, keepdims=True)
    high, middle, low = parts_of(mean_grad / counts * gain)
    gap = jnp.zeros((8, D), F32)
    shares = jnp.concatenate(
        [high, gap, middle, gap, low, gap, jnp.zeros((32, D), F32)], axis=0
    ).astype(BF16)
    for c in range(4):
        rows = slice(c * 256, (c + 1) * 256)
        zed_grad = nn(member_t[rows, :], shares)
        zed_rows = zed[rows, :]
        level = jnp.sum(zed_grad * zed_rows, axis=1, keepdims=True) * (1.0 / D)
        branch[rows, :] = (rms_inv[rows, :] * (zed_grad - zed_rows * level)).astype(BF16)
    by_token = folded(nt(factor_parts, branch[...]), RANK)
    row_part = row_part + folded(nt(stacked_parts(by_token), mixed_t[...]), RANK)

    def send_to(buffers, mine, device, send_sem, recv_sem):
        copy = pltpu.make_async_remote_copy(
            src_ref=buffers.at[mine],
            dst_ref=buffers.at[mine],
            send_sem=send_sem,
            recv_sem=recv_sem.at[mine],
            device_id=device,
            device_id_type=MESH,
        )
        copy.start()
        return copy

    def await_from(buffers, other, send_sem, recv_sem):
        pltpu.make_async_remote_copy(
            src_ref=buffers.at[other],
            dst_ref=buffers.at[other],
            send_sem=send_sem,
            recv_sem=recv_sem.at[other],
            device_id=sibling,
            device_id_type=MESH,
        ).wait_recv()

    def start_sum(which, plane):
        return [
            send_to(plane, spot, spot_device(k)[1], plane_send.at[which, k], plane_recv.at[which])
            for k in range(1, spots)
        ]

    def finish_sum(which, plane, started, along):
        for k in range(1, spots):
            await_from(plane, spot_device(k)[0], plane_send.at[which, 0], plane_recv.at[which])
        total = plane[0]
        for k in range(1, spots):
            total = total + plane[k]
        along[line] = total
        second = [
            send_to(along, line, line_device(k)[1], line_send.at[which, k], line_recv.at[which])
            for k in range(1, lines)
        ]
        for k in range(1, lines):
            await_from(along, line_device(k)[0], line_send.at[which, 0], line_recv.at[which])
        total = along[0]
        for k in range(1, lines):
            total = total + along[k]
        for copy in started + second:
            copy.wait_send()
        return total

    lane8 = lax.broadcasted_iota(jnp.int32, (1, LEN), 1)
    scalars = jnp.where(lane8 == 0, loss_own, jnp.where(lane8 == 1, scale_grad, 0.0))
    extra = jnp.concatenate(
        [gain_grad[:, k * LEN : (k + 1) * LEN] for k in range(6)]
        + [scalars, jnp.zeros((1, LEN), F32)],
        axis=0,
    )
    plane1[spot, :, 0:D] = row_part
    plane1[spot, :, D:WIDTH] = extra
    started = start_sum(0, plane1)

    for b in range(3):
        rows = slice(b * 256, (b + 1) * 256)
        full = error[rows, :] + nn(mixed_t[rows, :], branch[...])
        matrix[rows, :] = full
        high = full.astype(BF16)
        matrix_high[rows, :] = high
        matrix_low[rows, :] = (full - high.astype(F32)).astype(BF16)
    matrix_copy = pltpu.make_async_copy(matrix, matrix_hbm, out_sem)
    matrix_copy.start()

    for c in range(4):
        rows = slice(c * 256, (c + 1) * 256)
        mixed_grad[rows, :] = nt(branch[rows, :], weight_low[...]).astype(BF16)
    row8 = lax.broadcasted_iota(jnp.int32, (8, 1), 0)
    for p in range(PAIRS):
        cols = slice(p * LEN, (p + 1) * LEN)

        def back(r, acc):
            offset = pl.multiple_of(r * LEN, LEN)
            rows = pl.ds(offset, LEN)
            grad = mixed_grad[rows, cols]
            right = jnp.concatenate([grad * first, grad * second], axis=0)
            prob_grad = nt(proj[2, rows, cols], right)
            prob = jnp.concatenate(
                [probs[r * HEADS + 2 * p], probs[r * HEADS + 2 * p + 1]], axis=1
            )
            product = prob * prob_grad
            return acc + (product - prob * jnp.sum(product, axis=0, keepdims=True))

        acc = lax.fori_loop(0, ROWS_DEV, back, jnp.zeros((LEN, 2 * LEN), F32))
        for half in range(2):
            padded = jnp.concatenate(
                [acc[:, half * LEN : (half + 1) * LEN], jnp.zeros((LEN, LEN), F32)], axis=1
            )
            sheared = padded[0:8]
            for a in range(1, LEN // 8):
                sheared = sheared + pltpu.roll(padded[8 * a : 8 * a + 8], 2 * LEN - 8 * a, 1)
            for bit in (1, 2, 4):
                moved = pltpu.roll(sheared, 2 * LEN - bit, 1)
                sheared = jnp.where((row8 & bit) != 0, moved, sheared)
            head = 2 * p + half
            diagonals[head : head + 1, :] = jnp.sum(sheared, axis=0, keepdims=True)
    diagonals[HEADS:16, :] = jnp.zeros((16 - HEADS, 2 * LEN), F32)
    high, middle, low = parts_of(diagonals[...])
    by_bucket = folded(
        nn(jnp.concatenate([high, middle, low], axis=0).astype(BF16), onehot_ref[...]), 16
    )
    bias_grad = jnp.sum(by_bucket * head_mask_ref[...], axis=0, keepdims=True)

    total = finish_sum(0, plane1, started, line1)
    vec_ref[0:8, :] = total[:, D:WIDTH]
    ortho = total[:, 0:D]
    rank_row = lax.broadcasted_iota(jnp.int32, (RANK, 1), 0)
    for k in range(RANK):
        vector = ortho[k : k + 1, :]
        dots = jnp.sum(ortho * vector, axis=1, keepdims=True)
        norm = lax.rsqrt(dots[k : k + 1, :] + EPSILON)
        vector = vector * norm
        ortho = jnp.where(
            rank_row > k, ortho - (dots * norm) * vector, jnp.where(rank_row == k, vector, ortho)
        )
    ortho_ref[...] = ortho
    ortho_parts = stacked_parts(ortho)
    plane2[spot, :, 0:D] = folded(
        nn(ortho_parts, matrix_high[...]) + nn(ortho_parts, matrix_low[...]), RANK
    )
    plane2[spot, :, D:WIDTH] = jnp.concatenate(
        [bias_grad[:, k * LEN : (k + 1) * LEN] for k in range(3)] + [jnp.zeros((5, LEN), F32)],
        axis=0,
    )
    started = start_sum(1, plane2)
    total = finish_sum(1, plane2, started, line2)
    fnew_ref[...] = total[:, 0:D]
    vec_ref[8:16, :] = total[:, D:WIDTH]
    live_ref[...] = live_total
    matrix_copy.wait()


def update_kernel(
    count,
    ortho_ref,
    fnew_ref,
    vec_ref,
    weight_ref,
    momentum_ref,
    matrix_ref,
    vector_ref,
    vector_mom_ref,
    weight_out,
    momentum_out,
    error_out,
    vector_out,
    vector_mom_out,
    loss_out,
    norm_out,
):
    step = pl.program_id(0)
    ortho = ortho_ref[...]
    fnew = fnew_ref[...]
    square = jnp.zeros((RANK, 1), F32)
    for k in range(RANK):
        left = jnp.sum(ortho * ortho[k : k + 1, :], axis=1, keepdims=True)
        right = jnp.sum(fnew * fnew[k : k + 1, :], axis=1, keepdims=True)
        square = square + left * right
    square = jnp.sum(square, axis=0, keepdims=True)
    vec = vec_ref[...]
    lane = lax.broadcasted_iota(jnp.int32, (1, LEN), 1)
    scale_row = jnp.where(lane == 0, vec[6:7, 1:2], 0.0)
    grad = jnp.concatenate(
        [vec[0:6], vec[8:11], scale_row, jnp.zeros((6, LEN), F32)], axis=0
    )
    square = square + jnp.sum(
        jnp.sum(grad * grad, axis=1, keepdims=True), axis=0, keepdims=True
    )
    norm = jnp.sqrt(square)
    clip = CLIP_NORM / jnp.maximum(norm, CLIP_NORM)

    @pl.when(step == 0)
    def _():
        row = lax.broadcasted_iota(jnp.int32, (16, 1), 0)
        rate = jnp.where(row < 6, RATE_GAIN, jnp.where(row < 9, RATE_BIAS, RATE_SCALE))
        mom = MOMENTUM_DECAY * vector_mom_ref[...] + clip * grad
        vector_mom_out[...] = mom
        vector_out[...] = vector_ref[...] - rate * mom
        loss_out[...] = vec[6:7, 0:1]
        norm_out[...] = norm

    rows = pl.ds(pl.multiple_of(step * 256, 256), 256)
    block = ortho_ref[:, rows]
    oh, om, ol = parts_of(block)
    fh, fm, fl = parts_of(fnew)
    pad = jnp.zeros((16, 256), F32)
    left = jnp.concatenate([oh, oh, om, om, oh, ol, pad], axis=0).astype(BF16)
    pad = jnp.zeros((16, D), F32)
    right = jnp.concatenate([fh, fm, fh, fm, fl, fh, pad], axis=0).astype(BF16)
    approx = tn(left, right)
    mom = MOMENTUM_DECAY * momentum_ref[...] + clip * approx
    momentum_out[...] = mom
    weight_out[...] = weight_ref[...] - RATE_MATRIX * mom
    error_out[0] = matrix_ref[...] - approx * (1.0 / count)


def local(
    n_wide,
    n_narrow,
    projected,
    layer_input,
    segment_ids,
    pad_mask,
    roles,
    labelled,
    out_weight,
    out_momentum,
    errors,
    factors,
    norm_gain,
    position_bias,
    log_scale,
    gain_momentum,
    bias_momentum,
    scale_momentum,
):
    count = n_wide * n_narrow
    lines = n_wide // 2
    spots = 2 * n_narrow
    blocks = count // GROUP
    sends = (lines - 1) + lines * n_narrow + lines * (n_narrow - 1)
    anywhere = pl.BlockSpec(memory_space=pl.ANY)
    vmem = pl.BlockSpec(memory_space=pltpu.VMEM)
    ortho, fnew, vec, live_total, matrix = pl.pallas_call(
        functools.partial(step_kernel, n_wide, n_narrow),
        out_shape=(
            jax.ShapeDtypeStruct((RANK, D), F32),
            jax.ShapeDtypeStruct((RANK, D), F32),
            jax.ShapeDtypeStruct((16, LEN), F32),
            jax.ShapeDtypeStruct((1, 1), F32),
            jax.ShapeDtypeStruct((D, D), F32),
        ),
        in_specs=[anywhere] * 4 + [vmem] * 10,
        out_specs=(vmem, vmem, vmem, vmem, anywhere),
        scratch_shapes=[
            pltpu.VMEM((3, TOK, D), BF16),
            pltpu.VMEM((TOK, D), BF16),
            pltpu.VMEM((D, D), F32),
            pltpu.VMEM((D, D), F32),
            pltpu.VMEM((D, D), BF16),
            pltpu.VMEM((HEADS, LEN, LEN), F32),
            pltpu.VMEM((ROWS_DEV, LEN, LEN), BF16),
            pltpu.VMEM((ROWS_DEV, LEN, LEN), BF16),
            pltpu.VMEM((32, TOK), BF16),
            pltpu.VMEM((TOK, LEN), BF16),
            pltpu.VMEM((ROWS_DEV * HEADS, LEN, LEN), F32),
            pltpu.VMEM((D, TOK), BF16),
            pltpu.VMEM((TOK, D), F32),
            pltpu.VMEM((TOK, 1), F32),
            pltpu.VMEM((TOK, D), BF16),
            pltpu.VMEM((TOK, D), BF16),
            pltpu.VMEM((D, D), F32),
            pltpu.VMEM((D, D), BF16),
            pltpu.VMEM((D, D), BF16),
            pltpu.VMEM((count, 16, PACK), BF16),
            pltpu.VMEM((blocks, GROUP * 8, D), BF16),
            pltpu.VMEM((blocks, 16, GROUP * 16), F32),
            pltpu.VMEM((16, 2 * LEN), F32),
            pltpu.VMEM((spots, RANK, WIDTH), F32),
            pltpu.VMEM((lines, RANK, WIDTH), F32),
            pltpu.VMEM((spots, RANK, WIDTH), F32),
            pltpu.VMEM((lines, RANK, WIDTH), F32),
            pltpu.SemaphoreType.DMA((ROWS_DEV,)),
            pltpu.SemaphoreType.DMA,
            pltpu.SemaphoreType.DMA((2,)),
            pltpu.SemaphoreType.DMA,
            pltpu.SemaphoreType.DMA((sends,)),
            pltpu.SemaphoreType.DMA((count,)),
            pltpu.SemaphoreType.DMA((2, spots)),
            pltpu.SemaphoreType.DMA((2, spots)),
            pltpu.SemaphoreType.DMA((2, lines)),
            pltpu.SemaphoreType.DMA((2, lines)),
        ],
        compiler_params=pltpu.CompilerParams(
            collective_id=0, has_side_effects=True, vmem_limit_bytes=60 * 2**20
        ),
        name="step",
    )(
        projected,
        layer_input,
        out_weight,
        errors,
        segment_ids.reshape(ROWS_DEV, LEN),
        pad_mask.reshape(ROWS_DEV, LEN),
        roles,
        labelled.reshape(1, ROWS_DEV),
        factors,
        norm_gain.reshape(1, D),
        position_bias.reshape(1, FLAT),
        log_scale.reshape(1, 1),
        jnp.asarray(diagonal_onehot(), BF16),
        jnp.asarray(head_mask()),
    )
    padding = jnp.zeros((16 * LEN - D - FLAT - 1,), F32)
    vector = jnp.concatenate([norm_gain, position_bias.reshape(-1), log_scale, padding])
    vector_mom = jnp.concatenate([gain_momentum, bias_momentum.reshape(-1), scale_momentum, padding])
    whole = lambda *shape: pl.BlockSpec(shape, lambda i: (0,) * len(shape))
    rows = pl.BlockSpec((256, D), lambda i: (i, 0))
    outs = pl.pallas_call(
        functools.partial(update_kernel, count),
        grid=(3,),
        out_shape=(
            jax.ShapeDtypeStruct((D, D), F32),
            jax.ShapeDtypeStruct((D, D), F32),
            jax.ShapeDtypeStruct((1, D, D), F32),
            jax.ShapeDtypeStruct((16, LEN), F32),
            jax.ShapeDtypeStruct((16, LEN), F32),
            jax.ShapeDtypeStruct((1, 1), F32),
            jax.ShapeDtypeStruct((1, 1), F32),
        ),
        in_specs=[
            whole(RANK, D),
            whole(RANK, D),
            whole(16, LEN),
            rows,
            rows,
            rows,
            whole(16, LEN),
            whole(16, LEN),
        ],
        out_specs=(
            rows,
            rows,
            pl.BlockSpec((1, 256, D), lambda i: (0, i, 0)),
            whole(16, LEN),
            whole(16, LEN),
            whole(1, 1),
            whole(1, 1),
        ),
        name="update",
    )(
        ortho,
        fnew,
        vec,
        out_weight,
        out_momentum,
        matrix,
        vector.reshape(16, LEN),
        vector_mom.reshape(16, LEN),
    )
    weight_new, weight_mom, errors_new, vec_new, vec_mom, loss, norm = outs
    size = D + FLAT + 1
    return (
        weight_new,
        weight_mom,
        errors_new,
        fnew,
        vec_new.reshape(-1)[:size],
        vec_mom.reshape(-1)[:size],
        loss.reshape(1),
        live_total.reshape(1),
        norm.reshape(1),
    )


def solution(mesh):
    both = ("wide", "narrow")
    in_specs = (
        P(None, both, None),
        P(both, None),
        P(both),
        P(both),
        P(both, None),
        P(both),
        P(),
        P(),
        P(both, None, None),
        P(),
        P(),
        P(),
        P(),
        P(),
        P(),
        P(),
    )
    out_specs = (P(), P(), P(both, None, None), P(), P(), P(), P(), P(), P())
    return jax.shard_map(
        functools.partial(local, mesh.shape["wide"], mesh.shape["narrow"]),
        mesh=mesh,
        in_specs=in_specs,
        out_specs=out_specs,
        check_vma=False,
    )
```

```python
import functools

import jax
import jax.numpy as jnp
import numpy as np
from jax import lax
from jax.experimental import pallas as pl
from jax.experimental.pallas import tpu as pltpu
from jax.sharding import PartitionSpec as P

D = 768
HEADS = 12
HEAD_DIM = 64
BUCKETS = 32
LEN = 128
ROWS_DEV = 8
RANK = 8
TOK = ROWS_DEV * LEN
PAIRS = HEADS // 2
HALF = D // 2
FLAT = BUCKETS * HEADS
PACK = D + HALF
GROUP = 32
WIDTH = D + 128

EPSILON = 1e-06
MOMENTUM_DECAY = 0.9
CLIP_NORM = 0.01
RATE_MATRIX = 50000.0
RATE_GAIN = 4000.0
RATE_BIAS = 2000.0
RATE_SCALE = 10.0
MASKED = -float(2**30)
UNLABELLED = 2.0
F32 = jnp.float32
BF16 = jnp.bfloat16
MESH = pl.DeviceIdType.MESH


def diagonal_buckets():
    half_count = BUCKETS // 2
    exact_count = half_count // 2
    table = np.full((2 * LEN,), -1, np.int64)
    for k in range(2 * LEN):
        if k == LEN:
            continue
        relative = -k if k < LEN else 2 * LEN - k
        distance = abs(relative)
        larger = exact_count + int(
            np.log(np.maximum(distance, 1) / exact_count)
            / np.log(128.0 / exact_count)
            * (half_count - exact_count)
        )
        larger = min(larger, half_count - 1)
        table[k] = (half_count if relative > 0 else 0) + (
            distance if distance < exact_count else larger
        )
    return table


def diagonal_onehot(width):
    spread = np.arange(width) // (width // BUCKETS)
    return (diagonal_buckets()[:, None] == spread[None, :]).astype(np.float32)


def bucket_spread():
    return (np.arange(BUCKETS)[:, None] == (np.arange(FLAT) // HEADS)[None, :]).astype(np.float32)


def head_mask():
    return (np.arange(16)[:, None] == (np.arange(FLAT) % HEADS)[None, :]).astype(np.float32)


def nn(left, right):
    return lax.dot_general(
        left, right, (((1,), (0,)), ((), ())), preferred_element_type=F32
    )


def nt(left, right):
    return lax.dot_general(
        left, right, (((1,), (1,)), ((), ())), preferred_element_type=F32
    )


def tn(left, right):
    return lax.dot_general(
        left, right, (((0,), (0,)), ((), ())), preferred_element_type=F32
    )


def parts_of(x):
    high = x.astype(BF16).astype(F32)
    rest = x - high
    middle = rest.astype(BF16).astype(F32)
    return high, middle, rest - middle


def stacked_parts(x):
    high, middle, low = parts_of(x)
    return jnp.concatenate([high, middle, low, jnp.zeros_like(x)], axis=0).astype(BF16)


def folded(y, rows):
    return y[0:rows] + y[rows : 2 * rows] + y[2 * rows : 3 * rows]


def looped(count, body, carry):
    if count == 1:
        return body(0, carry)
    return lax.fori_loop(0, count, body, carry)


def step_kernel(
    n_wide,
    n_narrow,
    proj_hbm,
    resid_hbm,
    weight_hbm,
    error_hbm,
    seg_hbm,
    pad_hbm,
    roles_hbm,
    label_hbm,
    factor_hbm,
    gain_hbm,
    gain_mom_hbm,
    bias_hbm,
    bias_mom_hbm,
    scale_hbm,
    scale_mom_hbm,
    onehot_hbm,
    spread_hbm,
    diagonal_hbm,
    head_mask_hbm,
    small_ref,
    matrix_hbm,
    seg_ref,
    pad_ref,
    roles_ref,
    label_ref,
    factor_ref,
    gain_ref,
    gain_mom_ref,
    bias_ref,
    bias_mom_ref,
    scale_ref,
    scale_mom_ref,
    onehot_ref,
    spread_ref,
    diagonal_ref,
    head_mask_ref,
    small_sem,
    proj,
    resid,
    weight,
    error,
    weight_low,
    bias_table,
    key_extra,
    query_extra,
    member,
    member_t,
    probs,
    score_rows,
    prob_rows,
    mixed_t,
    zed,
    zed_high,
    zed_low,
    rms_inv,
    matrix,
    matrix_high,
    matrix_low,
    gather,
    anchors_all,
    own_scores,
    diagonals,
    plane1,
    line1,
    plane2,
    line2,
    row_sem,
    resid_sem,
    load_sem,
    out_sem,
    gather_send,
    gather_recv,
    plane_send,
    plane_recv,
    line_send,
    line_recv,
):
    count = n_wide * n_narrow
    lines = n_wide // 2
    spots = 2 * n_narrow
    cross = n_narrow
    wide = lax.axis_index("wide")
    narrow = lax.axis_index("narrow")
    me = wide * n_narrow + narrow
    line = wide // 2
    side = wide % 2
    spot = side * n_narrow + narrow
    cell = side * (n_narrow // 2) + narrow // 2

    def spot_device(k):
        other = (spot + k) % spots
        return other, (line * 2 + other // n_narrow, other % n_narrow)

    def line_device(k):
        other = (line + k) % lines
        return other, (other * 2 + side, narrow)

    def cell_device(k):
        other = (cell + k) % cross
        return other // (n_narrow // 2), (other % (n_narrow // 2)) * 2 + narrow % 2

    sibling = (wide, narrow + 1 - 2 * (narrow % 2))

    small_copies = [
        pltpu.make_async_copy(source, target, small_sem.at[k])
        for k, (source, target) in enumerate(
            (
                (seg_hbm, seg_ref),
                (pad_hbm, pad_ref),
                (roles_hbm, roles_ref),
                (label_hbm, label_ref),
                (factor_hbm, factor_ref),
                (gain_hbm, gain_ref),
                (gain_mom_hbm, gain_mom_ref),
                (bias_hbm, bias_ref),
                (bias_mom_hbm, bias_mom_ref),
                (scale_hbm, scale_ref),
                (scale_mom_hbm, scale_mom_ref),
                (onehot_hbm, onehot_ref),
                (spread_hbm, spread_ref),
                (diagonal_hbm, diagonal_ref),
                (head_mask_hbm, head_mask_ref),
            )
        )
    ]
    for copy in small_copies:
        copy.start()
    for r in range(ROWS_DEV):
        rows = pl.ds(r * LEN, LEN)
        pltpu.make_async_copy(proj_hbm.at[:, rows, :], proj.at[:, rows, :], row_sem.at[r]).start()
    weight_copy = pltpu.make_async_copy(weight_hbm, weight, load_sem.at[0])
    weight_copy.start()
    resid_copy = pltpu.make_async_copy(resid_hbm, resid, resid_sem)
    resid_copy.start()
    error_copy = pltpu.make_async_copy(error_hbm.at[0], error, load_sem.at[1])
    error_copy.start()
    barrier = pltpu.get_barrier_semaphore()
    for k in range(1, spots):
        pl.semaphore_signal(barrier, inc=1, device_id=spot_device(k)[1], device_id_type=MESH)
    for k in range(1, lines):
        pl.semaphore_signal(barrier, inc=1, device_id=line_device(k)[1], device_id_type=MESH)

    for copy in small_copies:
        copy.wait()
    high, middle, low = parts_of(bias_ref[...])
    gap = jnp.zeros((4, BUCKETS), F32)
    diag_bias = folded(
        nt(
            jnp.concatenate([high, gap, middle, gap, low, gap], axis=0).astype(BF16),
            diagonal_ref[...],
        ),
        16,
    )
    row8 = lax.broadcasted_iota(jnp.int32, (8, 1), 0)
    for h in range(HEADS):
        sheared = jnp.broadcast_to(diag_bias[h : h + 1, :], (8, 2 * LEN))
        for bit in (1, 2, 4):
            sheared = jnp.where((row8 & bit) != 0, pltpu.roll(sheared, bit, 1), sheared)
        bias_table[h, 0:8, :] = sheared[:, :LEN]
        for a in range(1, LEN // 8):
            bias_table[h, 8 * a : 8 * a + 8, :] = pltpu.roll(sheared, 8 * a, 1)[:, :LEN]

    code = jnp.where(pad_ref[...] == 1, seg_ref[...], 3).astype(F32)
    seg_f = seg_ref[...].astype(F32)
    fill = jnp.zeros((LEN - 16, LEN), F32)
    code_t = jnp.concatenate([code, seg_f, fill], axis=0).T
    roles_f = roles_ref[...].astype(F32)
    lane = lax.broadcasted_iota(jnp.int32, (1, LEN), 1)
    slot = lane % 32
    row_of = lax.broadcasted_iota(jnp.int32, (32, 1), 0)
    same = lax.broadcasted_iota(jnp.int32, (8, 8), 0) == lax.broadcasted_iota(jnp.int32, (8, 8), 1)

    def column_of(row):
        return jnp.sum(jnp.where(same, row, 0.0), axis=1, keepdims=True)

    role_col = jnp.concatenate(
        [column_of(roles_f[k : k + 1, :]) for k in range(3)] + [jnp.full((8, 1), 9.0, F32)], axis=0
    )
    sentence = lax.broadcasted_iota(jnp.int32, (1, LEN), 1).astype(F32)
    for r in range(ROWS_DEV):
        code_col = code_t[:, r : r + 1]
        seg_col = code_t[:, 8 + r : 9 + r]
        key_extra[r] = jnp.where(
            (sentence < 3.0) & (sentence != code_col), MASKED, 0.0
        ).astype(BF16)
        query_extra[r] = jnp.where(sentence == seg_col, 1.0, 0.0).astype(BF16)
        role_lane = jnp.where(
            slot < 8,
            roles_f[0:1, r : r + 1],
            jnp.where(slot < 16, roles_f[1:2, r : r + 1], roles_f[2:3, r : r + 1]),
        )
        role_lane = jnp.where((slot < 24) & (slot % 8 == r), role_lane, 9.0)
        member_t[r * LEN : (r + 1) * LEN, :] = jnp.where(role_lane == code_col, 1.0, 0.0).astype(
            BF16
        )
        member[:, r * LEN : (r + 1) * LEN] = jnp.where(
            (role_col == code[r : r + 1, :]) & (row_of % 8 == r), 1.0, 0.0
        ).astype(BF16)
    counts = jnp.sum(member[...].astype(F32), axis=1, keepdims=True)[0:24]

    first = jnp.where(lane < HEAD_DIM, 1.0, 0.0).astype(BF16)
    second = jnp.where(lane < HEAD_DIM, 0.0, 1.0).astype(BF16)
    nothing = jnp.zeros((HEAD_DIM, LEN), BF16)

    def rows_of(r):
        return pl.ds(r * LEN if isinstance(r, int) else pl.multiple_of(r * LEN, LEN), LEN)

    def arrive(r):
        rows = rows_of(r)
        pltpu.make_async_copy(proj_hbm.at[:, rows, :], proj.at[:, rows, :], row_sem.at[r]).wait()

    def score(r, p, k):
        rows = rows_of(r)
        cols = slice(p * LEN, (p + 1) * LEN)
        query = proj[0, rows, cols]
        query_more = query_extra[r]
        left = jnp.concatenate([proj[1, rows, cols], key_extra[r]], axis=1)
        right = jnp.concatenate(
            [
                jnp.concatenate([query * first, query_more], axis=1),
                jnp.concatenate([query * second, query_more], axis=1),
            ],
            axis=0,
        )
        score_rows[k, p] = nt(left, right)

    def soften(r, p, k):
        for half in range(2):
            head = 2 * p + half
            part = score_rows[k, p, :, half * LEN : (half + 1) * LEN] + bias_table[head]
            part = jnp.exp(part - jnp.max(part, axis=0, keepdims=True))
            part = part * (1.0 / jnp.sum(part, axis=0, keepdims=True))
            probs[r * HEADS + head] = part
            prob_rows[k, p, half * LEN : (half + 1) * LEN, :] = part.astype(BF16)

    def mix(r, p, k):
        rows = rows_of(r)
        cols = slice(p * LEN, (p + 1) * LEN)
        value_t = proj[2, rows, cols].T
        left = jnp.concatenate(
            [
                jnp.concatenate([value_t[:HEAD_DIM], nothing], axis=1),
                jnp.concatenate([nothing, value_t[HEAD_DIM:]], axis=1),
            ],
            axis=0,
        )
        mixed_t[cols, rows] = nn(left, prob_rows[k, p]).astype(BF16)

    arrive(0)
    for p in range(PAIRS):
        score(0, p, 0)
    arrive(1)
    for p in range(PAIRS):
        score(1, p, 1)
        soften(0, p, 0)

    def attend(i, carry):
        r = 2 * i + 2
        arrive(r)
        for p in range(PAIRS):
            score(r, p, 0)
            mix(r - 2, p, 0)
            soften(r - 1, p, 1)
        arrive(r + 1)
        for p in range(PAIRS):
            score(r + 1, p, 1)
            mix(r - 1, p, 1)
            soften(r, p, 0)
        return carry

    lax.fori_loop(0, ROWS_DEV // 2 - 1, attend, 0)
    for p in range(PAIRS):
        mix(ROWS_DEV - 2, p, 0)
        soften(ROWS_DEV - 1, p, 1)
    for p in range(PAIRS):
        mix(ROWS_DEV - 1, p, 1)

    weight_copy.wait()
    weight_low[...] = weight[...].astype(BF16)
    resid_copy.wait()
    for c in range(4):
        rows = slice(c * 256, (c + 1) * 256)
        zed[rows, :] = resid[rows, :].astype(F32) + tn(mixed_t[:, rows], weight_low[...])

    for b in range(TOK // 32):
        rows = slice(b * 32, (b + 1) * 32)
        hidden = zed[rows, :]
        inv = lax.rsqrt(jnp.sum(hidden * hidden, axis=1, keepdims=True) * (1.0 / D) + EPSILON)
        hidden = hidden * inv
        zed[rows, :] = hidden
        rms_inv[rows, :] = inv
        high = hidden.astype(BF16)
        zed_high[rows, :] = high
        zed_low[rows, :] = (hidden - high.astype(F32)).astype(BF16)
    sums = nn(member[...], zed_high[...]) + nn(member[...], zed_low[...])
    gain_rows = gain_ref[...]
    gain = jnp.concatenate([gain_rows[k : k + 1, :] for k in range(6)], axis=1)
    zed_mean = sums[0:24] / counts
    means = zed_mean * gain
    inverse = lax.rsqrt(jnp.sum(means * means, axis=1, keepdims=True) + EPSILON)
    unit = means * inverse

    live_own = column_of(label_ref[...].astype(F32))
    wide_lane = lax.broadcasted_iota(jnp.int32, (8, D), 1)
    marked = jnp.where(
        live_own > 0.5, unit[0:8], jnp.where(wide_lane == 0, UNLABELLED, 0.0)
    )
    own_cands = unit[8:24].astype(BF16)
    gather[me, :, 0:D] = own_cands
    gather[me, :, D:PACK] = jnp.concatenate([marked[:, :HALF], marked[:, HALF:]], axis=0).astype(
        BF16
    )
    own_anchors = jnp.concatenate([marked, jnp.zeros_like(marked)], axis=0).astype(BF16)

    pl.semaphore_wait(barrier, spots + lines - 2)
    sends = []

    def send_block(block, device):
        copy = pltpu.make_async_remote_copy(
            src_ref=gather.at[block],
            dst_ref=gather.at[block],
            send_sem=gather_send.at[len(sends)],
            recv_sem=gather_recv.at[block],
            device_id=device,
            device_id_type=MESH,
        )
        copy.start()
        sends.append(copy)

    def await_block(block):
        pltpu.make_async_remote_copy(
            src_ref=gather.at[block],
            dst_ref=gather.at[block],
            send_sem=gather_send.at[0],
            recv_sem=gather_recv.at[block],
            device_id=sibling,
            device_id_type=MESH,
        ).wait_recv()

    for k in range(1, lines):
        send_block(me, line_device(k)[1])
    for k in range(lines):
        block_line, (block_wide, _) = line_device(k)
        block = block_wide * n_narrow + narrow
        if k:
            await_block(block)
        for j in range(1, cross):
            other_side, other_narrow = cell_device(j)
            send_block(block, (line * 2 + other_side, other_narrow))
        send_block(block, sibling)
    for k in range(lines):
        for j in range(1, cross):
            other_side, other_narrow = cell_device(j)
            block = ((line + k) % lines * 2 + other_side) * n_narrow + other_narrow
            await_block(block)
            send_block(block, sibling)

    error_copy.wait()
    factor_parts = stacked_parts(factor_ref[...])
    error_rows = error[...]
    error_high = error_rows.astype(BF16)
    error_low = (error_rows - error_high.astype(F32)).astype(BF16)
    row_part = folded(nt(factor_parts, error_high) + nt(factor_parts, error_low), RANK)

    def flat_bias(x):
        high, middle, low = parts_of(x)
        spread = folded(
            nn(
                jnp.concatenate([high, gap, middle, gap, low, gap], axis=0).astype(BF16),
                spread_ref[...],
            ),
            16,
        )
        return jnp.sum(spread * head_mask_ref[...], axis=0, keepdims=True)

    def packed(gain_part, bias_part, scale_part):
        return jnp.concatenate(
            [gain_part]
            + [bias_part[:, k * LEN : (k + 1) * LEN] for k in range(3)]
            + [jnp.where(lane == 0, scale_part, 0.0), jnp.zeros((6, LEN), F32)],
            axis=0,
        )

    small_ref[16:32, LEN : 2 * LEN] = packed(gain_rows, flat_bias(bias_ref[...]), scale_ref[...])
    small_ref[16:32, 2 * LEN : 3 * LEN] = packed(gain_mom_ref[...], flat_bias(bias_mom_ref[...]), scale_mom_ref[...])

    for k in range(lines):
        for j in range(cross):
            other_side, other_narrow = cell_device(j)
            block = (
                ((line + k) % lines * 2 + other_side) * n_narrow
                + other_narrow
                + 1
                - 2 * (narrow % 2)
            )
            await_block(block)
    for copy in sends:
        copy.wait_send()

    blocks = count // GROUP
    temper = jnp.exp(scale_ref[...])

    def unpack(b, total):
        picked = gather[pl.ds(b * GROUP, GROUP), :, D:PACK].astype(F32)
        left = picked[:, 0:8, :].reshape(GROUP * 8, HALF)
        right = picked[:, 8:16, :].reshape(GROUP * 8, HALF)
        anchors_all[b] = jnp.concatenate([left, right], axis=1).astype(BF16)
        live = jnp.where(left[:, 0:1] < 1.5, 1.0, 0.0)
        return total + jnp.sum(live, axis=0, keepdims=True)

    live_total = looped(blocks, unpack, jnp.zeros((1, 1), F32))

    def cands_of(b):
        return gather[pl.ds(b * GROUP, GROUP), :, 0:D].reshape(GROUP * 16, D)

    first_lane = jnp.where(lax.broadcasted_iota(jnp.int32, (16, D), 1) == 0, 1.0, 0.0).astype(BF16)
    row16 = lax.broadcasted_iota(jnp.int32, (16, GROUP * 8), 0)
    lane16 = lax.broadcasted_iota(jnp.int32, (16, GROUP * 8), 1)
    per_live = 1.0 / live_total

    def columns(b, cand_grad):
        anchors = anchors_all[b]

        def part(c, state):
            top, total = state
            logits = temper * nt(cands_of(c), anchors)
            new_top = jnp.maximum(top, jnp.max(logits, axis=0, keepdims=True))
            total = total * jnp.exp(top - new_top) + jnp.sum(
                jnp.exp(logits - new_top), axis=0, keepdims=True
            )
            return new_top, total

        start = (jnp.full((1, GROUP * 8), -1e30, F32), jnp.zeros((1, GROUP * 8), F32))
        top, total = looped(blocks, part, start)
        log_total = top + jnp.log(total)
        live = jnp.where(nt(first_lane, anchors) < 1.5, per_live, 0.0)
        logits = temper * nt(own_cands, anchors)
        target = jnp.where(
            (row16 < 8) & (lane16 + b * (GROUP * 8) == row16 + me * ROWS_DEV), 1.0, 0.0
        )
        grad = (jnp.exp(logits - log_total) - target) * live
        return cand_grad + nn((temper * grad).astype(BF16), anchors)

    cand_grad = looped(blocks, columns, jnp.zeros((16, D), F32))

    def own_part(b, state):
        top, total = state
        logits = temper * nt(own_anchors, cands_of(b))
        own_scores[b] = logits
        new_top = jnp.maximum(top, jnp.max(logits, axis=1, keepdims=True))
        total = total * jnp.exp(top - new_top) + jnp.sum(
            jnp.exp(logits - new_top), axis=1, keepdims=True
        )
        return new_top, total

    start = (jnp.full((16, 1), -1e30, F32), jnp.zeros((16, 1), F32))
    top, total = looped(blocks, own_part, start)
    log_total = top + jnp.log(total)
    live16 = jnp.concatenate([live_own, jnp.zeros_like(live_own)], axis=0)
    row32 = lax.broadcasted_iota(jnp.int32, (16, GROUP * 16), 0)
    lane32 = lax.broadcasted_iota(jnp.int32, (16, GROUP * 16), 1)

    def own_grad(b, state):
        anchor_grad, positive, scale_grad = state
        logits = own_scores[b]
        target = jnp.where(
            (row32 < 8) & (lane32 + b * (GROUP * 16) == row32 + me * 2 * ROWS_DEV), 1.0, 0.0
        )
        positive = positive + jnp.sum(logits * target, axis=1, keepdims=True)
        grad = (jnp.exp(logits - log_total) - target) * (live16 * per_live)
        scale_grad = scale_grad + jnp.sum(grad * logits, axis=1, keepdims=True)
        anchor_grad = anchor_grad + nn((temper * grad).astype(BF16), cands_of(b))
        return anchor_grad, positive, scale_grad

    column = jnp.zeros((16, 1), F32)
    anchor_grad, positive, scale_grad = looped(
        blocks, own_grad, (jnp.zeros((16, D), F32), column, column)
    )
    loss_own = jnp.sum(live16 * (log_total - positive), axis=0, keepdims=True)
    scale_grad = jnp.sum(scale_grad, axis=0, keepdims=True)

    branch, mixed_grad = zed_high, zed_low
    unit_grad = jnp.concatenate([anchor_grad[0:8], cand_grad], axis=0)
    mean_grad = inverse * (unit_grad - unit * jnp.sum(unit * unit_grad, axis=1, keepdims=True))
    gain_grad = jnp.sum(mean_grad * zed_mean, axis=0, keepdims=True)
    high, middle, low = parts_of(mean_grad / counts * gain)
    wide_gap = jnp.zeros((8, D), F32)
    shares = jnp.concatenate(
        [high, wide_gap, middle, wide_gap, low, wide_gap, jnp.zeros((32, D), F32)], axis=0
    ).astype(BF16)
    for c in range(4):
        rows = slice(c * 256, (c + 1) * 256)
        zed_grad = nn(member_t[rows, :], shares)
        zed_rows = zed[rows, :]
        level = jnp.sum(zed_grad * zed_rows, axis=1, keepdims=True) * (1.0 / D)
        branch[rows, :] = (rms_inv[rows, :] * (zed_grad - zed_rows * level)).astype(BF16)
    by_token = folded(nt(factor_parts, branch[...]), RANK)
    row_part = row_part + folded(nt(stacked_parts(by_token), mixed_t[...]), RANK)

    def send_to(buffers, mine, device, send_sem, recv_sem):
        copy = pltpu.make_async_remote_copy(
            src_ref=buffers.at[mine],
            dst_ref=buffers.at[mine],
            send_sem=send_sem,
            recv_sem=recv_sem.at[mine],
            device_id=device,
            device_id_type=MESH,
        )
        copy.start()
        return copy

    def await_from(buffers, other, send_sem, recv_sem):
        pltpu.make_async_remote_copy(
            src_ref=buffers.at[other],
            dst_ref=buffers.at[other],
            send_sem=send_sem,
            recv_sem=recv_sem.at[other],
            device_id=sibling,
            device_id_type=MESH,
        ).wait_recv()

    def start_sum(which, plane):
        return [
            send_to(plane, spot, spot_device(k)[1], plane_send.at[which, k], plane_recv.at[which])
            for k in range(1, spots)
        ]

    def finish_sum(which, plane, started, along):
        for k in range(1, spots):
            await_from(plane, spot_device(k)[0], plane_send.at[which, 0], plane_recv.at[which])
        total = plane[0]
        for k in range(1, spots):
            total = total + plane[k]
        along[line] = total
        second = [
            send_to(along, line, line_device(k)[1], line_send.at[which, k], line_recv.at[which])
            for k in range(1, lines)
        ]
        for k in range(1, lines):
            await_from(along, line_device(k)[0], line_send.at[which, 0], line_recv.at[which])
        total = along[0]
        for k in range(1, lines):
            total = total + along[k]
        for copy in started + second:
            copy.wait_send()
        return total

    scalars = jnp.where(lane == 0, loss_own, jnp.where(lane == 1, scale_grad, 0.0))
    extra = jnp.concatenate(
        [gain_grad[:, k * LEN : (k + 1) * LEN] for k in range(6)]
        + [scalars, jnp.zeros((1, LEN), F32)],
        axis=0,
    )
    plane1[spot, :, 0:D] = row_part
    plane1[spot, :, D:WIDTH] = extra
    started = start_sum(0, plane1)

    for b in range(3):
        rows = slice(b * 256, (b + 1) * 256)
        full = error[rows, :] + nn(mixed_t[rows, :], branch[...])
        matrix[rows, :] = full
        high = full.astype(BF16)
        matrix_high[rows, :] = high
        matrix_low[rows, :] = (full - high.astype(F32)).astype(BF16)
    matrix_copy = pltpu.make_async_copy(matrix, matrix_hbm, out_sem)
    matrix_copy.start()

    for c in range(4):
        rows = slice(c * 256, (c + 1) * 256)
        mixed_grad[rows, :] = nt(branch[rows, :], weight_low[...]).astype(BF16)
    for p in range(PAIRS):
        cols = slice(p * LEN, (p + 1) * LEN)

        def back(r, acc):
            offset = pl.multiple_of(r * LEN, LEN)
            rows = pl.ds(offset, LEN)
            grad = mixed_grad[rows, cols]
            right = jnp.concatenate([grad * first, grad * second], axis=0)
            prob_grad = nt(proj[2, rows, cols], right)
            prob = jnp.concatenate(
                [probs[r * HEADS + 2 * p], probs[r * HEADS + 2 * p + 1]], axis=1
            )
            product = prob * prob_grad
            return acc + (product - prob * jnp.sum(product, axis=0, keepdims=True))

        acc = lax.fori_loop(0, ROWS_DEV, back, jnp.zeros((LEN, 2 * LEN), F32), unroll=True)
        for half in range(2):
            padded = jnp.concatenate(
                [acc[:, half * LEN : (half + 1) * LEN], jnp.zeros((LEN, LEN), F32)], axis=1
            )
            sheared = padded[0:8]
            for a in range(1, LEN // 8):
                sheared = sheared + pltpu.roll(padded[8 * a : 8 * a + 8], 2 * LEN - 8 * a, 1)
            for bit in (1, 2, 4):
                moved = pltpu.roll(sheared, 2 * LEN - bit, 1)
                sheared = jnp.where((row8 & bit) != 0, moved, sheared)
            head = 2 * p + half
            diagonals[head : head + 1, :] = jnp.sum(sheared, axis=0, keepdims=True)
    diagonals[HEADS:16, :] = jnp.zeros((16 - HEADS, 2 * LEN), F32)
    high, middle, low = parts_of(diagonals[...])
    by_bucket = folded(
        nn(jnp.concatenate([high, middle, low], axis=0).astype(BF16), onehot_ref[...]), 16
    )
    bias_grad = jnp.sum(by_bucket * head_mask_ref[...], axis=0, keepdims=True)

    total = finish_sum(0, plane1, started, line1)
    small_ref[16:24, 0:LEN] = total[:, D:WIDTH]
    ortho = total[:, 0:D]
    rank_row = lax.broadcasted_iota(jnp.int32, (RANK, 1), 0)
    for k in range(RANK):
        vector = ortho[k : k + 1, :]
        dots = jnp.sum(ortho * vector, axis=1, keepdims=True)
        norm = lax.rsqrt(dots[k : k + 1, :] + EPSILON)
        vector = vector * norm
        ortho = jnp.where(
            rank_row > k, ortho - (dots * norm) * vector, jnp.where(rank_row == k, vector, ortho)
        )
    small_ref[0:8, :] = ortho
    ortho_parts = stacked_parts(ortho)
    plane2[spot, :, 0:D] = folded(
        nn(ortho_parts, matrix_high[...]) + nn(ortho_parts, matrix_low[...]), RANK
    )
    plane2[spot, :, D:WIDTH] = jnp.concatenate(
        [bias_grad[:, k * LEN : (k + 1) * LEN] for k in range(3)] + [jnp.zeros((5, LEN), F32)],
        axis=0,
    )
    started = start_sum(1, plane2)
    total = finish_sum(1, plane2, started, line2)
    small_ref[8:16, :] = total[:, 0:D]
    small_ref[24:32, 0:LEN] = total[:, D:WIDTH]
    small_ref[16:32, 3 * LEN : 4 * LEN] = jnp.broadcast_to(live_total, (16, LEN))
    small_ref[16:32, 4 * LEN : D] = jnp.zeros((16, D - 4 * LEN), F32)
    matrix_copy.wait()


def update_kernel(
    count,
    small_ref,
    matrix_ref,
    weight_ref,
    momentum_ref,
    weight_out,
    momentum_out,
    error_out,
    vector_out,
    vector_mom_out,
    loss_out,
    norm_out,
    fnew_out,
    live_out,
    matrix,
    weight,
    momentum,
    store_sem,
):
    ortho = small_ref[0:8, :]
    fnew = small_ref[8:16, :]
    square = jnp.zeros((RANK, 1), F32)
    for k in range(RANK):
        left = jnp.sum(ortho * ortho[k : k + 1, :], axis=1, keepdims=True)
        right = jnp.sum(fnew * fnew[k : k + 1, :], axis=1, keepdims=True)
        square = square + left * right
    square = jnp.sum(square, axis=0, keepdims=True)
    vec = small_ref[16:32, 0:LEN]
    lane = lax.broadcasted_iota(jnp.int32, (1, LEN), 1)
    scale_row = jnp.where(lane == 0, vec[6:7, 1:2], 0.0)
    grad = jnp.concatenate(
        [vec[0:6], vec[8:11], scale_row, jnp.zeros((6, LEN), F32)], axis=0
    )
    square = square + jnp.sum(
        jnp.sum(grad * grad, axis=1, keepdims=True), axis=0, keepdims=True
    )
    norm = jnp.sqrt(square)
    clip = CLIP_NORM / jnp.maximum(norm, CLIP_NORM)

    oh, om, ol = parts_of(ortho)
    fh, fm, fl = parts_of(fnew)
    pad = jnp.zeros((16, D), F32)
    left = jnp.concatenate([oh, oh, om, om, oh, ol, pad], axis=0).astype(BF16)
    right = jnp.concatenate([fh, fm, fh, fm, fl, fh, pad], axis=0).astype(BF16)
    copies = []

    def send_out(source, target, rows, sem):
        copy = pltpu.make_async_copy(source.at[rows, :], target.at[rows, :], sem)
        copy.start()
        copies.append(copy)

    for b in range(3):
        rows = slice(b * 256, (b + 1) * 256)
        approx = tn(left[:, rows], right)
        mom = MOMENTUM_DECAY * momentum_ref[rows, :] + clip * approx
        momentum[rows, :] = mom
        send_out(momentum, momentum_out, rows, store_sem.at[b, 0])
        weight[rows, :] = weight_ref[rows, :] - RATE_MATRIX * mom
        send_out(weight, weight_out, rows, store_sem.at[b, 1])
        matrix[rows, :] = matrix_ref[rows, :] - approx * (1.0 / count)
        send_out(matrix, error_out.at[0], rows, store_sem.at[b, 2])

    row = lax.broadcasted_iota(jnp.int32, (16, 1), 0)
    rate = jnp.where(row < 6, RATE_GAIN, jnp.where(row < 9, RATE_BIAS, RATE_SCALE))
    mom = MOMENTUM_DECAY * small_ref[16:32, 2 * LEN : 3 * LEN] + clip * grad
    vector_mom_out[...] = mom
    vector_out[...] = small_ref[16:32, LEN : 2 * LEN] - rate * mom
    loss_out[...] = vec[6:7, 0:1]
    norm_out[...] = norm
    fnew_out[...] = fnew
    live_out[...] = small_ref[16:17, 3 * LEN : 3 * LEN + 1]
    for copy in copies:
        copy.wait()


def local(
    n_wide,
    n_narrow,
    projected,
    layer_input,
    segment_ids,
    pad_mask,
    roles,
    labelled,
    out_weight,
    out_momentum,
    errors,
    factors,
    norm_gain,
    position_bias,
    log_scale,
    gain_momentum,
    bias_momentum,
    scale_momentum,
):
    count = n_wide * n_narrow
    lines = n_wide // 2
    spots = 2 * n_narrow
    blocks = count // GROUP
    sends = (lines - 1) + lines * n_narrow + lines * (n_narrow - 1)
    anywhere = pl.BlockSpec(memory_space=pl.ANY)
    vmem = pl.BlockSpec(memory_space=pltpu.VMEM)

    def stay(x):
        return pltpu.with_memory_space_constraint(x, pltpu.HBM)

    in_hbm = pl.BlockSpec(memory_space=pltpu.HBM)
    small, matrix = pl.pallas_call(
        functools.partial(step_kernel, n_wide, n_narrow),
        out_shape=(
            jax.ShapeDtypeStruct((32, D), F32),
            jax.ShapeDtypeStruct((D, D), F32),
        ),
        in_specs=[in_hbm] * 19,
        out_specs=(vmem, anywhere),
        scratch_shapes=[
            pltpu.VMEM((ROWS_DEV, LEN), jnp.int32),
            pltpu.VMEM((ROWS_DEV, LEN), jnp.int32),
            pltpu.VMEM((3, ROWS_DEV), jnp.int32),
            pltpu.VMEM((1, ROWS_DEV), jnp.int32),
            pltpu.VMEM((RANK, D), F32),
            pltpu.VMEM((6, LEN), F32),
            pltpu.VMEM((6, LEN), F32),
            pltpu.VMEM((HEADS, BUCKETS), F32),
            pltpu.VMEM((HEADS, BUCKETS), F32),
            pltpu.VMEM((1, 1), F32),
            pltpu.VMEM((1, 1), F32),
            pltpu.VMEM((2 * LEN, FLAT), BF16),
            pltpu.VMEM((BUCKETS, FLAT), BF16),
            pltpu.VMEM((2 * LEN, BUCKETS), BF16),
            pltpu.VMEM((16, FLAT), F32),
            pltpu.SemaphoreType.DMA((15,)),
            pltpu.VMEM((3, TOK, D), BF16),
            pltpu.VMEM((TOK, D), BF16),
            pltpu.VMEM((D, D), F32),
            pltpu.VMEM((D, D), F32),
            pltpu.VMEM((D, D), BF16),
            pltpu.VMEM((HEADS, LEN, LEN), F32),
            pltpu.VMEM((ROWS_DEV, LEN, LEN), BF16),
            pltpu.VMEM((ROWS_DEV, LEN, LEN), BF16),
            pltpu.VMEM((32, TOK), BF16),
            pltpu.VMEM((TOK, LEN), BF16),
            pltpu.VMEM((ROWS_DEV * HEADS, LEN, LEN), F32),
            pltpu.VMEM((2, PAIRS, LEN, 2 * LEN), F32),
            pltpu.VMEM((2, PAIRS, 2 * LEN, LEN), BF16),
            pltpu.VMEM((D, TOK), BF16),
            pltpu.VMEM((TOK, D), F32),
            pltpu.VMEM((TOK, D), BF16),
            pltpu.VMEM((TOK, D), BF16),
            pltpu.VMEM((TOK, 1), F32),
            pltpu.VMEM((D, D), F32),
            pltpu.VMEM((D, D), BF16),
            pltpu.VMEM((D, D), BF16),
            pltpu.VMEM((count, 16, PACK), BF16),
            pltpu.VMEM((blocks, GROUP * 8, D), BF16),
            pltpu.VMEM((blocks, 16, GROUP * 16), F32),
            pltpu.VMEM((16, 2 * LEN), F32),
            pltpu.VMEM((spots, RANK, WIDTH), F32),
            pltpu.VMEM((lines, RANK, WIDTH), F32),
            pltpu.VMEM((spots, RANK, WIDTH), F32),
            pltpu.VMEM((lines, RANK, WIDTH), F32),
            pltpu.SemaphoreType.DMA((ROWS_DEV,)),
            pltpu.SemaphoreType.DMA,
            pltpu.SemaphoreType.DMA((2,)),
            pltpu.SemaphoreType.DMA,
            pltpu.SemaphoreType.DMA((sends,)),
            pltpu.SemaphoreType.DMA((count,)),
            pltpu.SemaphoreType.DMA((2, spots)),
            pltpu.SemaphoreType.DMA((2, spots)),
            pltpu.SemaphoreType.DMA((2, lines)),
            pltpu.SemaphoreType.DMA((2, lines)),
        ],
        compiler_params=pltpu.CompilerParams(
            collective_id=0, has_side_effects=True, vmem_limit_bytes=(48 if blocks == 1 else 60) * 2**20
        ),
        name="step",
    )(
        stay(projected),
        stay(layer_input),
        stay(out_weight),
        stay(errors),
        stay(segment_ids.reshape(ROWS_DEV, LEN)),
        stay(pad_mask.reshape(ROWS_DEV, LEN)),
        stay(roles.T),
        stay(labelled.reshape(1, ROWS_DEV)),
        stay(factors),
        stay(norm_gain.reshape(6, LEN)),
        stay(gain_momentum.reshape(6, LEN)),
        stay(position_bias.T),
        stay(bias_momentum.T),
        log_scale.reshape(1, 1),
        scale_momentum.reshape(1, 1),
        stay(jnp.asarray(diagonal_onehot(FLAT), BF16)),
        stay(jnp.asarray(bucket_spread(), BF16)),
        stay(jnp.asarray(diagonal_onehot(BUCKETS), BF16)),
        stay(jnp.asarray(head_mask())),
    )
    outs = pl.pallas_call(
        functools.partial(update_kernel, count),
        out_shape=(
            jax.ShapeDtypeStruct((D, D), F32),
            jax.ShapeDtypeStruct((D, D), F32),
            jax.ShapeDtypeStruct((1, D, D), F32),
            jax.ShapeDtypeStruct((16, LEN), F32),
            jax.ShapeDtypeStruct((16, LEN), F32),
            jax.ShapeDtypeStruct((1, 1), F32),
            jax.ShapeDtypeStruct((1, 1), F32),
            jax.ShapeDtypeStruct((RANK, D), F32),
            jax.ShapeDtypeStruct((1, 1), F32),
        ),
        in_specs=[vmem] * 4,
        out_specs=(anywhere,) * 3 + (vmem,) * 6,
        scratch_shapes=[
            pltpu.VMEM((D, D), F32),
            pltpu.VMEM((D, D), F32),
            pltpu.VMEM((D, D), F32),
            pltpu.SemaphoreType.DMA((3, 3)),
        ],
        compiler_params=pltpu.CompilerParams(vmem_limit_bytes=24 * 2**20),
        name="update",
    )(small, matrix, out_weight, out_momentum)
    weight_new, weight_mom, errors_new, vec_new, vec_mom, loss, norm, fnew, live_total = outs
    size = D + FLAT + 1
    return (
        weight_new,
        weight_mom,
        errors_new,
        fnew,
        vec_new.reshape(-1)[:size],
        vec_mom.reshape(-1)[:size],
        loss.reshape(1),
        live_total.reshape(1),
        norm.reshape(1),
    )


def solution(mesh):
    both = ("wide", "narrow")
    in_specs = (
        P(None, both, None),
        P(both, None),
        P(both),
        P(both),
        P(both, None),
        P(both),
        P(),
        P(),
        P(both, None, None),
        P(),
        P(),
        P(),
        P(),
        P(),
        P(),
        P(),
    )
    out_specs = (P(), P(), P(both, None, None), P(), P(), P(), P(), P(), P())
    return jax.shard_map(
        functools.partial(local, mesh.shape["wide"], mesh.shape["narrow"]),
        mesh=mesh,
        in_specs=in_specs,
        out_specs=out_specs,
        check_vma=False,
    )
```

```python
import functools

import jax
import jax.numpy as jnp
import numpy as np
from jax import lax
from jax.experimental import pallas as pl
from jax.experimental.pallas import tpu as pltpu
from jax.sharding import PartitionSpec as P

D = 768
HEADS = 12
HEAD_DIM = 64
BUCKETS = 32
LEN = 128
ROWS_DEV = 8
RANK = 8
TOK = ROWS_DEV * LEN
PAIRS = HEADS // 2
HALF = D // 2
FLAT = BUCKETS * HEADS
PACK = D + HALF
GROUP = 32
WIDTH = D + 128

EPSILON = 1e-06
MOMENTUM_DECAY = 0.9
CLIP_NORM = 0.01
RATE_MATRIX = 50000.0
RATE_GAIN = 4000.0
RATE_BIAS = 2000.0
RATE_SCALE = 10.0
MASKED = -float(2**30)
UNLABELLED = 2.0
F32 = jnp.float32
BF16 = jnp.bfloat16
MESH = pl.DeviceIdType.MESH


def diagonal_buckets():
    half_count = BUCKETS // 2
    exact_count = half_count // 2
    table = np.full((2 * LEN,), -1, np.int64)
    for k in range(2 * LEN):
        if k == LEN:
            continue
        relative = -k if k < LEN else 2 * LEN - k
        distance = abs(relative)
        larger = exact_count + int(
            np.log(np.maximum(distance, 1) / exact_count)
            / np.log(128.0 / exact_count)
            * (half_count - exact_count)
        )
        larger = min(larger, half_count - 1)
        table[k] = (half_count if relative > 0 else 0) + (
            distance if distance < exact_count else larger
        )
    return table


def diagonal_onehot(width):
    spread = np.arange(width) // (width // BUCKETS)
    return (diagonal_buckets()[:, None] == spread[None, :]).astype(np.float32)


def bucket_spread():
    return (np.arange(BUCKETS)[:, None] == (np.arange(FLAT) // HEADS)[None, :]).astype(np.float32)


def head_mask():
    return (np.arange(16)[:, None] == (np.arange(FLAT) % HEADS)[None, :]).astype(np.float32)


def nn(left, right):
    return lax.dot_general(
        left, right, (((1,), (0,)), ((), ())), preferred_element_type=F32
    )


def nt(left, right):
    return lax.dot_general(
        left, right, (((1,), (1,)), ((), ())), preferred_element_type=F32
    )


def tn(left, right):
    return lax.dot_general(
        left, right, (((0,), (0,)), ((), ())), preferred_element_type=F32
    )


def parts_of(x):
    high = x.astype(BF16).astype(F32)
    rest = x - high
    middle = rest.astype(BF16).astype(F32)
    return high, middle, rest - middle


def stacked_parts(x):
    high, middle, low = parts_of(x)
    return jnp.concatenate([high, middle, low, jnp.zeros_like(x)], axis=0).astype(BF16)


def folded(y, rows):
    return y[0:rows] + y[rows : 2 * rows] + y[2 * rows : 3 * rows]


def looped(count, body, carry):
    if count == 1:
        return body(0, carry)
    return lax.fori_loop(0, count, body, carry)


def step_kernel(
    n_wide,
    n_narrow,
    proj_hbm,
    resid_hbm,
    weight_hbm,
    error_hbm,
    momentum_hbm,
    seg_hbm,
    pad_hbm,
    roles_hbm,
    label_hbm,
    factor_hbm,
    gain_hbm,
    gain_mom_hbm,
    bias_hbm,
    bias_mom_hbm,
    scale_hbm,
    scale_mom_hbm,
    onehot_hbm,
    spread_hbm,
    diagonal_hbm,
    head_mask_hbm,
    small_ref,
    matrix_hbm,
    weight_keep,
    momentum_keep,
    seg_ref,
    pad_ref,
    roles_ref,
    label_ref,
    factor_ref,
    gain_ref,
    gain_mom_ref,
    bias_ref,
    bias_mom_ref,
    scale_ref,
    scale_mom_ref,
    onehot_ref,
    spread_ref,
    diagonal_ref,
    head_mask_ref,
    small_sem,
    proj,
    resid,
    weight,
    error,
    weight_low,
    bias_table,
    key_extra,
    query_extra,
    member,
    member_t,
    probs,
    score_even,
    score_odd,
    prob_even,
    prob_odd,
    mixed_t,
    wide_rows,
    zed,
    zed_high,
    zed_low,
    rms_inv,
    matrix,
    matrix_high,
    matrix_low,
    gather,
    anchors_all,
    own_scores,
    diagonals,
    plane1,
    line1,
    plane2,
    line2,
    row_sem,
    resid_sem,
    load_sem,
    out_sem,
    gather_send,
    gather_recv,
    plane_send,
    plane_recv,
    line_send,
    line_recv,
):
    count = n_wide * n_narrow
    lines = n_wide // 2
    spots = 2 * n_narrow
    wide = lax.axis_index("wide")
    narrow = lax.axis_index("narrow")
    me = wide * n_narrow + narrow
    line = wide // 2
    side = wide % 2
    spot = side * n_narrow + narrow

    y_size = n_narrow // 2
    row_at, core = narrow // 2, narrow % 2
    offsets = sorted(
        (
            (dx, dy, dc)
            for dx in range(2)
            for dy in range(y_size)
            for dc in range(2)
            if dx or dy or dc
        ),
        key=lambda d: (-(d[0] > 0) - (d[1] > 0), -d[2]),
    )
    far_lines = sorted(range(1, lines), key=lambda k: -min(k, lines - k))

    def spot_device(d):
        dx, dy, dc = d
        other_side = (side + dx) % 2
        other_narrow = (row_at + dy) % y_size * 2 + (core + dc) % 2
        return other_side * n_narrow + other_narrow, (line * 2 + other_side, other_narrow)

    def line_device(k):
        other = (line + k) % lines
        return other, (other * 2 + side, narrow)

    def other_line(k):
        return k + (k - line + lines) // lines

    cells = [d for d in offsets if not d[2]]

    sibling = (wide, narrow + 1 - 2 * (narrow % 2))

    def load(source, target, sem):
        copy = pltpu.make_async_copy(source, target, sem)
        copy.start()
        return copy

    def load_row(r):
        rows = pl.ds(r * LEN, LEN)
        load(proj_hbm.at[:, rows, :], proj.at[:, rows, :], row_sem.at[r])

    mask_loads = [load(seg_hbm, seg_ref, small_sem.at[0]), load(pad_hbm, pad_ref, small_sem.at[1])]
    load_row(0)
    bias_loads = [
        load(bias_hbm, bias_ref, small_sem.at[2]),
        load(diagonal_hbm, diagonal_ref, small_sem.at[3]),
    ]
    load_row(1)
    load_row(2)
    rest_loads = [
        load(source, target, small_sem.at[4 + k])
        for k, (source, target) in enumerate(
            (
                (roles_hbm, roles_ref),
                (label_hbm, label_ref),
                (factor_hbm, factor_ref),
                (gain_hbm, gain_ref),
                (gain_mom_hbm, gain_mom_ref),
                (bias_mom_hbm, bias_mom_ref),
                (scale_hbm, scale_ref),
                (scale_mom_hbm, scale_mom_ref),
                (onehot_hbm, onehot_ref),
                (spread_hbm, spread_ref),
                (head_mask_hbm, head_mask_ref),
            )
        )
    ]
    barrier = pltpu.get_barrier_semaphore()
    for d in offsets:
        pl.semaphore_signal(barrier, inc=1, device_id=spot_device(d)[1], device_id_type=MESH)
    for k in far_lines:
        pl.semaphore_signal(barrier, inc=1, device_id=line_device(k)[1], device_id_type=MESH)

    for copy in mask_loads:
        copy.wait()
    code = jnp.where(pad_ref[...] == 1, seg_ref[...], 3).astype(F32)
    seg_f = seg_ref[...].astype(F32)
    fill = jnp.zeros((LEN - 16, LEN), F32)
    code_t = jnp.concatenate([code, seg_f, fill], axis=0).T
    lane = lax.broadcasted_iota(jnp.int32, (1, LEN), 1)
    sentence = lane.astype(F32)
    for r in range(ROWS_DEV):
        code_col = code_t[:, r : r + 1]
        seg_col = code_t[:, 8 + r : 9 + r]
        key_extra[r] = jnp.where(
            (sentence < 3.0) & (sentence != code_col), MASKED, 0.0
        ).astype(BF16)
        query_extra[r] = jnp.where(sentence == seg_col, 1.0, 0.0).astype(BF16)

    first = jnp.where(lane < HEAD_DIM, 1.0, 0.0).astype(BF16)
    second = jnp.where(lane < HEAD_DIM, 0.0, 1.0).astype(BF16)
    nothing = jnp.zeros((HEAD_DIM, LEN), BF16)

    score_rows = (score_even, score_odd)
    prob_rows = (prob_even, prob_odd)

    def rows_of(r):
        return slice(r * LEN, (r + 1) * LEN)

    def arrive(r):
        rows = rows_of(r)
        pltpu.make_async_copy(proj_hbm.at[:, rows, :], proj.at[:, rows, :], row_sem.at[r]).wait()

    def score(r, p):
        rows = rows_of(r)
        cols = slice(p * LEN, (p + 1) * LEN)
        query = proj[0, rows, cols]
        query_more = query_extra[r]
        left = jnp.concatenate([proj[1, rows, cols], key_extra[r]], axis=1)
        right = jnp.concatenate(
            [
                jnp.concatenate([query * first, query_more], axis=1),
                jnp.concatenate([query * second, query_more], axis=1),
            ],
            axis=0,
        )
        score_rows[r % 2][p] = nt(left, right)

    def soften(r, p):
        for half in range(2):
            head = 2 * p + half
            part = score_rows[r % 2][p, :, half * LEN : (half + 1) * LEN] + bias_table[head]
            part = jnp.exp(part - jnp.max(part, axis=0, keepdims=True))
            part = part * (1.0 / jnp.sum(part, axis=0, keepdims=True))
            probs[r * HEADS + head] = part
            prob_rows[r % 2][p, half * LEN : (half + 1) * LEN, :] = part.astype(BF16)

    def mix(r, p):
        rows = rows_of(r)
        cols = slice(p * LEN, (p + 1) * LEN)
        value_t = proj[2, rows, cols].T
        left = jnp.concatenate(
            [
                jnp.concatenate([value_t[:HEAD_DIM], nothing], axis=1),
                jnp.concatenate([nothing, value_t[HEAD_DIM:]], axis=1),
            ],
            axis=0,
        )
        mixed_t[cols, rows] = nn(left, prob_rows[r % 2][p]).astype(BF16)

    arrive(0)
    for p in range(PAIRS):
        score(0, p)
    for r in range(3, ROWS_DEV):
        load_row(r)

    for copy in bias_loads:
        copy.wait()
    high, middle, low = parts_of(bias_ref[...])
    gap = jnp.zeros((4, BUCKETS), F32)
    diag_bias = folded(
        nt(
            jnp.concatenate([high, gap, middle, gap, low, gap], axis=0).astype(BF16),
            diagonal_ref[...],
        ),
        16,
    )
    row8 = lax.broadcasted_iota(jnp.int32, (8, 1), 0)
    for h in range(HEADS):
        sheared = jnp.broadcast_to(diag_bias[h : h + 1, :], (8, 2 * LEN))
        for bit in (1, 2, 4):
            sheared = jnp.where((row8 & bit) != 0, pltpu.roll(sheared, bit, 1), sheared)
        bias_table[h, 0:8, :] = sheared[:, :LEN]
        for a in range(1, LEN // 8):
            bias_table[h, 8 * a : 8 * a + 8, :] = pltpu.roll(sheared, 8 * a, 1)[:, :LEN]

    for copy in rest_loads:
        copy.wait()
    roles_f = roles_ref[...].astype(F32)
    slot = lane % 32
    row_of = lax.broadcasted_iota(jnp.int32, (32, 1), 0)
    same = lax.broadcasted_iota(jnp.int32, (8, 8), 0) == lax.broadcasted_iota(jnp.int32, (8, 8), 1)

    def column_of(row):
        return jnp.sum(jnp.where(same, row, 0.0), axis=1, keepdims=True)

    role_col = jnp.concatenate(
        [column_of(roles_f[k : k + 1, :]) for k in range(3)] + [jnp.full((8, 1), 9.0, F32)], axis=0
    )
    for r in range(ROWS_DEV):
        role_lane = jnp.where(
            slot < 8,
            roles_f[0:1, r : r + 1],
            jnp.where(slot < 16, roles_f[1:2, r : r + 1], roles_f[2:3, r : r + 1]),
        )
        role_lane = jnp.where((slot < 24) & (slot % 8 == r), role_lane, 9.0)
        member_t[r * LEN : (r + 1) * LEN, :] = jnp.where(
            role_lane == code_t[:, r : r + 1], 1.0, 0.0
        ).astype(BF16)
        member[:, r * LEN : (r + 1) * LEN] = jnp.where(
            (role_col == code[r : r + 1, :]) & (row_of % 8 == r), 1.0, 0.0
        ).astype(BF16)

    def project(c):
        rows = slice(c * 256, (c + 1) * 256)
        zed[rows, :] = resid[rows, :].astype(F32) + tn(mixed_t[:, rows], weight_low[...])

    def normalise():
        for b in range(TOK // 32):
            rows = slice(b * 32, (b + 1) * 32)
            hidden = zed[rows, :]
            inv = lax.rsqrt(jnp.sum(hidden * hidden, axis=1, keepdims=True) * (1.0 / D) + EPSILON)
            hidden = hidden * inv
            zed[rows, :] = hidden
            rms_inv[rows, :] = inv
            high = hidden.astype(BF16)
            zed_high[rows, :] = high
            zed_low[rows, :] = (hidden - high.astype(F32)).astype(BF16)
        return nn(member[...], zed_high[...]) + nn(member[...], zed_low[...])

    for step in range(1, ROWS_DEV + 2):
        if step < ROWS_DEV:
            arrive(step)
        for p in range(PAIRS):
            if step < ROWS_DEV:
                score(step, p)
            if step > 1:
                mix(step - 2, p)
            if step <= ROWS_DEV:
                soften(step - 1, p)
        if step == 2:
            weight_copy = load(weight_hbm, weight, load_sem.at[0])
            resid_copy = load(resid_hbm, resid, resid_sem)
    weight_copy.wait()
    resid_copy.wait()
    weight_low[...] = weight[...].astype(BF16)
    for c in range(4):
        project(c)
    sums = normalise()
    error_copy = load(error_hbm.at[0], error, load_sem.at[1])
    keep_copies = [
        load(momentum_hbm, momentum_keep, load_sem.at[2]),
        load(weight, weight_keep, load_sem.at[3]),
    ]
    counts = jnp.sum(member[...].astype(F32), axis=1, keepdims=True)[0:24]
    gain_rows = gain_ref[...]
    gain = jnp.concatenate([gain_rows[k : k + 1, :] for k in range(6)], axis=1)
    zed_mean = sums[0:24] / counts
    means = zed_mean * gain
    inverse = lax.rsqrt(jnp.sum(means * means, axis=1, keepdims=True) + EPSILON)
    unit = means * inverse

    live_own = column_of(label_ref[...].astype(F32))
    wide_lane = lax.broadcasted_iota(jnp.int32, (8, D), 1)
    marked = jnp.where(
        live_own > 0.5, unit[0:8], jnp.where(wide_lane == 0, UNLABELLED, 0.0)
    )
    own_cands = unit[8:24].astype(BF16)
    gather[me, :, 0:D] = own_cands
    gather[me, :, D:PACK] = jnp.concatenate([marked[:, :HALF], marked[:, HALF:]], axis=0).astype(
        BF16
    )
    own_anchors = jnp.concatenate([marked, jnp.zeros_like(marked)], axis=0).astype(BF16)

    pl.semaphore_wait(barrier, spots + lines - 2)
    sends = []

    def send_block(block, device):
        copy = pltpu.make_async_remote_copy(
            src_ref=gather.at[block],
            dst_ref=gather.at[block],
            send_sem=gather_send.at[len(sends)],
            recv_sem=gather_recv.at[block],
            device_id=device,
            device_id_type=MESH,
        )
        copy.start()
        sends.append(copy)

    def await_block(block):
        pltpu.make_async_remote_copy(
            src_ref=gather.at[block],
            dst_ref=gather.at[block],
            send_sem=gather_send.at[0],
            recv_sem=gather_recv.at[block],
            device_id=sibling,
            device_id_type=MESH,
        ).wait_recv()

    line_order = [line] + [other_line(k) for k in range(lines - 1)]
    for k in far_lines:
        send_block(me, line_device(k)[1])
    for k in range(lines):
        block = (line_order[k] * 2 + side) * n_narrow + narrow
        if k:
            await_block(block)
        for d in cells:
            send_block(block, spot_device(d)[1])
        send_block(block, sibling)

    error_copy.wait()
    factor_parts = stacked_parts(factor_ref[...])
    error_rows = error[...]
    error_high = error_rows.astype(BF16)
    error_low = (error_rows - error_high.astype(F32)).astype(BF16)
    row_part = folded(nt(factor_parts, error_high) + nt(factor_parts, error_low), RANK)

    def flat_bias(x):
        high, middle, low = parts_of(x)
        spread = folded(
            nn(
                jnp.concatenate([high, gap, middle, gap, low, gap], axis=0).astype(BF16),
                spread_ref[...],
            ),
            16,
        )
        return jnp.sum(spread * head_mask_ref[...], axis=0, keepdims=True)

    def packed(gain_part, bias_part, scale_part):
        return jnp.concatenate(
            [gain_part]
            + [bias_part[:, k * LEN : (k + 1) * LEN] for k in range(3)]
            + [jnp.where(lane == 0, scale_part, 0.0), jnp.zeros((6, LEN), F32)],
            axis=0,
        )

    small_ref[16:32, LEN : 2 * LEN] = packed(gain_rows, flat_bias(bias_ref[...]), scale_ref[...])
    small_ref[16:32, 2 * LEN : 3 * LEN] = packed(gain_mom_ref[...], flat_bias(bias_mom_ref[...]), scale_mom_ref[...])

    for k in range(lines):
        for d in cells[::-1]:
            _, (other_wide, other_narrow) = spot_device(d)
            block = (line_order[k] * 2 + other_wide % 2) * n_narrow + other_narrow
            await_block(block)
            send_block(block, sibling)
    for k in range(lines):
        for d in [(0, 0, 0)] + cells[::-1]:
            _, (other_wide, other_narrow) = spot_device(d)
            block = (
                (line_order[k] * 2 + other_wide % 2) * n_narrow
                + other_narrow
                + 1
                - 2 * (narrow % 2)
            )
            await_block(block)
    for copy in sends:
        copy.wait_send()

    blocks = count // GROUP
    temper = jnp.exp(scale_ref[...])

    def unpack(b, total):
        picked = gather[pl.ds(b * GROUP, GROUP), :, D:PACK].astype(F32)
        left = picked[:, 0:8, :].reshape(GROUP * 8, HALF)
        right = picked[:, 8:16, :].reshape(GROUP * 8, HALF)
        anchors_all[b] = jnp.concatenate([left, right], axis=1).astype(BF16)
        live = jnp.where(left[:, 0:1] < 1.5, 1.0, 0.0)
        return total + jnp.sum(live, axis=0, keepdims=True)

    live_total = looped(blocks, unpack, jnp.zeros((1, 1), F32))

    def cands_of(b):
        return gather[pl.ds(b * GROUP, GROUP), :, 0:D].reshape(GROUP * 16, D)

    first_lane = jnp.where(lax.broadcasted_iota(jnp.int32, (16, D), 1) == 0, 1.0, 0.0).astype(BF16)
    row16 = lax.broadcasted_iota(jnp.int32, (16, GROUP * 8), 0)
    lane16 = lax.broadcasted_iota(jnp.int32, (16, GROUP * 8), 1)
    per_live = 1.0 / live_total

    def columns(b, cand_grad):
        anchors = anchors_all[b]

        def part(c, state):
            top, total = state
            logits = temper * nt(cands_of(c), anchors)
            new_top = jnp.maximum(top, jnp.max(logits, axis=0, keepdims=True))
            total = total * jnp.exp(top - new_top) + jnp.sum(
                jnp.exp(logits - new_top), axis=0, keepdims=True
            )
            return new_top, total

        start = (jnp.full((1, GROUP * 8), -1e30, F32), jnp.zeros((1, GROUP * 8), F32))
        top, total = looped(blocks, part, start)
        log_total = top + jnp.log(total)
        live = jnp.where(nt(first_lane, anchors) < 1.5, per_live, 0.0)
        logits = temper * nt(own_cands, anchors)
        target = jnp.where(
            (row16 < 8) & (lane16 + b * (GROUP * 8) == row16 + me * ROWS_DEV), 1.0, 0.0
        )
        grad = (jnp.exp(logits - log_total) - target) * live
        return cand_grad + nn((temper * grad).astype(BF16), anchors)

    cand_grad = looped(blocks, columns, jnp.zeros((16, D), F32))

    def own_part(b, state):
        top, total = state
        logits = temper * nt(own_anchors, cands_of(b))
        own_scores[b] = logits
        new_top = jnp.maximum(top, jnp.max(logits, axis=1, keepdims=True))
        total = total * jnp.exp(top - new_top) + jnp.sum(
            jnp.exp(logits - new_top), axis=1, keepdims=True
        )
        return new_top, total

    start = (jnp.full((16, 1), -1e30, F32), jnp.zeros((16, 1), F32))
    top, total = looped(blocks, own_part, start)
    log_total = top + jnp.log(total)
    live16 = jnp.concatenate([live_own, jnp.zeros_like(live_own)], axis=0)
    row32 = lax.broadcasted_iota(jnp.int32, (16, GROUP * 16), 0)
    lane32 = lax.broadcasted_iota(jnp.int32, (16, GROUP * 16), 1)

    def own_grad(b, state):
        anchor_grad, positive, scale_grad = state
        logits = own_scores[b]
        target = jnp.where(
            (row32 < 8) & (lane32 + b * (GROUP * 16) == row32 + me * 2 * ROWS_DEV), 1.0, 0.0
        )
        positive = positive + jnp.sum(logits * target, axis=1, keepdims=True)
        grad = (jnp.exp(logits - log_total) - target) * (live16 * per_live)
        scale_grad = scale_grad + jnp.sum(grad * logits, axis=1, keepdims=True)
        anchor_grad = anchor_grad + nn((temper * grad).astype(BF16), cands_of(b))
        return anchor_grad, positive, scale_grad

    column = jnp.zeros((16, 1), F32)
    anchor_grad, positive, scale_grad = looped(
        blocks, own_grad, (jnp.zeros((16, D), F32), column, column)
    )
    loss_own = jnp.sum(live16 * (log_total - positive), axis=0, keepdims=True)
    scale_grad = jnp.sum(scale_grad, axis=0, keepdims=True)

    branch, mixed_grad = zed_high, zed_low
    unit_grad = jnp.concatenate([anchor_grad[0:8], cand_grad], axis=0)
    mean_grad = inverse * (unit_grad - unit * jnp.sum(unit * unit_grad, axis=1, keepdims=True))
    gain_grad = jnp.sum(mean_grad * zed_mean, axis=0, keepdims=True)
    high, middle, low = parts_of(mean_grad / counts * gain)
    wide_gap = jnp.zeros((8, D), F32)
    shares = jnp.concatenate(
        [high, wide_gap, middle, wide_gap, low, wide_gap, jnp.zeros((32, D), F32)], axis=0
    ).astype(BF16)
    wide_rows[...] = nn(member_t[...], shares)
    for b in range(TOK // 32):
        rows = slice(b * 32, (b + 1) * 32)
        zed_grad = wide_rows[rows, :]
        zed_rows = zed[rows, :]
        level = jnp.sum(zed_grad * zed_rows, axis=1, keepdims=True) * (1.0 / D)
        branch[rows, :] = (rms_inv[rows, :] * (zed_grad - zed_rows * level)).astype(BF16)
    by_token = folded(nt(factor_parts, branch[...]), RANK)
    row_part = row_part + folded(nt(stacked_parts(by_token), mixed_t[...]), RANK)

    def send_to(buffers, mine, device, send_sem, recv_sem):
        copy = pltpu.make_async_remote_copy(
            src_ref=buffers.at[mine],
            dst_ref=buffers.at[mine],
            send_sem=send_sem,
            recv_sem=recv_sem.at[mine],
            device_id=device,
            device_id_type=MESH,
        )
        copy.start()
        return copy

    def await_from(buffers, other, send_sem, recv_sem):
        pltpu.make_async_remote_copy(
            src_ref=buffers.at[other],
            dst_ref=buffers.at[other],
            send_sem=send_sem,
            recv_sem=recv_sem.at[other],
            device_id=sibling,
            device_id_type=MESH,
        ).wait_recv()

    def start_sum(which, plane):
        return [
            send_to(plane, spot, spot_device(d)[1], plane_send.at[which, k], plane_recv.at[which])
            for k, d in enumerate(offsets)
        ]

    def middle_sum(which, plane, along):
        for d in offsets[::-1]:
            await_from(plane, spot_device(d)[0], plane_send.at[which, 0], plane_recv.at[which])
        total = plane[0]
        for k in range(1, spots):
            total = total + plane[k]
        along[line] = total
        return [
            send_to(along, line, line_device(k)[1], line_send.at[which, k], line_recv.at[which])
            for k in far_lines
        ]

    def finish_sum(which, along, started):
        for k in far_lines[::-1]:
            await_from(along, line_device(k)[0], line_send.at[which, 0], line_recv.at[which])
        total = along[0]
        for k in range(1, lines):
            total = total + along[k]
        for copy in started:
            copy.wait_send()
        return total

    scalars = jnp.where(lane == 0, loss_own, jnp.where(lane == 1, scale_grad, 0.0))
    extra = jnp.concatenate(
        [gain_grad[:, k * LEN : (k + 1) * LEN] for k in range(6)]
        + [scalars, jnp.zeros((1, LEN), F32)],
        axis=0,
    )
    plane1[spot, :, 0:D] = row_part
    plane1[spot, :, D:WIDTH] = extra
    started = start_sum(0, plane1)

    for b in range(3):
        rows = slice(b * 256, (b + 1) * 256)
        full = error[rows, :] + nn(mixed_t[rows, :], branch[...])
        matrix[rows, :] = full
        high = full.astype(BF16)
        matrix_high[rows, :] = high
        matrix_low[rows, :] = (full - high.astype(F32)).astype(BF16)
    matrix_copy = pltpu.make_async_copy(matrix, matrix_hbm, out_sem)
    matrix_copy.start()

    for c in range(4):
        rows = slice(c * 256, (c + 1) * 256)
        mixed_grad[rows, :] = nt(branch[rows, :], weight_low[...]).astype(BF16)
    started = started + middle_sum(0, plane1, line1)
    for p in range(PAIRS):
        cols = slice(p * LEN, (p + 1) * LEN)

        def back(r, acc):
            offset = pl.multiple_of(r * LEN, LEN)
            rows = pl.ds(offset, LEN)
            grad = mixed_grad[rows, cols]
            right = jnp.concatenate([grad * first, grad * second], axis=0)
            prob_grad = nt(proj[2, rows, cols], right)
            prob = jnp.concatenate(
                [probs[r * HEADS + 2 * p], probs[r * HEADS + 2 * p + 1]], axis=1
            )
            product = prob * prob_grad
            return acc + (product - prob * jnp.sum(product, axis=0, keepdims=True))

        acc = lax.fori_loop(0, ROWS_DEV, back, jnp.zeros((LEN, 2 * LEN), F32), unroll=True)
        for half in range(2):
            padded = jnp.concatenate(
                [acc[:, half * LEN : (half + 1) * LEN], jnp.zeros((LEN, LEN), F32)], axis=1
            )
            sheared = padded[0:8]
            for a in range(1, LEN // 8):
                sheared = sheared + pltpu.roll(padded[8 * a : 8 * a + 8], 2 * LEN - 8 * a, 1)
            for bit in (1, 2, 4):
                moved = pltpu.roll(sheared, 2 * LEN - bit, 1)
                sheared = jnp.where((row8 & bit) != 0, moved, sheared)
            head = 2 * p + half
            diagonals[head : head + 1, :] = jnp.sum(sheared, axis=0, keepdims=True)
    diagonals[HEADS:16, :] = jnp.zeros((16 - HEADS, 2 * LEN), F32)
    high, middle, low = parts_of(diagonals[...])
    by_bucket = folded(
        nn(jnp.concatenate([high, middle, low], axis=0).astype(BF16), onehot_ref[...]), 16
    )
    bias_grad = jnp.sum(by_bucket * head_mask_ref[...], axis=0, keepdims=True)

    total = finish_sum(0, line1, started)
    small_ref[16:24, 0:LEN] = total[:, D:WIDTH]
    ortho = total[:, 0:D]
    rank_row = lax.broadcasted_iota(jnp.int32, (RANK, 1), 0)
    for k in range(RANK):
        vector = ortho[k : k + 1, :]
        dots = jnp.sum(ortho * vector, axis=1, keepdims=True)
        norm = lax.rsqrt(dots[k : k + 1, :] + EPSILON)
        vector = vector * norm
        ortho = jnp.where(
            rank_row > k, ortho - (dots * norm) * vector, jnp.where(rank_row == k, vector, ortho)
        )
    small_ref[0:8, :] = ortho
    ortho_parts = stacked_parts(ortho)
    plane2[spot, :, 0:D] = folded(
        nn(ortho_parts, matrix_high[...]) + nn(ortho_parts, matrix_low[...]), RANK
    )
    plane2[spot, :, D:WIDTH] = jnp.concatenate(
        [bias_grad[:, k * LEN : (k + 1) * LEN] for k in range(3)] + [jnp.zeros((5, LEN), F32)],
        axis=0,
    )
    started = start_sum(1, plane2)
    started = started + middle_sum(1, plane2, line2)
    total = finish_sum(1, line2, started)
    small_ref[8:16, :] = total[:, 0:D]
    small_ref[24:32, 0:LEN] = total[:, D:WIDTH]
    small_ref[16:32, 3 * LEN : 4 * LEN] = jnp.broadcast_to(live_total, (16, LEN))
    small_ref[16:32, 4 * LEN : D] = jnp.zeros((16, D - 4 * LEN), F32)
    matrix_copy.wait()
    for copy in keep_copies:
        copy.wait()


def update_kernel(
    count,
    small_ref,
    matrix_ref,
    weight_ref,
    momentum_ref,
    weight_out,
    momentum_out,
    error_out,
    vector_out,
    vector_mom_out,
    loss_out,
    norm_out,
    fnew_out,
    live_out,
    matrix,
    weight,
    momentum,
    store_sem,
):
    ortho = small_ref[0:8, :]
    fnew = small_ref[8:16, :]
    oh, om, ol = parts_of(ortho)
    fh, fm, fl = parts_of(fnew)
    pad = jnp.zeros((16, D), F32)
    left = jnp.concatenate([oh, oh, om, om, oh, ol, pad], axis=0).astype(BF16)
    right = jnp.concatenate([fh, fm, fh, fm, fl, fh, pad], axis=0).astype(BF16)
    copies = []

    def send_out(source, target, rows, sem):
        copy = pltpu.make_async_copy(source.at[rows, :], target.at[rows, :], sem)
        copy.start()
        copies.append(copy)

    for b in range(3):
        rows = slice(b * 256, (b + 1) * 256)
        approx = tn(left[:, rows], right)
        weight[rows, :] = approx
        matrix[rows, :] = matrix_ref[rows, :] - approx * (1.0 / count)
        send_out(matrix, error_out.at[0], rows, store_sem.at[b, 2])

    square = jnp.zeros((RANK, 1), F32)
    for k in range(RANK):
        left = jnp.sum(ortho * ortho[k : k + 1, :], axis=1, keepdims=True)
        right = jnp.sum(fnew * fnew[k : k + 1, :], axis=1, keepdims=True)
        square = square + left * right
    square = jnp.sum(square, axis=0, keepdims=True)
    vec = small_ref[16:32, 0:LEN]
    lane = lax.broadcasted_iota(jnp.int32, (1, LEN), 1)
    scale_row = jnp.where(lane == 0, vec[6:7, 1:2], 0.0)
    grad = jnp.concatenate(
        [vec[0:6], vec[8:11], scale_row, jnp.zeros((6, LEN), F32)], axis=0
    )
    square = square + jnp.sum(
        jnp.sum(grad * grad, axis=1, keepdims=True), axis=0, keepdims=True
    )
    norm = jnp.sqrt(square)
    clip = CLIP_NORM / jnp.maximum(norm, CLIP_NORM)

    for b in range(3):
        rows = slice(b * 256, (b + 1) * 256)
        mom = MOMENTUM_DECAY * momentum_ref[rows, :] + clip * weight[rows, :]
        momentum[rows, :] = mom
        send_out(momentum, momentum_out, rows, store_sem.at[b, 0])
        weight[rows, :] = weight_ref[rows, :] - RATE_MATRIX * mom
        send_out(weight, weight_out, rows, store_sem.at[b, 1])

    row = lax.broadcasted_iota(jnp.int32, (16, 1), 0)
    rate = jnp.where(row < 6, RATE_GAIN, jnp.where(row < 9, RATE_BIAS, RATE_SCALE))
    mom = MOMENTUM_DECAY * small_ref[16:32, 2 * LEN : 3 * LEN] + clip * grad
    vector_mom_out[...] = mom
    vector_out[...] = small_ref[16:32, LEN : 2 * LEN] - rate * mom
    loss_out[...] = vec[6:7, 0:1]
    norm_out[...] = norm
    fnew_out[...] = fnew
    live_out[...] = small_ref[16:17, 3 * LEN : 3 * LEN + 1]
    for copy in copies:
        copy.wait()


def local(
    n_wide,
    n_narrow,
    projected,
    layer_input,
    segment_ids,
    pad_mask,
    roles,
    labelled,
    out_weight,
    out_momentum,
    errors,
    factors,
    norm_gain,
    position_bias,
    log_scale,
    gain_momentum,
    bias_momentum,
    scale_momentum,
):
    count = n_wide * n_narrow
    lines = n_wide // 2
    spots = 2 * n_narrow
    blocks = count // GROUP
    sends = (lines - 1) + lines * n_narrow + lines * (n_narrow - 1)
    anywhere = pl.BlockSpec(memory_space=pl.ANY)
    vmem = pl.BlockSpec(memory_space=pltpu.VMEM)

    def stay(x):
        return pltpu.with_memory_space_constraint(x, pltpu.HBM)

    in_hbm = pl.BlockSpec(memory_space=pltpu.HBM)
    kept = pl.pallas_call(
        functools.partial(step_kernel, n_wide, n_narrow),
        out_shape=(
            jax.ShapeDtypeStruct((32, D), F32),
            jax.ShapeDtypeStruct((D, D), F32),
            jax.ShapeDtypeStruct((D, D), F32),
            jax.ShapeDtypeStruct((D, D), F32),
        ),
        in_specs=[in_hbm] * 20,
        out_specs=(vmem, anywhere, anywhere, anywhere),
        scratch_shapes=[
            pltpu.VMEM((ROWS_DEV, LEN), jnp.int32),
            pltpu.VMEM((ROWS_DEV, LEN), jnp.int32),
            pltpu.VMEM((3, ROWS_DEV), jnp.int32),
            pltpu.VMEM((1, ROWS_DEV), jnp.int32),
            pltpu.VMEM((RANK, D), F32),
            pltpu.VMEM((6, LEN), F32),
            pltpu.VMEM((6, LEN), F32),
            pltpu.VMEM((HEADS, BUCKETS), F32),
            pltpu.VMEM((HEADS, BUCKETS), F32),
            pltpu.VMEM((1, 1), F32),
            pltpu.VMEM((1, 1), F32),
            pltpu.VMEM((2 * LEN, FLAT), BF16),
            pltpu.VMEM((BUCKETS, FLAT), BF16),
            pltpu.VMEM((2 * LEN, BUCKETS), BF16),
            pltpu.VMEM((16, FLAT), F32),
            pltpu.SemaphoreType.DMA((15,)),
            pltpu.VMEM((3, TOK, D), BF16),
            pltpu.VMEM((TOK, D), BF16),
            pltpu.VMEM((D, D), F32),
            pltpu.VMEM((D, D), F32),
            pltpu.VMEM((D, D), BF16),
            pltpu.VMEM((HEADS, LEN, LEN), F32),
            pltpu.VMEM((ROWS_DEV, LEN, LEN), BF16),
            pltpu.VMEM((ROWS_DEV, LEN, LEN), BF16),
            pltpu.VMEM((32, TOK), BF16),
            pltpu.VMEM((TOK, LEN), BF16),
            pltpu.VMEM((ROWS_DEV * HEADS, LEN, LEN), F32),
            pltpu.VMEM((PAIRS, LEN, 2 * LEN), F32),
            pltpu.VMEM((PAIRS, LEN, 2 * LEN), F32),
            pltpu.VMEM((PAIRS, 2 * LEN, LEN), BF16),
            pltpu.VMEM((PAIRS, 2 * LEN, LEN), BF16),
            pltpu.VMEM((D, TOK), BF16),
            pltpu.VMEM((TOK, D), F32),
            pltpu.VMEM((TOK, D), F32),
            pltpu.VMEM((TOK, D), BF16),
            pltpu.VMEM((TOK, D), BF16),
            pltpu.VMEM((TOK, 1), F32),
            pltpu.VMEM((D, D), F32),
            pltpu.VMEM((D, D), BF16),
            pltpu.VMEM((D, D), BF16),
            pltpu.VMEM((count, 16, PACK), BF16),
            pltpu.VMEM((blocks, GROUP * 8, D), BF16),
            pltpu.VMEM((blocks, 16, GROUP * 16), F32),
            pltpu.VMEM((16, 2 * LEN), F32),
            pltpu.VMEM((spots, RANK, WIDTH), F32),
            pltpu.VMEM((lines, RANK, WIDTH), F32),
            pltpu.VMEM((spots, RANK, WIDTH), F32),
            pltpu.VMEM((lines, RANK, WIDTH), F32),
            pltpu.SemaphoreType.DMA((ROWS_DEV,)),
            pltpu.SemaphoreType.DMA,
            pltpu.SemaphoreType.DMA((4,)),
            pltpu.SemaphoreType.DMA,
            pltpu.SemaphoreType.DMA((sends,)),
            pltpu.SemaphoreType.DMA((count,)),
            pltpu.SemaphoreType.DMA((2, spots)),
            pltpu.SemaphoreType.DMA((2, spots)),
            pltpu.SemaphoreType.DMA((2, lines)),
            pltpu.SemaphoreType.DMA((2, lines)),
        ],
        compiler_params=pltpu.CompilerParams(
            collective_id=0, has_side_effects=True, vmem_limit_bytes=(45 if blocks == 1 else 60) * 2**20
        ),
        name="step",
    )(
        stay(projected),
        stay(layer_input),
        stay(out_weight),
        stay(errors),
        stay(out_momentum),
        stay(segment_ids.reshape(ROWS_DEV, LEN)),
        stay(pad_mask.reshape(ROWS_DEV, LEN)),
        stay(roles.T),
        stay(labelled.reshape(1, ROWS_DEV)),
        stay(factors),
        stay(norm_gain.reshape(6, LEN)),
        stay(gain_momentum.reshape(6, LEN)),
        stay(position_bias.T),
        stay(bias_momentum.T),
        log_scale.reshape(1, 1),
        scale_momentum.reshape(1, 1),
        stay(jnp.asarray(diagonal_onehot(FLAT), BF16)),
        stay(jnp.asarray(bucket_spread(), BF16)),
        stay(jnp.asarray(diagonal_onehot(BUCKETS), BF16)),
        stay(jnp.asarray(head_mask())),
    )
    outs = pl.pallas_call(
        functools.partial(update_kernel, count),
        out_shape=(
            jax.ShapeDtypeStruct((D, D), F32),
            jax.ShapeDtypeStruct((D, D), F32),
            jax.ShapeDtypeStruct((1, D, D), F32),
            jax.ShapeDtypeStruct((16, LEN), F32),
            jax.ShapeDtypeStruct((16, LEN), F32),
            jax.ShapeDtypeStruct((1, 1), F32),
            jax.ShapeDtypeStruct((1, 1), F32),
            jax.ShapeDtypeStruct((RANK, D), F32),
            jax.ShapeDtypeStruct((1, 1), F32),
        ),
        in_specs=[vmem] * 4,
        out_specs=(anywhere,) * 3 + (vmem,) * 6,
        scratch_shapes=[
            pltpu.VMEM((D, D), F32),
            pltpu.VMEM((D, D), F32),
            pltpu.VMEM((D, D), F32),
            pltpu.SemaphoreType.DMA((3, 3)),
        ],
        compiler_params=pltpu.CompilerParams(vmem_limit_bytes=24 * 2**20),
        name="update",
    )(*kept)
    weight_new, weight_mom, errors_new, vec_new, vec_mom, loss, norm, fnew, live_total = outs
    size = D + FLAT + 1
    return (
        weight_new,
        weight_mom,
        errors_new,
        fnew,
        vec_new.reshape(-1)[:size],
        vec_mom.reshape(-1)[:size],
        loss.reshape(1),
        live_total.reshape(1),
        norm.reshape(1),
    )


def solution(mesh):
    both = ("wide", "narrow")
    in_specs = (
        P(None, both, None),
        P(both, None),
        P(both),
        P(both),
        P(both, None),
        P(both),
        P(),
        P(),
        P(both, None, None),
        P(),
        P(),
        P(),
        P(),
        P(),
        P(),
        P(),
    )
    out_specs = (P(), P(), P(both, None, None), P(), P(), P(), P(), P(), P())
    return jax.shard_map(
        functools.partial(local, mesh.shape["wide"], mesh.shape["narrow"]),
        mesh=mesh,
        in_specs=in_specs,
        out_specs=out_specs,
        check_vma=False,
    )
```

```python
import functools

import jax
import jax.numpy as jnp
import numpy as np
from jax import lax
from jax.experimental import pallas as pl
from jax.experimental.pallas import tpu as pltpu
from jax.sharding import PartitionSpec as P

D = 768
HEADS = 12
HEAD_DIM = 64
BUCKETS = 32
LEN = 128
ROWS_DEV = 8
RANK = 8
TOK = ROWS_DEV * LEN
PAIRS = HEADS // 2
HALF = D // 2
FLAT = BUCKETS * HEADS
PACK = D + HALF
GROUP = 32
WIDTH = D + 128

EPSILON = 1e-06
MOMENTUM_DECAY = 0.9
CLIP_NORM = 0.01
RATE_MATRIX = 50000.0
RATE_GAIN = 4000.0
RATE_BIAS = 2000.0
RATE_SCALE = 10.0
MASKED = -float(2**30)
UNLABELLED = 2.0
F32 = jnp.float32
BF16 = jnp.bfloat16
MESH = pl.DeviceIdType.MESH


def diagonal_buckets():
    half_count = BUCKETS // 2
    exact_count = half_count // 2
    table = np.full((2 * LEN,), -1, np.int64)
    for k in range(2 * LEN):
        if k == LEN:
            continue
        relative = -k if k < LEN else 2 * LEN - k
        distance = abs(relative)
        larger = exact_count + int(
            np.log(np.maximum(distance, 1) / exact_count)
            / np.log(128.0 / exact_count)
            * (half_count - exact_count)
        )
        larger = min(larger, half_count - 1)
        table[k] = (half_count if relative > 0 else 0) + (
            distance if distance < exact_count else larger
        )
    return table


def diagonal_onehot(width):
    spread = np.arange(width) // (width // BUCKETS)
    return (diagonal_buckets()[:, None] == spread[None, :]).astype(np.float32)


def bucket_spread():
    return (np.arange(BUCKETS)[:, None] == (np.arange(FLAT) // HEADS)[None, :]).astype(np.float32)


def head_mask():
    return (np.arange(16)[:, None] == (np.arange(FLAT) % HEADS)[None, :]).astype(np.float32)


def nn(left, right):
    return lax.dot_general(
        left, right, (((1,), (0,)), ((), ())), preferred_element_type=F32
    )


def nt(left, right):
    return lax.dot_general(
        left, right, (((1,), (1,)), ((), ())), preferred_element_type=F32
    )


def tn(left, right):
    return lax.dot_general(
        left, right, (((0,), (0,)), ((), ())), preferred_element_type=F32
    )


def parts_of(x):
    high = x.astype(BF16).astype(F32)
    rest = x - high
    middle = rest.astype(BF16).astype(F32)
    return high, middle, rest - middle


def stacked_parts(x):
    high, middle, low = parts_of(x)
    return jnp.concatenate([high, middle, low, jnp.zeros_like(x)], axis=0).astype(BF16)


def folded(y, rows):
    return y[0:rows] + y[rows : 2 * rows] + y[2 * rows : 3 * rows]


def looped(count, body, carry):
    if count == 1:
        return body(0, carry)
    return lax.fori_loop(0, count, body, carry)


def step_kernel(
    n_wide,
    n_narrow,
    proj_hbm,
    resid_hbm,
    weight_hbm,
    error_hbm,
    momentum_hbm,
    seg_hbm,
    pad_hbm,
    roles_hbm,
    label_hbm,
    factor_hbm,
    gain_hbm,
    gain_mom_hbm,
    bias_hbm,
    bias_mom_hbm,
    scale_hbm,
    scale_mom_hbm,
    onehot_hbm,
    spread_hbm,
    diagonal_hbm,
    head_mask_hbm,
    small_ref,
    matrix_hbm,
    weight_keep,
    momentum_keep,
    seg_ref,
    pad_ref,
    roles_ref,
    label_ref,
    factor_ref,
    gain_ref,
    gain_mom_ref,
    bias_ref,
    bias_mom_ref,
    scale_ref,
    scale_mom_ref,
    onehot_ref,
    spread_ref,
    diagonal_ref,
    head_mask_ref,
    small_sem,
    proj,
    resid,
    weight,
    error,
    weight_low,
    bias_table,
    key_extra,
    query_extra,
    member,
    member_t,
    probs,
    score_even,
    score_odd,
    prob_even,
    prob_odd,
    mixed_t,
    wide_rows,
    zed,
    zed_high,
    zed_low,
    rms_inv,
    levels,
    matrix,
    matrix_high,
    matrix_low,
    gather,
    anchors_all,
    own_scores,
    diagonals,
    plane1,
    line1,
    plane2,
    line2,
    row_sem,
    resid_sem,
    load_sem,
    out_sem,
    gather_send,
    gather_recv,
    plane_send,
    plane_recv,
    line_send,
    line_recv,
):
    count = n_wide * n_narrow
    lines = n_wide // 2
    spots = 2 * n_narrow
    wide = lax.axis_index("wide")
    narrow = lax.axis_index("narrow")
    me = wide * n_narrow + narrow
    line = wide // 2
    side = wide % 2
    spot = side * n_narrow + narrow

    y_size = n_narrow // 2
    row_at, core = narrow // 2, narrow % 2
    offsets = sorted(
        (
            (dx, dy, dc)
            for dx in range(2)
            for dy in range(y_size)
            for dc in range(2)
            if dx or dy or dc
        ),
        key=lambda d: (-(d[0] > 0) - (d[1] > 0), -d[2]),
    )
    far_lines = sorted(range(1, lines), key=lambda k: -min(k, lines - k))

    def spot_device(d):
        dx, dy, dc = d
        other_side = (side + dx) % 2
        other_narrow = (row_at + dy) % y_size * 2 + (core + dc) % 2
        return other_side * n_narrow + other_narrow, (line * 2 + other_side, other_narrow)

    def line_device(k):
        other = (line + k) % lines
        return other, (other * 2 + side, narrow)

    def other_line(k):
        return k + (k - line + lines) // lines

    cells = [d for d in offsets if not d[2]]

    sibling = (wide, narrow + 1 - 2 * (narrow % 2))

    def load(source, target, sem):
        copy = pltpu.make_async_copy(source, target, sem)
        copy.start()
        return copy

    def load_row(r):
        rows = pl.ds(r * LEN, LEN)
        load(proj_hbm.at[:, rows, :], proj.at[:, rows, :], row_sem.at[r])

    mask_loads = [load(seg_hbm, seg_ref, small_sem.at[0]), load(pad_hbm, pad_ref, small_sem.at[1])]
    load_row(0)
    bias_loads = [
        load(bias_hbm, bias_ref, small_sem.at[2]),
        load(diagonal_hbm, diagonal_ref, small_sem.at[3]),
    ]
    for r in range(1, ROWS_DEV):
        load_row(r)
    rest_loads = [
        load(source, target, small_sem.at[4 + k])
        for k, (source, target) in enumerate(
            (
                (roles_hbm, roles_ref),
                (label_hbm, label_ref),
                (factor_hbm, factor_ref),
                (gain_hbm, gain_ref),
                (gain_mom_hbm, gain_mom_ref),
                (bias_mom_hbm, bias_mom_ref),
                (scale_hbm, scale_ref),
                (scale_mom_hbm, scale_mom_ref),
                (onehot_hbm, onehot_ref),
                (spread_hbm, spread_ref),
                (head_mask_hbm, head_mask_ref),
            )
        )
    ]
    barrier = pltpu.get_barrier_semaphore()
    for d in offsets:
        pl.semaphore_signal(barrier, inc=1, device_id=spot_device(d)[1], device_id_type=MESH)
    for k in far_lines:
        pl.semaphore_signal(barrier, inc=1, device_id=line_device(k)[1], device_id_type=MESH)

    for copy in mask_loads:
        copy.wait()
    code = jnp.where(pad_ref[...] == 1, seg_ref[...], 3).astype(F32)
    seg_f = seg_ref[...].astype(F32)
    fill = jnp.zeros((LEN - 16, LEN), F32)
    code_t = jnp.concatenate([code, seg_f, fill], axis=0).T
    lane = lax.broadcasted_iota(jnp.int32, (1, LEN), 1)
    sentence = lane.astype(F32)
    for r in range(ROWS_DEV):
        code_col = code_t[:, r : r + 1]
        seg_col = code_t[:, 8 + r : 9 + r]
        key_extra[r] = jnp.where(
            (sentence < 3.0) & (sentence != code_col), MASKED, 0.0
        ).astype(BF16)
        query_extra[r] = jnp.where(sentence == seg_col, 1.0, 0.0).astype(BF16)

    first = jnp.where(lane < HEAD_DIM, 1.0, 0.0).astype(BF16)
    second = jnp.where(lane < HEAD_DIM, 0.0, 1.0).astype(BF16)
    nothing = jnp.zeros((HEAD_DIM, LEN), BF16)

    score_rows = (score_even, score_odd)
    prob_rows = (prob_even, prob_odd)

    def rows_of(r):
        return slice(r * LEN, (r + 1) * LEN)

    def arrive(r):
        rows = rows_of(r)
        pltpu.make_async_copy(proj_hbm.at[:, rows, :], proj.at[:, rows, :], row_sem.at[r]).wait()

    def score(r, p):
        rows = rows_of(r)
        cols = slice(p * LEN, (p + 1) * LEN)
        query = proj[0, rows, cols]
        query_more = query_extra[r]
        left = jnp.concatenate([proj[1, rows, cols], key_extra[r]], axis=1)
        right = jnp.concatenate(
            [
                jnp.concatenate([query * first, query_more], axis=1),
                jnp.concatenate([query * second, query_more], axis=1),
            ],
            axis=0,
        )
        score_rows[r % 2][p] = nt(left, right)

    def soften(r, p):
        for half in range(2):
            head = 2 * p + half
            part = score_rows[r % 2][p, :, half * LEN : (half + 1) * LEN] + bias_table[head]
            part = jnp.exp(part - jnp.max(part, axis=0, keepdims=True))
            part = part * (1.0 / jnp.sum(part, axis=0, keepdims=True))
            probs[r * HEADS + head] = part
            prob_rows[r % 2][p, half * LEN : (half + 1) * LEN, :] = part.astype(BF16)

    def mix(r, p):
        rows = rows_of(r)
        cols = slice(p * LEN, (p + 1) * LEN)
        value_t = proj[2, rows, cols].T
        left = jnp.concatenate(
            [
                jnp.concatenate([value_t[:HEAD_DIM], nothing], axis=1),
                jnp.concatenate([nothing, value_t[HEAD_DIM:]], axis=1),
            ],
            axis=0,
        )
        mixed_t[cols, rows] = nn(left, prob_rows[r % 2][p]).astype(BF16)

    arrive(0)
    for p in range(PAIRS):
        score(0, p)

    for copy in bias_loads:
        copy.wait()
    high, middle, low = parts_of(bias_ref[...])
    gap = jnp.zeros((4, BUCKETS), F32)
    diag_bias = folded(
        nt(
            jnp.concatenate([high, gap, middle, gap, low, gap], axis=0).astype(BF16),
            diagonal_ref[...],
        ),
        16,
    )
    row8 = lax.broadcasted_iota(jnp.int32, (8, 1), 0)
    for h in range(HEADS):
        sheared = jnp.broadcast_to(diag_bias[h : h + 1, :], (8, 2 * LEN))
        for bit in (1, 2, 4):
            sheared = jnp.where((row8 & bit) != 0, pltpu.roll(sheared, bit, 1), sheared)
        bias_table[h, 0:8, :] = sheared[:, :LEN]
        for a in range(1, LEN // 8):
            bias_table[h, 8 * a : 8 * a + 8, :] = pltpu.roll(sheared, 8 * a, 1)[:, :LEN]

    for copy in rest_loads:
        copy.wait()
    roles_f = roles_ref[...].astype(F32)
    slot = lane % 32
    row_of = lax.broadcasted_iota(jnp.int32, (32, 1), 0)
    same = lax.broadcasted_iota(jnp.int32, (8, 8), 0) == lax.broadcasted_iota(jnp.int32, (8, 8), 1)

    def column_of(row):
        return jnp.sum(jnp.where(same, row, 0.0), axis=1, keepdims=True)

    role_col = jnp.concatenate(
        [column_of(roles_f[k : k + 1, :]) for k in range(3)] + [jnp.full((8, 1), 9.0, F32)], axis=0
    )
    for r in range(ROWS_DEV):
        role_lane = jnp.where(
            slot < 8,
            roles_f[0:1, r : r + 1],
            jnp.where(slot < 16, roles_f[1:2, r : r + 1], roles_f[2:3, r : r + 1]),
        )
        role_lane = jnp.where((slot < 24) & (slot % 8 == r), role_lane, 9.0)
        member_t[r * LEN : (r + 1) * LEN, :] = jnp.where(
            role_lane == code_t[:, r : r + 1], 1.0, 0.0
        ).astype(BF16)
        member[:, r * LEN : (r + 1) * LEN] = jnp.where(
            (role_col == code[r : r + 1, :]) & (row_of % 8 == r), 1.0, 0.0
        ).astype(BF16)

    def project(c):
        rows = slice(c * 256, (c + 1) * 256)
        zed[rows, :] = resid[rows, :].astype(F32) + tn(mixed_t[:, rows], weight_low[...])

    def normalise():
        for b in range(TOK // 32):
            rows = slice(b * 32, (b + 1) * 32)
            hidden = zed[rows, :]
            inv = lax.rsqrt(jnp.sum(hidden * hidden, axis=1, keepdims=True) * (1.0 / D) + EPSILON)
            hidden = hidden * inv
            zed[rows, :] = hidden
            rms_inv[rows, :] = inv
            high = hidden.astype(BF16)
            zed_high[rows, :] = high
            zed_low[rows, :] = (hidden - high.astype(F32)).astype(BF16)
        return nn(member[...], zed_high[...]) + nn(member[...], zed_low[...])

    for r in range(1, ROWS_DEV):
        arrive(r)
    weight_copy = load(weight_hbm, weight, load_sem.at[0])
    resid_copy = load(resid_hbm, resid, resid_sem)
    for step in range(1, ROWS_DEV + 2):
        for p in range(PAIRS):
            if step < ROWS_DEV:
                score(step, p)
            if step > 1:
                mix(step - 2, p)
            if step <= ROWS_DEV:
                soften(step - 1, p)
    weight_copy.wait()
    resid_copy.wait()
    weight_low[...] = weight[...].astype(BF16)
    for c in range(4):
        project(c)
    sums = normalise()
    error_copy = load(error_hbm.at[0], error, load_sem.at[1])
    keep_copies = [
        load(momentum_hbm, momentum_keep, load_sem.at[2]),
        load(weight, weight_keep, load_sem.at[3]),
    ]
    counts = jnp.sum(member[...].astype(F32), axis=1, keepdims=True)[0:24]
    gain_rows = gain_ref[...]
    gain = jnp.concatenate([gain_rows[k : k + 1, :] for k in range(6)], axis=1)
    zed_mean = sums[0:24] / counts
    means = zed_mean * gain
    inverse = lax.rsqrt(jnp.sum(means * means, axis=1, keepdims=True) + EPSILON)
    unit = means * inverse

    live_own = column_of(label_ref[...].astype(F32))
    wide_lane = lax.broadcasted_iota(jnp.int32, (8, D), 1)
    marked = jnp.where(
        live_own > 0.5, unit[0:8], jnp.where(wide_lane == 0, UNLABELLED, 0.0)
    )
    own_cands = unit[8:24].astype(BF16)
    gather[me, :, 0:D] = own_cands
    gather[me, :, D:PACK] = jnp.concatenate([marked[:, :HALF], marked[:, HALF:]], axis=0).astype(
        BF16
    )
    own_anchors = jnp.concatenate([marked, jnp.zeros_like(marked)], axis=0).astype(BF16)

    pl.semaphore_wait(barrier, spots + lines - 2)
    sends = []

    def send_block(block, device):
        copy = pltpu.make_async_remote_copy(
            src_ref=gather.at[block],
            dst_ref=gather.at[block],
            send_sem=gather_send.at[len(sends)],
            recv_sem=gather_recv.at[block],
            device_id=device,
            device_id_type=MESH,
        )
        copy.start()
        sends.append(copy)

    def await_block(block):
        pltpu.make_async_remote_copy(
            src_ref=gather.at[block],
            dst_ref=gather.at[block],
            send_sem=gather_send.at[0],
            recv_sem=gather_recv.at[block],
            device_id=sibling,
            device_id_type=MESH,
        ).wait_recv()

    line_order = [line] + [other_line(k) for k in range(lines - 1)]
    for k in far_lines:
        send_block(me, line_device(k)[1])
    for k in range(lines):
        block = (line_order[k] * 2 + side) * n_narrow + narrow
        if k:
            await_block(block)
        for d in cells:
            send_block(block, spot_device(d)[1])
        send_block(block, sibling)

    error_copy.wait()
    factor_parts = stacked_parts(factor_ref[...])
    error_rows = error[...]
    error_high = error_rows.astype(BF16)
    error_low = (error_rows - error_high.astype(F32)).astype(BF16)
    row_part = folded(nt(factor_parts, error_high) + nt(factor_parts, error_low), RANK)

    def flat_bias(x):
        high, middle, low = parts_of(x)
        spread = folded(
            nn(
                jnp.concatenate([high, gap, middle, gap, low, gap], axis=0).astype(BF16),
                spread_ref[...],
            ),
            16,
        )
        return jnp.sum(spread * head_mask_ref[...], axis=0, keepdims=True)

    def packed(gain_part, bias_part, scale_part):
        return jnp.concatenate(
            [gain_part]
            + [bias_part[:, k * LEN : (k + 1) * LEN] for k in range(3)]
            + [jnp.where(lane == 0, scale_part, 0.0), jnp.zeros((6, LEN), F32)],
            axis=0,
        )

    small_ref[16:32, LEN : 2 * LEN] = packed(gain_rows, flat_bias(bias_ref[...]), scale_ref[...])
    small_ref[16:32, 2 * LEN : 3 * LEN] = packed(gain_mom_ref[...], flat_bias(bias_mom_ref[...]), scale_mom_ref[...])

    for k in range(lines):
        for d in cells[::-1]:
            _, (other_wide, other_narrow) = spot_device(d)
            block = (line_order[k] * 2 + other_wide % 2) * n_narrow + other_narrow
            await_block(block)
            send_block(block, sibling)
    for k in range(lines):
        for d in [(0, 0, 0)] + cells[::-1]:
            _, (other_wide, other_narrow) = spot_device(d)
            block = (
                (line_order[k] * 2 + other_wide % 2) * n_narrow
                + other_narrow
                + 1
                - 2 * (narrow % 2)
            )
            await_block(block)
    blocks = count // GROUP
    temper = jnp.exp(scale_ref[...])

    def unpack(b, total):
        picked = gather[pl.ds(b * GROUP, GROUP), :, D:PACK].astype(F32)
        left = picked[:, 0:8, :].reshape(GROUP * 8, HALF)
        right = picked[:, 8:16, :].reshape(GROUP * 8, HALF)
        anchors_all[b] = jnp.concatenate([left, right], axis=1).astype(BF16)
        live = jnp.where(left[:, 0:1] < 1.5, 1.0, 0.0)
        return total + jnp.sum(live, axis=0, keepdims=True)

    live_total = looped(blocks, unpack, jnp.zeros((1, 1), F32))

    def cands_of(b):
        return gather[pl.ds(b * GROUP, GROUP), :, 0:D].reshape(GROUP * 16, D)

    first_lane = jnp.where(lax.broadcasted_iota(jnp.int32, (16, D), 1) == 0, 1.0, 0.0).astype(BF16)
    row16 = lax.broadcasted_iota(jnp.int32, (16, GROUP * 8), 0)
    lane16 = lax.broadcasted_iota(jnp.int32, (16, GROUP * 8), 1)
    per_live = 1.0 / live_total

    def columns(b, cand_grad):
        anchors = anchors_all[b]

        def part(c, state):
            top, total = state
            logits = temper * nt(cands_of(c), anchors)
            new_top = jnp.maximum(top, jnp.max(logits, axis=0, keepdims=True))
            total = total * jnp.exp(top - new_top) + jnp.sum(
                jnp.exp(logits - new_top), axis=0, keepdims=True
            )
            return new_top, total

        start = (jnp.full((1, GROUP * 8), -1e30, F32), jnp.zeros((1, GROUP * 8), F32))
        top, total = looped(blocks, part, start)
        log_total = top + jnp.log(total)
        live = jnp.where(nt(first_lane, anchors) < 1.5, per_live, 0.0)
        logits = temper * nt(own_cands, anchors)
        target = jnp.where(
            (row16 < 8) & (lane16 + b * (GROUP * 8) == row16 + me * ROWS_DEV), 1.0, 0.0
        )
        grad = (jnp.exp(logits - log_total) - target) * live
        return cand_grad + nn((temper * grad).astype(BF16), anchors)

    cand_grad = looped(blocks, columns, jnp.zeros((16, D), F32))

    def own_part(b, state):
        top, total = state
        logits = temper * nt(own_anchors, cands_of(b))
        own_scores[b] = logits
        new_top = jnp.maximum(top, jnp.max(logits, axis=1, keepdims=True))
        total = total * jnp.exp(top - new_top) + jnp.sum(
            jnp.exp(logits - new_top), axis=1, keepdims=True
        )
        return new_top, total

    start = (jnp.full((16, 1), -1e30, F32), jnp.zeros((16, 1), F32))
    top, total = looped(blocks, own_part, start)
    log_total = top + jnp.log(total)
    live16 = jnp.concatenate([live_own, jnp.zeros_like(live_own)], axis=0)
    row32 = lax.broadcasted_iota(jnp.int32, (16, GROUP * 16), 0)
    lane32 = lax.broadcasted_iota(jnp.int32, (16, GROUP * 16), 1)

    def own_grad(b, state):
        anchor_grad, positive, scale_grad = state
        logits = own_scores[b]
        target = jnp.where(
            (row32 < 8) & (lane32 + b * (GROUP * 16) == row32 + me * 2 * ROWS_DEV), 1.0, 0.0
        )
        positive = positive + jnp.sum(logits * target, axis=1, keepdims=True)
        grad = (jnp.exp(logits - log_total) - target) * (live16 * per_live)
        scale_grad = scale_grad + jnp.sum(grad * logits, axis=1, keepdims=True)
        anchor_grad = anchor_grad + nn((temper * grad).astype(BF16), cands_of(b))
        return anchor_grad, positive, scale_grad

    column = jnp.zeros((16, 1), F32)
    anchor_grad, positive, scale_grad = looped(
        blocks, own_grad, (jnp.zeros((16, D), F32), column, column)
    )
    loss_own = jnp.sum(live16 * (log_total - positive), axis=0, keepdims=True)
    scale_grad = jnp.sum(scale_grad, axis=0, keepdims=True)

    branch, mixed_grad = resid, zed_low
    unit_grad = jnp.concatenate([anchor_grad[0:8], cand_grad], axis=0)
    mean_grad = inverse * (unit_grad - unit * jnp.sum(unit * unit_grad, axis=1, keepdims=True))
    gain_grad = jnp.sum(mean_grad * zed_mean, axis=0, keepdims=True)
    high, middle, low = parts_of(mean_grad / counts * gain)
    wide_gap = jnp.zeros((8, D), F32)
    shares = jnp.concatenate(
        [high, wide_gap, middle, wide_gap, low, wide_gap, jnp.zeros((32, D), F32)], axis=0
    ).astype(BF16)
    wide_rows[...] = nn(member_t[...], shares)
    for b in range(TOK // 32):
        rows = slice(b * 32, (b + 1) * 32)
        zed_grad = wide_rows[rows, :]
        zed_rows = zed[rows, :]
        level = jnp.sum(zed_grad * zed_rows, axis=1, keepdims=True) * (1.0 / D)
        branch[rows, :] = (rms_inv[rows, :] * (zed_grad - zed_rows * level)).astype(BF16)
    by_token = folded(nt(factor_parts, branch[...]), RANK)
    row_part = row_part + folded(nt(stacked_parts(by_token), mixed_t[...]), RANK)

    def send_to(buffers, mine, device, send_sem, recv_sem):
        copy = pltpu.make_async_remote_copy(
            src_ref=buffers.at[mine],
            dst_ref=buffers.at[mine],
            send_sem=send_sem,
            recv_sem=recv_sem.at[mine],
            device_id=device,
            device_id_type=MESH,
        )
        copy.start()
        return copy

    def await_from(buffers, other, send_sem, recv_sem):
        pltpu.make_async_remote_copy(
            src_ref=buffers.at[other],
            dst_ref=buffers.at[other],
            send_sem=send_sem,
            recv_sem=recv_sem.at[other],
            device_id=sibling,
            device_id_type=MESH,
        ).wait_recv()

    def start_sum(which, plane):
        return [
            send_to(plane, spot, spot_device(d)[1], plane_send.at[which, k], plane_recv.at[which])
            for k, d in enumerate(offsets)
        ]

    def middle_sum(which, plane, along):
        for d in offsets[::-1]:
            await_from(plane, spot_device(d)[0], plane_send.at[which, 0], plane_recv.at[which])
        total = plane[0]
        for k in range(1, spots):
            total = total + plane[k]
        along[line] = total
        return [
            send_to(along, line, line_device(k)[1], line_send.at[which, k], line_recv.at[which])
            for k in far_lines
        ]

    def finish_sum(which, along):
        for k in far_lines[::-1]:
            await_from(along, line_device(k)[0], line_send.at[which, 0], line_recv.at[which])
        total = along[0]
        for k in range(1, lines):
            total = total + along[k]
        return total

    scalars = jnp.where(lane == 0, loss_own, jnp.where(lane == 1, scale_grad, 0.0))
    extra = jnp.concatenate(
        [gain_grad[:, k * LEN : (k + 1) * LEN] for k in range(6)]
        + [scalars, jnp.zeros((1, LEN), F32)],
        axis=0,
    )
    plane1[spot, :, 0:D] = row_part
    plane1[spot, :, D:WIDTH] = extra
    sends.extend(start_sum(0, plane1))

    for b in range(3):
        rows = slice(b * 256, (b + 1) * 256)
        full = error[rows, :] + nn(mixed_t[rows, :], branch[...])
        matrix[rows, :] = full
        high = full.astype(BF16)
        matrix_high[rows, :] = high
        matrix_low[rows, :] = (full - high.astype(F32)).astype(BF16)
    matrix_copy = pltpu.make_async_copy(matrix, matrix_hbm, out_sem)
    matrix_copy.start()

    for c in range(4):
        rows = slice(c * 256, (c + 1) * 256)
        mixed_grad[rows, :] = nt(branch[rows, :], weight_low[...]).astype(BF16)
    sends.extend(middle_sum(0, plane1, line1))
    for p in range(PAIRS):
        cols = slice(p * LEN, (p + 1) * LEN)

        def back(r, acc):
            offset = pl.multiple_of(r * LEN, LEN)
            rows = pl.ds(offset, LEN)
            grad = mixed_grad[rows, cols]
            right = jnp.concatenate([grad * first, grad * second], axis=0)
            prob_grad = nt(proj[2, rows, cols], right)
            prob = jnp.concatenate(
                [probs[r * HEADS + 2 * p], probs[r * HEADS + 2 * p + 1]], axis=1
            )
            product = prob * prob_grad
            return acc + (product - prob * jnp.sum(product, axis=0, keepdims=True))

        acc = lax.fori_loop(0, ROWS_DEV, back, jnp.zeros((LEN, 2 * LEN), F32), unroll=True)
        for half in range(2):
            padded = jnp.concatenate(
                [acc[:, half * LEN : (half + 1) * LEN], jnp.zeros((LEN, LEN), F32)], axis=1
            )
            sheared = padded[0:8]
            for a in range(1, LEN // 8):
                sheared = sheared + pltpu.roll(padded[8 * a : 8 * a + 8], 2 * LEN - 8 * a, 1)
            for bit in (1, 2, 4):
                moved = pltpu.roll(sheared, 2 * LEN - bit, 1)
                sheared = jnp.where((row8 & bit) != 0, moved, sheared)
            head = 2 * p + half
            diagonals[head : head + 1, :] = jnp.sum(sheared, axis=0, keepdims=True)
    diagonals[HEADS:16, :] = jnp.zeros((16 - HEADS, 2 * LEN), F32)
    high, middle, low = parts_of(diagonals[...])
    by_bucket = folded(
        nn(jnp.concatenate([high, middle, low], axis=0).astype(BF16), onehot_ref[...]), 16
    )
    bias_grad = jnp.sum(by_bucket * head_mask_ref[...], axis=0, keepdims=True)

    total = finish_sum(0, line1)
    small_ref[16:24, 0:LEN] = total[:, D:WIDTH]
    ortho = total[:, 0:D]
    rank_row = lax.broadcasted_iota(jnp.int32, (RANK, 1), 0)
    for k in range(RANK):
        vector = ortho[k : k + 1, :]
        dots = jnp.sum(ortho * vector, axis=1, keepdims=True)
        norm = lax.rsqrt(dots[k : k + 1, :] + EPSILON)
        vector = vector * norm
        ortho = jnp.where(
            rank_row > k, ortho - (dots * norm) * vector, jnp.where(rank_row == k, vector, ortho)
        )
    small_ref[0:8, :] = ortho
    ortho_parts = stacked_parts(ortho)
    plane2[spot, :, 0:D] = folded(
        nn(ortho_parts, matrix_high[...]) + nn(ortho_parts, matrix_low[...]), RANK
    )
    plane2[spot, :, D:WIDTH] = jnp.concatenate(
        [bias_grad[:, k * LEN : (k + 1) * LEN] for k in range(3)] + [jnp.zeros((5, LEN), F32)],
        axis=0,
    )
    sends.extend(start_sum(1, plane2))
    for copy in sends:
        copy.wait_send()
    matrix_copy.wait()
    for copy in keep_copies:
        copy.wait()
    last_sends = middle_sum(1, plane2, line2)
    total = finish_sum(1, line2)
    small_ref[8:16, :] = total[:, 0:D]
    small_ref[24:32, 0:LEN] = total[:, D:WIDTH]
    small_ref[16:32, 3 * LEN : 4 * LEN] = jnp.broadcast_to(live_total, (16, LEN))
    small_ref[16:32, 4 * LEN : D] = jnp.zeros((16, D - 4 * LEN), F32)
    for copy in last_sends:
        copy.wait_send()


def update_kernel(
    count,
    small_ref,
    matrix_ref,
    weight_ref,
    momentum_ref,
    weight_out,
    momentum_out,
    error_out,
    vector_out,
    vector_mom_out,
    loss_out,
    norm_out,
    fnew_out,
    live_out,
    matrix,
    weight,
    momentum,
    store_sem,
):
    ortho = small_ref[0:8, :]
    fnew = small_ref[8:16, :]
    oh, om, ol = parts_of(ortho)
    fh, fm, fl = parts_of(fnew)
    pad = jnp.zeros((16, D), F32)
    left = jnp.concatenate([oh, oh, om, om, oh, ol, pad], axis=0).astype(BF16)
    right = jnp.concatenate([fh, fm, fh, fm, fl, fh, pad], axis=0).astype(BF16)
    copies = []

    def send_out(source, target, rows, sem):
        copy = pltpu.make_async_copy(source.at[rows, :], target.at[rows, :], sem)
        copy.start()
        copies.append(copy)

    for b in range(6):
        rows = slice(b * LEN, (b + 1) * LEN)
        approx = tn(left[:, rows], right)
        weight[rows, :] = approx
        matrix[rows, :] = matrix_ref[rows, :] - approx * (1.0 / count)
        send_out(matrix, error_out.at[0], rows, store_sem.at[b, 2])

    square = jnp.zeros((RANK, 1), F32)
    for k in range(RANK):
        left = jnp.sum(ortho * ortho[k : k + 1, :], axis=1, keepdims=True)
        right = jnp.sum(fnew * fnew[k : k + 1, :], axis=1, keepdims=True)
        square = square + left * right
    square = jnp.sum(square, axis=0, keepdims=True)
    vec = small_ref[16:32, 0:LEN]
    lane = lax.broadcasted_iota(jnp.int32, (1, LEN), 1)
    scale_row = jnp.where(lane == 0, vec[6:7, 1:2], 0.0)
    grad = jnp.concatenate(
        [vec[0:6], vec[8:11], scale_row, jnp.zeros((6, LEN), F32)], axis=0
    )
    square = square + jnp.sum(
        jnp.sum(grad * grad, axis=1, keepdims=True), axis=0, keepdims=True
    )
    norm = jnp.sqrt(square)
    clip = CLIP_NORM / jnp.maximum(norm, CLIP_NORM)

    for b in range(6):
        rows = slice(b * LEN, (b + 1) * LEN)
        mom = MOMENTUM_DECAY * momentum_ref[rows, :] + clip * weight[rows, :]
        momentum[rows, :] = mom
        send_out(momentum, momentum_out, rows, store_sem.at[b, 0])
        weight[rows, :] = weight_ref[rows, :] - RATE_MATRIX * mom
        send_out(weight, weight_out, rows, store_sem.at[b, 1])

    row = lax.broadcasted_iota(jnp.int32, (16, 1), 0)
    rate = jnp.where(row < 6, RATE_GAIN, jnp.where(row < 9, RATE_BIAS, RATE_SCALE))
    mom = MOMENTUM_DECAY * small_ref[16:32, 2 * LEN : 3 * LEN] + clip * grad
    vector_mom_out[...] = mom
    vector_out[...] = small_ref[16:32, LEN : 2 * LEN] - rate * mom
    loss_out[...] = vec[6:7, 0:1]
    norm_out[...] = norm
    fnew_out[...] = fnew
    live_out[...] = small_ref[16:17, 3 * LEN : 3 * LEN + 1]
    for copy in copies:
        copy.wait()


def local(
    n_wide,
    n_narrow,
    projected,
    layer_input,
    segment_ids,
    pad_mask,
    roles,
    labelled,
    out_weight,
    out_momentum,
    errors,
    factors,
    norm_gain,
    position_bias,
    log_scale,
    gain_momentum,
    bias_momentum,
    scale_momentum,
):
    count = n_wide * n_narrow
    lines = n_wide // 2
    spots = 2 * n_narrow
    blocks = count // GROUP
    sends = (lines - 1) + lines * n_narrow + lines * (n_narrow - 1)
    anywhere = pl.BlockSpec(memory_space=pl.ANY)
    vmem = pl.BlockSpec(memory_space=pltpu.VMEM)

    def stay(x):
        return pltpu.with_memory_space_constraint(x, pltpu.HBM)

    in_hbm = pl.BlockSpec(memory_space=pltpu.HBM)
    kept = pl.pallas_call(
        functools.partial(step_kernel, n_wide, n_narrow),
        out_shape=(
            jax.ShapeDtypeStruct((32, D), F32),
            jax.ShapeDtypeStruct((D, D), F32),
            jax.ShapeDtypeStruct((D, D), F32),
            jax.ShapeDtypeStruct((D, D), F32),
        ),
        in_specs=[in_hbm] * 20,
        out_specs=(vmem, anywhere, anywhere, anywhere),
        scratch_shapes=[
            pltpu.VMEM((ROWS_DEV, LEN), jnp.int32),
            pltpu.VMEM((ROWS_DEV, LEN), jnp.int32),
            pltpu.VMEM((3, ROWS_DEV), jnp.int32),
            pltpu.VMEM((1, ROWS_DEV), jnp.int32),
            pltpu.VMEM((RANK, D), F32),
            pltpu.VMEM((6, LEN), F32),
            pltpu.VMEM((6, LEN), F32),
            pltpu.VMEM((HEADS, BUCKETS), F32),
            pltpu.VMEM((HEADS, BUCKETS), F32),
            pltpu.VMEM((1, 1), F32),
            pltpu.VMEM((1, 1), F32),
            pltpu.VMEM((2 * LEN, FLAT), BF16),
            pltpu.VMEM((BUCKETS, FLAT), BF16),
            pltpu.VMEM((2 * LEN, BUCKETS), BF16),
            pltpu.VMEM((16, FLAT), F32),
            pltpu.SemaphoreType.DMA((15,)),
            pltpu.VMEM((3, TOK, D), BF16),
            pltpu.VMEM((TOK, D), BF16),
            pltpu.VMEM((D, D), F32),
            pltpu.VMEM((D, D), F32),
            pltpu.VMEM((D, D), BF16),
            pltpu.VMEM((HEADS, LEN, LEN), F32),
            pltpu.VMEM((ROWS_DEV, LEN, LEN), BF16),
            pltpu.VMEM((ROWS_DEV, LEN, LEN), BF16),
            pltpu.VMEM((32, TOK), BF16),
            pltpu.VMEM((TOK, LEN), BF16),
            pltpu.VMEM((ROWS_DEV * HEADS, LEN, LEN), F32),
            pltpu.VMEM((PAIRS, LEN, 2 * LEN), F32),
            pltpu.VMEM((PAIRS, LEN, 2 * LEN), F32),
            pltpu.VMEM((PAIRS, 2 * LEN, LEN), BF16),
            pltpu.VMEM((PAIRS, 2 * LEN, LEN), BF16),
            pltpu.VMEM((D, TOK), BF16),
            pltpu.VMEM((TOK, D), F32),
            pltpu.VMEM((TOK, D), F32),
            pltpu.VMEM((TOK, D), BF16),
            pltpu.VMEM((TOK, D), BF16),
            pltpu.VMEM((TOK, 1), F32),
            pltpu.VMEM((TOK, 1), F32),
            pltpu.VMEM((D, D), F32),
            pltpu.VMEM((D, D), BF16),
            pltpu.VMEM((D, D), BF16),
            pltpu.VMEM((count, 16, PACK), BF16),
            pltpu.VMEM((blocks, GROUP * 8, D), BF16),
            pltpu.VMEM((blocks, 16, GROUP * 16), F32),
            pltpu.VMEM((16, 2 * LEN), F32),
            pltpu.VMEM((spots, RANK, WIDTH), F32),
            pltpu.VMEM((lines, RANK, WIDTH), F32),
            pltpu.VMEM((spots, RANK, WIDTH), F32),
            pltpu.VMEM((lines, RANK, WIDTH), F32),
            pltpu.SemaphoreType.DMA((ROWS_DEV,)),
            pltpu.SemaphoreType.DMA,
            pltpu.SemaphoreType.DMA((4,)),
            pltpu.SemaphoreType.DMA,
            pltpu.SemaphoreType.DMA((sends,)),
            pltpu.SemaphoreType.DMA((count,)),
            pltpu.SemaphoreType.DMA((2, spots)),
            pltpu.SemaphoreType.DMA((2, spots)),
            pltpu.SemaphoreType.DMA((2, lines)),
            pltpu.SemaphoreType.DMA((2, lines)),
        ],
        compiler_params=pltpu.CompilerParams(
            collective_id=0, has_side_effects=True, vmem_limit_bytes=(45 if blocks == 1 else 60) * 2**20
        ),
        name="step",
    )(
        stay(projected),
        stay(layer_input),
        stay(out_weight),
        stay(errors),
        stay(out_momentum),
        stay(segment_ids.reshape(ROWS_DEV, LEN)),
        stay(pad_mask.reshape(ROWS_DEV, LEN)),
        stay(roles.T),
        stay(labelled.reshape(1, ROWS_DEV)),
        stay(factors),
        stay(norm_gain.reshape(6, LEN)),
        stay(gain_momentum.reshape(6, LEN)),
        stay(position_bias.T),
        stay(bias_momentum.T),
        log_scale.reshape(1, 1),
        scale_momentum.reshape(1, 1),
        stay(jnp.asarray(diagonal_onehot(FLAT), BF16)),
        stay(jnp.asarray(bucket_spread(), BF16)),
        stay(jnp.asarray(diagonal_onehot(BUCKETS), BF16)),
        stay(jnp.asarray(head_mask())),
    )
    outs = pl.pallas_call(
        functools.partial(update_kernel, count),
        out_shape=(
            jax.ShapeDtypeStruct((D, D), F32),
            jax.ShapeDtypeStruct((D, D), F32),
            jax.ShapeDtypeStruct((1, D, D), F32),
            jax.ShapeDtypeStruct((16, LEN), F32),
            jax.ShapeDtypeStruct((16, LEN), F32),
            jax.ShapeDtypeStruct((1, 1), F32),
            jax.ShapeDtypeStruct((1, 1), F32),
            jax.ShapeDtypeStruct((RANK, D), F32),
            jax.ShapeDtypeStruct((1, 1), F32),
        ),
        in_specs=[vmem] * 4,
        out_specs=(anywhere,) * 3 + (vmem,) * 6,
        scratch_shapes=[
            pltpu.VMEM((D, D), F32),
            pltpu.VMEM((D, D), F32),
            pltpu.VMEM((D, D), F32),
            pltpu.SemaphoreType.DMA((6, 3)),
        ],
        compiler_params=pltpu.CompilerParams(vmem_limit_bytes=24 * 2**20),
        name="update",
    )(*kept)
    weight_new, weight_mom, errors_new, vec_new, vec_mom, loss, norm, fnew, live_total = outs
    size = D + FLAT + 1
    return (
        weight_new,
        weight_mom,
        errors_new,
        fnew,
        vec_new.reshape(-1)[:size],
        vec_mom.reshape(-1)[:size],
        loss.reshape(1),
        live_total.reshape(1),
        norm.reshape(1),
    )


def solution(mesh):
    both = ("wide", "narrow")
    in_specs = (
        P(None, both, None),
        P(both, None),
        P(both),
        P(both),
        P(both, None),
        P(both),
        P(),
        P(),
        P(both, None, None),
        P(),
        P(),
        P(),
        P(),
        P(),
        P(),
        P(),
    )
    out_specs = (P(), P(), P(both, None, None), P(), P(), P(), P(), P(), P())
    return jax.shard_map(
        functools.partial(local, mesh.shape["wide"], mesh.shape["narrow"]),
        mesh=mesh,
        in_specs=in_specs,
        out_specs=out_specs,
        check_vma=False,
    )
```

```python
import functools

import jax
import jax.numpy as jnp
import numpy as np
from jax import lax
from jax.experimental import pallas as pl
from jax.experimental.pallas import tpu as pltpu
from jax.sharding import PartitionSpec as P

D = 768
HEADS = 12
HEAD_DIM = 64
BUCKETS = 32
LEN = 128
ROWS_DEV = 8
RANK = 8
TOK = ROWS_DEV * LEN
PAIRS = HEADS // 2
HALF = D // 2
FLAT = BUCKETS * HEADS
PACK = D + HALF
GROUP = 32
WIDTH = D + 128

EPSILON = 1e-06
MOMENTUM_DECAY = 0.9
CLIP_NORM = 0.01
RATE_MATRIX = 50000.0
RATE_GAIN = 4000.0
RATE_BIAS = 2000.0
RATE_SCALE = 10.0
MASKED = -float(2**30)
UNLABELLED = 2.0
F32 = jnp.float32
BF16 = jnp.bfloat16
MESH = pl.DeviceIdType.MESH


def diagonal_buckets():
    half_count = BUCKETS // 2
    exact_count = half_count // 2
    table = np.full((2 * LEN,), -1, np.int64)
    for k in range(2 * LEN):
        if k == LEN:
            continue
        relative = -k if k < LEN else 2 * LEN - k
        distance = abs(relative)
        larger = exact_count + int(
            np.log(np.maximum(distance, 1) / exact_count)
            / np.log(128.0 / exact_count)
            * (half_count - exact_count)
        )
        larger = min(larger, half_count - 1)
        table[k] = (half_count if relative > 0 else 0) + (
            distance if distance < exact_count else larger
        )
    return table


def diagonal_onehot(width):
    spread = np.arange(width) // (width // BUCKETS)
    return (diagonal_buckets()[:, None] == spread[None, :]).astype(np.float32)


def bucket_spread():
    return (np.arange(BUCKETS)[:, None] == (np.arange(FLAT) // HEADS)[None, :]).astype(np.float32)


def head_mask():
    return (np.arange(16)[:, None] == (np.arange(FLAT) % HEADS)[None, :]).astype(np.float32)


def nn(left, right):
    return lax.dot_general(
        left, right, (((1,), (0,)), ((), ())), preferred_element_type=F32
    )


def nt(left, right):
    return lax.dot_general(
        left, right, (((1,), (1,)), ((), ())), preferred_element_type=F32
    )


def tn(left, right):
    return lax.dot_general(
        left, right, (((0,), (0,)), ((), ())), preferred_element_type=F32
    )


def parts_of(x):
    high = x.astype(BF16).astype(F32)
    rest = x - high
    middle = rest.astype(BF16).astype(F32)
    return high, middle, rest - middle


def stacked_parts(x):
    high, middle, low = parts_of(x)
    return jnp.concatenate([high, middle, low, jnp.zeros_like(x)], axis=0).astype(BF16)


def folded(y, rows):
    return y[0:rows] + y[rows : 2 * rows] + y[2 * rows : 3 * rows]


def looped(count, body, carry):
    if count == 1:
        return body(0, carry)
    return lax.fori_loop(0, count, body, carry)


def step_kernel(
    n_wide,
    n_narrow,
    proj_hbm,
    resid_hbm,
    weight_hbm,
    error_hbm,
    momentum_hbm,
    seg_hbm,
    pad_hbm,
    roles_hbm,
    label_hbm,
    factor_hbm,
    gain_hbm,
    gain_mom_hbm,
    bias_hbm,
    bias_mom_hbm,
    scale_hbm,
    scale_mom_hbm,
    onehot_hbm,
    spread_hbm,
    diagonal_hbm,
    head_mask_hbm,
    small_ref,
    matrix_hbm,
    weight_keep,
    momentum_keep,
    seg_ref,
    pad_ref,
    roles_ref,
    label_ref,
    factor_ref,
    gain_ref,
    gain_mom_ref,
    bias_ref,
    bias_mom_ref,
    scale_ref,
    scale_mom_ref,
    onehot_ref,
    spread_ref,
    diagonal_ref,
    head_mask_ref,
    small_sem,
    proj,
    resid,
    weight,
    error,
    weight_low,
    bias_table,
    key_extra,
    query_extra,
    member,
    member_t,
    probs,
    score_even,
    score_odd,
    prob_even,
    prob_odd,
    mixed_t,
    wide_rows,
    zed,
    zed_high,
    zed_low,
    rms_inv,
    levels,
    matrix,
    matrix_high,
    matrix_low,
    matrix_rest,
    gather,
    anchors_all,
    own_scores,
    diagonals,
    plane1,
    line1,
    plane2,
    line2,
    row_sem,
    resid_sem,
    load_sem,
    out_sem,
    gather_send,
    gather_recv,
    plane_send,
    plane_recv,
    line_send,
    line_recv,
):
    count = n_wide * n_narrow
    lines = n_wide // 2
    spots = 2 * n_narrow
    wide = lax.axis_index("wide")
    narrow = lax.axis_index("narrow")
    me = wide * n_narrow + narrow
    line = wide // 2
    side = wide % 2
    spot = side * n_narrow + narrow

    y_size = n_narrow // 2
    row_at, core = narrow // 2, narrow % 2
    offsets = sorted(
        (
            (dx, dy, dc)
            for dx in range(2)
            for dy in range(y_size)
            for dc in range(2)
            if dx or dy or dc
        ),
        key=lambda d: (-(d[0] > 0) - (d[1] > 0), -d[2]),
    )
    far_lines = sorted(range(1, lines), key=lambda k: -min(k, lines - k))

    def spot_device(d):
        dx, dy, dc = d
        other_side = (side + dx) % 2
        other_narrow = (row_at + dy) % y_size * 2 + (core + dc) % 2
        return other_side * n_narrow + other_narrow, (line * 2 + other_side, other_narrow)

    def line_device(k):
        other = (line + k) % lines
        return other, (other * 2 + side, narrow)

    def other_line(k):
        return k + (k - line + lines) // lines

    cells = [d for d in offsets if not d[2]]

    sibling = (wide, narrow + 1 - 2 * (narrow % 2))

    def load(source, target, sem):
        copy = pltpu.make_async_copy(source, target, sem)
        copy.start()
        return copy

    mask_loads = [load(seg_hbm, seg_ref, small_sem.at[0]), load(pad_hbm, pad_ref, small_sem.at[1])]
    first_row = load(
        proj_hbm.at[:, pl.ds(0, LEN), :], proj.at[:, pl.ds(0, LEN), :], row_sem.at[0]
    )
    bias_loads = [
        load(bias_hbm, bias_ref, small_sem.at[2]),
        load(diagonal_hbm, diagonal_ref, small_sem.at[3]),
    ]
    later = pl.ds(LEN, TOK - LEN)
    later_rows = load(proj_hbm.at[:, later, :], proj.at[:, later, :], row_sem.at[1])
    rest_loads = [
        load(source, target, small_sem.at[4 + k])
        for k, (source, target) in enumerate(
            (
                (roles_hbm, roles_ref),
                (label_hbm, label_ref),
                (factor_hbm, factor_ref),
                (gain_hbm, gain_ref),
                (gain_mom_hbm, gain_mom_ref),
                (bias_mom_hbm, bias_mom_ref),
                (scale_hbm, scale_ref),
                (scale_mom_hbm, scale_mom_ref),
                (onehot_hbm, onehot_ref),
                (spread_hbm, spread_ref),
                (head_mask_hbm, head_mask_ref),
            )
        )
    ]
    barrier = pltpu.get_barrier_semaphore()
    for d in offsets:
        pl.semaphore_signal(barrier, inc=1, device_id=spot_device(d)[1], device_id_type=MESH)
    for k in far_lines:
        pl.semaphore_signal(barrier, inc=1, device_id=line_device(k)[1], device_id_type=MESH)

    for copy in mask_loads:
        copy.wait()
    code = jnp.where(pad_ref[...] == 1, seg_ref[...], 3).astype(F32)
    seg_f = seg_ref[...].astype(F32)
    fill = jnp.zeros((LEN - 16, LEN), F32)
    code_t = jnp.concatenate([code, seg_f, fill], axis=0).T
    lane = lax.broadcasted_iota(jnp.int32, (1, LEN), 1)
    sentence = lane.astype(F32)
    for r in range(ROWS_DEV):
        code_col = code_t[:, r : r + 1]
        seg_col = code_t[:, 8 + r : 9 + r]
        key_extra[r] = jnp.where(
            (sentence < 3.0) & (sentence != code_col), MASKED, 0.0
        ).astype(BF16)
        query_extra[r] = jnp.where(sentence == seg_col, 1.0, 0.0).astype(BF16)

    first = jnp.where(lane < HEAD_DIM, 1.0, 0.0).astype(BF16)
    second = jnp.where(lane < HEAD_DIM, 0.0, 1.0).astype(BF16)
    nothing = jnp.zeros((HEAD_DIM, LEN), BF16)

    score_rows = (score_even, score_odd)
    prob_rows = (prob_even, prob_odd)

    def rows_of(r):
        return slice(r * LEN, (r + 1) * LEN)

    def score(r, p):
        rows = rows_of(r)
        cols = slice(p * LEN, (p + 1) * LEN)
        query = proj[0, rows, cols]
        query_more = query_extra[r]
        left = jnp.concatenate([proj[1, rows, cols], key_extra[r]], axis=1)
        right = jnp.concatenate(
            [
                jnp.concatenate([query * first, query_more], axis=1),
                jnp.concatenate([query * second, query_more], axis=1),
            ],
            axis=0,
        )
        score_rows[r % 2][p] = nt(left, right)

    def soften(r, p):
        for half in range(2):
            head = 2 * p + half
            part = score_rows[r % 2][p, :, half * LEN : (half + 1) * LEN] + bias_table[head]
            part = jnp.exp(part - jnp.max(part, axis=0, keepdims=True))
            part = part * (1.0 / jnp.sum(part, axis=0, keepdims=True))
            probs[r * HEADS + head] = part
            prob_rows[r % 2][p, half * LEN : (half + 1) * LEN, :] = part.astype(BF16)

    def mix(r, p):
        rows = rows_of(r)
        cols = slice(p * LEN, (p + 1) * LEN)
        value_t = proj[2, rows, cols].T
        left = jnp.concatenate(
            [
                jnp.concatenate([value_t[:HEAD_DIM], nothing], axis=1),
                jnp.concatenate([nothing, value_t[HEAD_DIM:]], axis=1),
            ],
            axis=0,
        )
        mixed_t[cols, rows] = nn(left, prob_rows[r % 2][p]).astype(BF16)

    first_row.wait()
    for p in range(PAIRS):
        score(0, p)

    for copy in bias_loads:
        copy.wait()
    high, middle, low = parts_of(bias_ref[...])
    gap = jnp.zeros((4, BUCKETS), F32)
    diag_bias = folded(
        nt(
            jnp.concatenate([high, gap, middle, gap, low, gap], axis=0).astype(BF16),
            diagonal_ref[...],
        ),
        16,
    )
    row8 = lax.broadcasted_iota(jnp.int32, (8, 1), 0)
    for h in range(HEADS):
        sheared = jnp.broadcast_to(diag_bias[h : h + 1, :], (8, 2 * LEN))
        for bit in (1, 2, 4):
            sheared = jnp.where((row8 & bit) != 0, pltpu.roll(sheared, bit, 1), sheared)
        bias_table[h, 0:8, :] = sheared[:, :LEN]
        for a in range(1, LEN // 8):
            bias_table[h, 8 * a : 8 * a + 8, :] = pltpu.roll(sheared, 8 * a, 1)[:, :LEN]

    for copy in rest_loads:
        copy.wait()
    roles_f = roles_ref[...].astype(F32)
    slot = lane % 32
    row_of = lax.broadcasted_iota(jnp.int32, (32, 1), 0)
    same = lax.broadcasted_iota(jnp.int32, (8, 8), 0) == lax.broadcasted_iota(jnp.int32, (8, 8), 1)

    def column_of(row):
        return jnp.sum(jnp.where(same, row, 0.0), axis=1, keepdims=True)

    role_col = jnp.concatenate(
        [column_of(roles_f[k : k + 1, :]) for k in range(3)] + [jnp.full((8, 1), 9.0, F32)], axis=0
    )
    for r in range(ROWS_DEV):
        role_lane = jnp.where(
            slot < 8,
            roles_f[0:1, r : r + 1],
            jnp.where(slot < 16, roles_f[1:2, r : r + 1], roles_f[2:3, r : r + 1]),
        )
        role_lane = jnp.where((slot < 24) & (slot % 8 == r), role_lane, 9.0)
        member_t[r * LEN : (r + 1) * LEN, :] = jnp.where(
            role_lane == code_t[:, r : r + 1], 1.0, 0.0
        ).astype(BF16)
        member[:, r * LEN : (r + 1) * LEN] = jnp.where(
            (role_col == code[r : r + 1, :]) & (row_of % 8 == r), 1.0, 0.0
        ).astype(BF16)

    def project(c):
        rows = slice(c * 256, (c + 1) * 256)
        zed[rows, :] = resid[rows, :].astype(F32) + tn(mixed_t[:, rows], weight_low[...])

    def normalise():
        for b in range(TOK // 32):
            rows = slice(b * 32, (b + 1) * 32)
            hidden = zed[rows, :]
            inv = lax.rsqrt(jnp.sum(hidden * hidden, axis=1, keepdims=True) * (1.0 / D) + EPSILON)
            hidden = hidden * inv
            zed[rows, :] = hidden
            rms_inv[rows, :] = inv
            high = hidden.astype(BF16)
            zed_high[rows, :] = high
            zed_low[rows, :] = (hidden - high.astype(F32)).astype(BF16)
        return nn(member[...], zed_high[...]) + nn(member[...], zed_low[...])

    later_rows.wait()
    weight_copy = load(weight_hbm, weight, load_sem.at[0])
    resid_copy = load(resid_hbm, resid, resid_sem)
    for step in range(1, ROWS_DEV + 2):
        for p in range(PAIRS):
            if step < ROWS_DEV:
                score(step, p)
            if step > 1:
                mix(step - 2, p)
            if step <= ROWS_DEV:
                soften(step - 1, p)
    weight_copy.wait()
    resid_copy.wait()
    weight_low[...] = weight[...].astype(BF16)
    for c in range(4):
        project(c)
    sums = normalise()
    error_copy = load(error_hbm.at[0], error, load_sem.at[1])
    keep_copies = [
        load(momentum_hbm, momentum_keep, load_sem.at[2]),
        load(weight, weight_keep, load_sem.at[3]),
    ]
    counts = jnp.sum(member[...].astype(F32), axis=1, keepdims=True)[0:24]
    gain_rows = gain_ref[...]
    gain = jnp.concatenate([gain_rows[k : k + 1, :] for k in range(6)], axis=1)
    zed_mean = sums[0:24] / counts
    means = zed_mean * gain
    inverse = lax.rsqrt(jnp.sum(means * means, axis=1, keepdims=True) + EPSILON)
    unit = means * inverse

    live_own = column_of(label_ref[...].astype(F32))
    wide_lane = lax.broadcasted_iota(jnp.int32, (8, D), 1)
    marked = jnp.where(
        live_own > 0.5, unit[0:8], jnp.where(wide_lane == 0, UNLABELLED, 0.0)
    )
    own_cands = unit[8:24].astype(BF16)
    gather[me, :, 0:D] = own_cands
    gather[me, :, D:PACK] = jnp.concatenate([marked[:, :HALF], marked[:, HALF:]], axis=0).astype(
        BF16
    )
    own_anchors = jnp.concatenate([marked, jnp.zeros_like(marked)], axis=0).astype(BF16)

    pl.semaphore_wait(barrier, spots + lines - 2)
    sends = []

    def send_block(block, device):
        copy = pltpu.make_async_remote_copy(
            src_ref=gather.at[block],
            dst_ref=gather.at[block],
            send_sem=gather_send,
            recv_sem=gather_recv.at[block],
            device_id=device,
            device_id_type=MESH,
        )
        copy.start()
        sends.append(block)

    def await_block(block):
        pltpu.make_async_remote_copy(
            src_ref=gather.at[block],
            dst_ref=gather.at[block],
            send_sem=gather_send,
            recv_sem=gather_recv.at[block],
            device_id=sibling,
            device_id_type=MESH,
        ).wait_recv()

    line_order = [line] + [other_line(k) for k in range(lines - 1)]
    for k in far_lines:
        send_block(me, line_device(k)[1])
    for k in range(lines):
        block = (line_order[k] * 2 + side) * n_narrow + narrow
        if k:
            await_block(block)
        for d in cells:
            send_block(block, spot_device(d)[1])
        send_block(block, sibling)

    error_copy.wait()
    factor_parts = stacked_parts(factor_ref[...])
    error_rows = error[...]
    error_high = error_rows.astype(BF16)
    error_low = (error_rows - error_high.astype(F32)).astype(BF16)
    row_part = folded(nt(factor_parts, error_high) + nt(factor_parts, error_low), RANK)

    def flat_bias(x):
        high, middle, low = parts_of(x)
        spread = folded(
            nn(
                jnp.concatenate([high, gap, middle, gap, low, gap], axis=0).astype(BF16),
                spread_ref[...],
            ),
            16,
        )
        return jnp.sum(spread * head_mask_ref[...], axis=0, keepdims=True)

    def packed(gain_part, bias_part, scale_part):
        return jnp.concatenate(
            [gain_part]
            + [bias_part[:, k * LEN : (k + 1) * LEN] for k in range(3)]
            + [jnp.where(lane == 0, scale_part, 0.0), jnp.zeros((6, LEN), F32)],
            axis=0,
        )

    small_ref[16:32, LEN : 2 * LEN] = packed(gain_rows, flat_bias(bias_ref[...]), scale_ref[...])
    small_ref[16:32, 2 * LEN : 3 * LEN] = packed(gain_mom_ref[...], flat_bias(bias_mom_ref[...]), scale_mom_ref[...])

    for k in range(lines):
        for d in cells[::-1]:
            _, (other_wide, other_narrow) = spot_device(d)
            block = (line_order[k] * 2 + other_wide % 2) * n_narrow + other_narrow
            await_block(block)
            send_block(block, sibling)
    for k in range(lines):
        for d in [(0, 0, 0)] + cells[::-1]:
            _, (other_wide, other_narrow) = spot_device(d)
            block = (
                (line_order[k] * 2 + other_wide % 2) * n_narrow
                + other_narrow
                + 1
                - 2 * (narrow % 2)
            )
            await_block(block)
    blocks = count // GROUP
    temper = jnp.exp(scale_ref[...])

    def unpack(b, total):
        picked = gather[pl.ds(b * GROUP, GROUP), :, D:PACK].astype(F32)
        left = picked[:, 0:8, :].reshape(GROUP * 8, HALF)
        right = picked[:, 8:16, :].reshape(GROUP * 8, HALF)
        anchors_all[b] = jnp.concatenate([left, right], axis=1).astype(BF16)
        live = jnp.where(left[:, 0:1] < 1.5, 1.0, 0.0)
        return total + jnp.sum(live, axis=0, keepdims=True)

    live_total = looped(blocks, unpack, jnp.zeros((1, 1), F32))

    def cands_of(b):
        return gather[pl.ds(b * GROUP, GROUP), :, 0:D].reshape(GROUP * 16, D)

    first_lane = jnp.where(lax.broadcasted_iota(jnp.int32, (16, D), 1) == 0, 1.0, 0.0).astype(BF16)
    row16 = lax.broadcasted_iota(jnp.int32, (16, GROUP * 8), 0)
    lane16 = lax.broadcasted_iota(jnp.int32, (16, GROUP * 8), 1)
    per_live = 1.0 / live_total

    def columns(b, cand_grad):
        anchors = anchors_all[b]

        def part(c, state):
            top, total = state
            logits = temper * nt(cands_of(c), anchors)
            new_top = jnp.maximum(top, jnp.max(logits, axis=0, keepdims=True))
            total = total * jnp.exp(top - new_top) + jnp.sum(
                jnp.exp(logits - new_top), axis=0, keepdims=True
            )
            return new_top, total

        start = (jnp.full((1, GROUP * 8), -1e30, F32), jnp.zeros((1, GROUP * 8), F32))
        top, total = looped(blocks, part, start)
        log_total = top + jnp.log(total)
        live = jnp.where(nt(first_lane, anchors) < 1.5, per_live, 0.0)
        logits = temper * nt(own_cands, anchors)
        target = jnp.where(
            (row16 < 8) & (lane16 + b * (GROUP * 8) == row16 + me * ROWS_DEV), 1.0, 0.0
        )
        grad = (jnp.exp(logits - log_total) - target) * live
        return cand_grad + nn((temper * grad).astype(BF16), anchors)

    cand_grad = looped(blocks, columns, jnp.zeros((16, D), F32))

    def own_part(b, state):
        top, total = state
        logits = temper * nt(own_anchors, cands_of(b))
        own_scores[b] = logits
        new_top = jnp.maximum(top, jnp.max(logits, axis=1, keepdims=True))
        total = total * jnp.exp(top - new_top) + jnp.sum(
            jnp.exp(logits - new_top), axis=1, keepdims=True
        )
        return new_top, total

    start = (jnp.full((16, 1), -1e30, F32), jnp.zeros((16, 1), F32))
    top, total = looped(blocks, own_part, start)
    log_total = top + jnp.log(total)
    live16 = jnp.concatenate([live_own, jnp.zeros_like(live_own)], axis=0)
    row32 = lax.broadcasted_iota(jnp.int32, (16, GROUP * 16), 0)
    lane32 = lax.broadcasted_iota(jnp.int32, (16, GROUP * 16), 1)

    def own_grad(b, state):
        anchor_grad, positive, scale_grad = state
        logits = own_scores[b]
        target = jnp.where(
            (row32 < 8) & (lane32 + b * (GROUP * 16) == row32 + me * 2 * ROWS_DEV), 1.0, 0.0
        )
        positive = positive + jnp.sum(logits * target, axis=1, keepdims=True)
        grad = (jnp.exp(logits - log_total) - target) * (live16 * per_live)
        scale_grad = scale_grad + jnp.sum(grad * logits, axis=1, keepdims=True)
        anchor_grad = anchor_grad + nn((temper * grad).astype(BF16), cands_of(b))
        return anchor_grad, positive, scale_grad

    column = jnp.zeros((16, 1), F32)
    anchor_grad, positive, scale_grad = looped(
        blocks, own_grad, (jnp.zeros((16, D), F32), column, column)
    )
    loss_own = jnp.sum(live16 * (log_total - positive), axis=0, keepdims=True)
    scale_grad = jnp.sum(scale_grad, axis=0, keepdims=True)

    branch, mixed_grad = resid, zed_low
    unit_grad = jnp.concatenate([anchor_grad[0:8], cand_grad], axis=0)
    mean_grad = inverse * (unit_grad - unit * jnp.sum(unit * unit_grad, axis=1, keepdims=True))
    gain_grad = jnp.sum(mean_grad * zed_mean, axis=0, keepdims=True)
    high, middle, low = parts_of(mean_grad / counts * gain)
    wide_gap = jnp.zeros((8, D), F32)
    shares = jnp.concatenate(
        [high, wide_gap, middle, wide_gap, low, wide_gap, jnp.zeros((32, D), F32)], axis=0
    ).astype(BF16)
    wide_rows[...] = nn(member_t[...], shares)
    for b in range(TOK // 32):
        rows = slice(b * 32, (b + 1) * 32)
        zed_grad = wide_rows[rows, :]
        zed_rows = zed[rows, :]
        level = jnp.sum(zed_grad * zed_rows, axis=1, keepdims=True) * (1.0 / D)
        branch[rows, :] = (rms_inv[rows, :] * (zed_grad - zed_rows * level)).astype(BF16)
    by_token = folded(nt(factor_parts, branch[...]), RANK)
    row_part = row_part + folded(nt(stacked_parts(by_token), mixed_t[...]), RANK)

    def exchange(buffers, mine, devices, send_sem, recv_sem):
        for device in devices:
            pltpu.make_async_remote_copy(
                src_ref=buffers.at[mine],
                dst_ref=buffers.at[mine],
                send_sem=send_sem,
                recv_sem=recv_sem,
                device_id=device,
                device_id_type=MESH,
            ).start()

    def bytes_of(buffers, blocks, sem):
        part = buffers.at[pl.ds(0, blocks)]
        return pltpu.make_async_copy(part, part, sem)

    def start_sum(which, plane):
        devices = [spot_device(d)[1] for d in offsets]
        exchange(plane, spot, devices, plane_send.at[which], plane_recv.at[which])

    def middle_sum(which, plane, along):
        bytes_of(plane, spots - 1, plane_recv.at[which]).wait()
        total = plane[0]
        for k in range(1, spots):
            total = total + plane[k]
        along[line] = total
        devices = [line_device(k)[1] for k in far_lines]
        exchange(along, line, devices, line_send.at[which], line_recv.at[which])

    def finish_sum(which, along):
        bytes_of(along, lines - 1, line_recv.at[which]).wait()
        total = along[0]
        for k in range(1, lines):
            total = total + along[k]
        return total

    scalars = jnp.where(lane == 0, loss_own, jnp.where(lane == 1, scale_grad, 0.0))
    extra = jnp.concatenate(
        [gain_grad[:, k * LEN : (k + 1) * LEN] for k in range(6)]
        + [scalars, jnp.zeros((1, LEN), F32)],
        axis=0,
    )
    plane1[spot, :, 0:D] = row_part
    plane1[spot, :, D:WIDTH] = extra
    start_sum(0, plane1)

    for b in range(3):
        rows = slice(b * 256, (b + 1) * 256)
        full = error[rows, :] + nn(mixed_t[rows, :], branch[...])
        matrix[rows, :] = full
        high = full.astype(BF16)
        matrix_high[rows, :] = high
        rest = full - high.astype(F32)
        low = rest.astype(BF16)
        matrix_low[rows, :] = low
        matrix_rest[rows, :] = (rest - low.astype(F32)).astype(BF16)
    matrix_copy = pltpu.make_async_copy(matrix, matrix_hbm, out_sem)
    matrix_copy.start()

    for c in range(4):
        rows = slice(c * 256, (c + 1) * 256)
        mixed_grad[rows, :] = nt(branch[rows, :], weight_low[...]).astype(BF16)
    middle_sum(0, plane1, line1)
    for p in range(PAIRS):
        cols = slice(p * LEN, (p + 1) * LEN)

        def back(r, acc):
            offset = pl.multiple_of(r * LEN, LEN)
            rows = pl.ds(offset, LEN)
            grad = mixed_grad[rows, cols]
            right = jnp.concatenate([grad * first, grad * second], axis=0)
            prob_grad = nt(proj[2, rows, cols], right)
            prob = jnp.concatenate(
                [probs[r * HEADS + 2 * p], probs[r * HEADS + 2 * p + 1]], axis=1
            )
            product = prob * prob_grad
            return acc + (product - prob * jnp.sum(product, axis=0, keepdims=True))

        acc = lax.fori_loop(0, ROWS_DEV, back, jnp.zeros((LEN, 2 * LEN), F32), unroll=True)
        for half in range(2):
            padded = jnp.concatenate(
                [acc[:, half * LEN : (half + 1) * LEN], jnp.zeros((LEN, LEN), F32)], axis=1
            )
            sheared = padded[0:8]
            for a in range(1, LEN // 8):
                sheared = sheared + pltpu.roll(padded[8 * a : 8 * a + 8], 2 * LEN - 8 * a, 1)
            for bit in (1, 2, 4):
                moved = pltpu.roll(sheared, 2 * LEN - bit, 1)
                sheared = jnp.where((row8 & bit) != 0, moved, sheared)
            head = 2 * p + half
            diagonals[head : head + 1, :] = jnp.sum(sheared, axis=0, keepdims=True)
    diagonals[HEADS:16, :] = jnp.zeros((16 - HEADS, 2 * LEN), F32)
    high, middle, low = parts_of(diagonals[...])
    by_bucket = folded(
        nn(jnp.concatenate([high, middle, low], axis=0).astype(BF16), onehot_ref[...]), 16
    )
    bias_grad = jnp.sum(by_bucket * head_mask_ref[...], axis=0, keepdims=True)

    total = finish_sum(0, line1)
    small_ref[16:24, 0:LEN] = total[:, D:WIDTH]
    ortho = total[:, 0:D]
    row_parts = stacked_parts(ortho)
    product = folded(
        nn(row_parts, matrix_high[...])
        + nn(row_parts, matrix_low[...])
        + nn(row_parts, matrix_rest[...]),
        RANK,
    )
    rank_row = lax.broadcasted_iota(jnp.int32, (RANK, 1), 0)
    weights = []
    for k in range(RANK):
        vector = ortho[k : k + 1, :]
        dots = jnp.sum(ortho * vector, axis=1, keepdims=True)
        norm = lax.rsqrt(dots[k : k + 1, :] + EPSILON)
        vector = vector * norm
        weight_k = jnp.where(rank_row > k, dots * norm, 0.0)
        ortho = jnp.where(rank_row == k, vector, ortho - weight_k * vector)
        weights.append((norm, weight_k))
    for k, (norm, weight_k) in enumerate(weights):
        vector = product[k : k + 1, :] * norm
        product = jnp.where(rank_row == k, vector, product - weight_k * vector)
    small_ref[0:8, :] = ortho
    plane2[spot, :, 0:D] = product
    plane2[spot, :, D:WIDTH] = jnp.concatenate(
        [bias_grad[:, k * LEN : (k + 1) * LEN] for k in range(3)] + [jnp.zeros((5, LEN), F32)],
        axis=0,
    )
    start_sum(1, plane2)
    bytes_of(gather, len(sends), gather_send).wait()
    bytes_of(plane1, spots - 1, plane_send.at[0]).wait()
    bytes_of(line1, lines - 1, line_send.at[0]).wait()
    matrix_copy.wait()
    for copy in keep_copies:
        copy.wait()
    middle_sum(1, plane2, line2)
    total = finish_sum(1, line2)
    small_ref[8:16, :] = total[:, 0:D]
    small_ref[24:32, 0:LEN] = total[:, D:WIDTH]
    small_ref[16:32, 3 * LEN : 4 * LEN] = jnp.broadcast_to(live_total, (16, LEN))
    small_ref[16:32, 4 * LEN : D] = jnp.zeros((16, D - 4 * LEN), F32)
    bytes_of(plane2, spots - 1, plane_send.at[1]).wait()
    bytes_of(line2, lines - 1, line_send.at[1]).wait()


def update_kernel(
    count,
    small_ref,
    matrix_ref,
    weight_ref,
    momentum_ref,
    weight_out,
    momentum_out,
    error_out,
    vector_out,
    vector_mom_out,
    loss_out,
    norm_out,
    fnew_out,
    live_out,
    matrix,
    weight,
    momentum,
    store_sem,
):
    ortho = small_ref[0:8, :]
    fnew = small_ref[8:16, :]
    oh, om, ol = parts_of(ortho)
    fh, fm, fl = parts_of(fnew)
    pad = jnp.zeros((16, D), F32)
    left = jnp.concatenate([oh, oh, om, om, oh, ol, pad], axis=0).astype(BF16)
    right = jnp.concatenate([fh, fm, fh, fm, fl, fh, pad], axis=0).astype(BF16)
    copies = []

    def send_out(source, target, rows, sem):
        copy = pltpu.make_async_copy(source.at[rows, :], target.at[rows, :], sem)
        copy.start()
        copies.append(copy)

    for b in range(6):
        rows = slice(b * LEN, (b + 1) * LEN)
        approx = tn(left[:, rows], right)
        weight[rows, :] = approx
        matrix[rows, :] = matrix_ref[rows, :] - approx * (1.0 / count)
        send_out(matrix, error_out.at[0], rows, store_sem.at[b, 2])

    square = jnp.zeros((RANK, 1), F32)
    for k in range(RANK):
        left = jnp.sum(ortho * ortho[k : k + 1, :], axis=1, keepdims=True)
        right = jnp.sum(fnew * fnew[k : k + 1, :], axis=1, keepdims=True)
        square = square + left * right
    square = jnp.sum(square, axis=0, keepdims=True)
    vec = small_ref[16:32, 0:LEN]
    lane = lax.broadcasted_iota(jnp.int32, (1, LEN), 1)
    scale_row = jnp.where(lane == 0, vec[6:7, 1:2], 0.0)
    grad = jnp.concatenate(
        [vec[0:6], vec[8:11], scale_row, jnp.zeros((6, LEN), F32)], axis=0
    )
    square = square + jnp.sum(
        jnp.sum(grad * grad, axis=1, keepdims=True), axis=0, keepdims=True
    )
    norm = jnp.sqrt(square)
    clip = CLIP_NORM / jnp.maximum(norm, CLIP_NORM)

    for b in range(6):
        rows = slice(b * LEN, (b + 1) * LEN)
        mom = MOMENTUM_DECAY * momentum_ref[rows, :] + clip * weight[rows, :]
        momentum[rows, :] = mom
        send_out(momentum, momentum_out, rows, store_sem.at[b, 0])
        weight[rows, :] = weight_ref[rows, :] - RATE_MATRIX * mom
        send_out(weight, weight_out, rows, store_sem.at[b, 1])

    row = lax.broadcasted_iota(jnp.int32, (16, 1), 0)
    rate = jnp.where(row < 6, RATE_GAIN, jnp.where(row < 9, RATE_BIAS, RATE_SCALE))
    mom = MOMENTUM_DECAY * small_ref[16:32, 2 * LEN : 3 * LEN] + clip * grad
    vector_mom_out[...] = mom
    vector_out[...] = small_ref[16:32, LEN : 2 * LEN] - rate * mom
    loss_out[...] = vec[6:7, 0:1]
    norm_out[...] = norm
    fnew_out[...] = fnew
    live_out[...] = small_ref[16:17, 3 * LEN : 3 * LEN + 1]
    for copy in copies:
        copy.wait()


def local(
    n_wide,
    n_narrow,
    projected,
    layer_input,
    segment_ids,
    pad_mask,
    roles,
    labelled,
    out_weight,
    out_momentum,
    errors,
    factors,
    norm_gain,
    position_bias,
    log_scale,
    gain_momentum,
    bias_momentum,
    scale_momentum,
):
    count = n_wide * n_narrow
    lines = n_wide // 2
    spots = 2 * n_narrow
    blocks = count // GROUP
    anywhere = pl.BlockSpec(memory_space=pl.ANY)
    vmem = pl.BlockSpec(memory_space=pltpu.VMEM)

    def stay(x):
        return pltpu.with_memory_space_constraint(x, pltpu.HBM)

    in_hbm = pl.BlockSpec(memory_space=pltpu.HBM)
    kept = pl.pallas_call(
        functools.partial(step_kernel, n_wide, n_narrow),
        out_shape=(
            jax.ShapeDtypeStruct((32, D), F32),
            jax.ShapeDtypeStruct((D, D), F32),
            jax.ShapeDtypeStruct((D, D), F32),
            jax.ShapeDtypeStruct((D, D), F32),
        ),
        in_specs=[in_hbm] * 20,
        out_specs=(vmem, anywhere, anywhere, anywhere),
        scratch_shapes=[
            pltpu.VMEM((ROWS_DEV, LEN), jnp.int32),
            pltpu.VMEM((ROWS_DEV, LEN), jnp.int32),
            pltpu.VMEM((3, ROWS_DEV), jnp.int32),
            pltpu.VMEM((1, ROWS_DEV), jnp.int32),
            pltpu.VMEM((RANK, D), F32),
            pltpu.VMEM((6, LEN), F32),
            pltpu.VMEM((6, LEN), F32),
            pltpu.VMEM((HEADS, BUCKETS), F32),
            pltpu.VMEM((HEADS, BUCKETS), F32),
            pltpu.VMEM((1, 1), F32),
            pltpu.VMEM((1, 1), F32),
            pltpu.VMEM((2 * LEN, FLAT), BF16),
            pltpu.VMEM((BUCKETS, FLAT), BF16),
            pltpu.VMEM((2 * LEN, BUCKETS), BF16),
            pltpu.VMEM((16, FLAT), F32),
            pltpu.SemaphoreType.DMA((15,)),
            pltpu.VMEM((3, TOK, D), BF16),
            pltpu.VMEM((TOK, D), BF16),
            pltpu.VMEM((D, D), F32),
            pltpu.VMEM((D, D), F32),
            pltpu.VMEM((D, D), BF16),
            pltpu.VMEM((HEADS, LEN, LEN), F32),
            pltpu.VMEM((ROWS_DEV, LEN, LEN), BF16),
            pltpu.VMEM((ROWS_DEV, LEN, LEN), BF16),
            pltpu.VMEM((32, TOK), BF16),
            pltpu.VMEM((TOK, LEN), BF16),
            pltpu.VMEM((ROWS_DEV * HEADS, LEN, LEN), F32),
            pltpu.VMEM((PAIRS, LEN, 2 * LEN), F32),
            pltpu.VMEM((PAIRS, LEN, 2 * LEN), F32),
            pltpu.VMEM((PAIRS, 2 * LEN, LEN), BF16),
            pltpu.VMEM((PAIRS, 2 * LEN, LEN), BF16),
            pltpu.VMEM((D, TOK), BF16),
            pltpu.VMEM((TOK, D), F32),
            pltpu.VMEM((TOK, D), F32),
            pltpu.VMEM((TOK, D), BF16),
            pltpu.VMEM((TOK, D), BF16),
            pltpu.VMEM((TOK, 1), F32),
            pltpu.VMEM((TOK, 1), F32),
            pltpu.VMEM((D, D), F32),
            pltpu.VMEM((D, D), BF16),
            pltpu.VMEM((D, D), BF16),
            pltpu.VMEM((D, D), BF16),
            pltpu.VMEM((count, 16, PACK), BF16),
            pltpu.VMEM((blocks, GROUP * 8, D), BF16),
            pltpu.VMEM((blocks, 16, GROUP * 16), F32),
            pltpu.VMEM((16, 2 * LEN), F32),
            pltpu.VMEM((spots, RANK, WIDTH), F32),
            pltpu.VMEM((lines, RANK, WIDTH), F32),
            pltpu.VMEM((spots, RANK, WIDTH), F32),
            pltpu.VMEM((lines, RANK, WIDTH), F32),
            pltpu.SemaphoreType.DMA((2,)),
            pltpu.SemaphoreType.DMA,
            pltpu.SemaphoreType.DMA((4,)),
            pltpu.SemaphoreType.DMA,
            pltpu.SemaphoreType.DMA,
            pltpu.SemaphoreType.DMA((count,)),
            pltpu.SemaphoreType.DMA((2,)),
            pltpu.SemaphoreType.DMA((2,)),
            pltpu.SemaphoreType.DMA((2,)),
            pltpu.SemaphoreType.DMA((2,)),
        ],
        compiler_params=pltpu.CompilerParams(
            collective_id=0, has_side_effects=True, vmem_limit_bytes=(45 if blocks == 1 else 60) * 2**20
        ),
        name="step",
    )(
        stay(projected),
        stay(layer_input),
        stay(out_weight),
        stay(errors),
        stay(out_momentum),
        stay(segment_ids.reshape(ROWS_DEV, LEN)),
        stay(pad_mask.reshape(ROWS_DEV, LEN)),
        stay(roles.T),
        stay(labelled.reshape(1, ROWS_DEV)),
        stay(factors),
        stay(norm_gain.reshape(6, LEN)),
        stay(gain_momentum.reshape(6, LEN)),
        stay(position_bias.T),
        stay(bias_momentum.T),
        log_scale.reshape(1, 1),
        scale_momentum.reshape(1, 1),
        stay(jnp.asarray(diagonal_onehot(FLAT), BF16)),
        stay(jnp.asarray(bucket_spread(), BF16)),
        stay(jnp.asarray(diagonal_onehot(BUCKETS), BF16)),
        stay(jnp.asarray(head_mask())),
    )
    outs = pl.pallas_call(
        functools.partial(update_kernel, count),
        out_shape=(
            jax.ShapeDtypeStruct((D, D), F32),
            jax.ShapeDtypeStruct((D, D), F32),
            jax.ShapeDtypeStruct((1, D, D), F32),
            jax.ShapeDtypeStruct((16, LEN), F32),
            jax.ShapeDtypeStruct((16, LEN), F32),
            jax.ShapeDtypeStruct((1, 1), F32),
            jax.ShapeDtypeStruct((1, 1), F32),
            jax.ShapeDtypeStruct((RANK, D), F32),
            jax.ShapeDtypeStruct((1, 1), F32),
        ),
        in_specs=[vmem] * 4,
        out_specs=(anywhere,) * 3 + (vmem,) * 6,
        scratch_shapes=[
            pltpu.VMEM((D, D), F32),
            pltpu.VMEM((D, D), F32),
            pltpu.VMEM((D, D), F32),
            pltpu.SemaphoreType.DMA((6, 3)),
        ],
        compiler_params=pltpu.CompilerParams(vmem_limit_bytes=24 * 2**20),
        name="update",
    )(*kept)
    weight_new, weight_mom, errors_new, vec_new, vec_mom, loss, norm, fnew, live_total = outs
    size = D + FLAT + 1
    return (
        weight_new,
        weight_mom,
        errors_new,
        fnew,
        vec_new.reshape(-1)[:size],
        vec_mom.reshape(-1)[:size],
        loss.reshape(1),
        live_total.reshape(1),
        norm.reshape(1),
    )


def solution(mesh):
    both = ("wide", "narrow")
    in_specs = (
        P(None, both, None),
        P(both, None),
        P(both),
        P(both),
        P(both, None),
        P(both),
        P(),
        P(),
        P(both, None, None),
        P(),
        P(),
        P(),
        P(),
        P(),
        P(),
        P(),
    )
    out_specs = (P(), P(), P(both, None, None), P(), P(), P(), P(), P(), P())
    return jax.shard_map(
        functools.partial(local, mesh.shape["wide"], mesh.shape["narrow"]),
        mesh=mesh,
        in_specs=in_specs,
        out_specs=out_specs,
        check_vma=False,
    )
```

```python
import functools

import jax
import jax.numpy as jnp
import numpy as np
from jax import lax
from jax.experimental import pallas as pl
from jax.experimental.pallas import tpu as pltpu
from jax.sharding import PartitionSpec as P

D = 768
HEADS = 12
HEAD_DIM = 64
BUCKETS = 32
LEN = 128
ROWS_DEV = 8
RANK = 8
TOK = ROWS_DEV * LEN
PAIRS = HEADS // 2
HALF = D // 2
FLAT = BUCKETS * HEADS
PACK = D + HALF
GROUP = 32
WIDTH = D + 128

EPSILON = 1e-06
MOMENTUM_DECAY = 0.9
CLIP_NORM = 0.01
RATE_MATRIX = 50000.0
RATE_GAIN = 4000.0
RATE_BIAS = 2000.0
RATE_SCALE = 10.0
MASKED = -float(2**30)
UNLABELLED = 2.0
F32 = jnp.float32
BF16 = jnp.bfloat16
MESH = pl.DeviceIdType.MESH


def diagonal_buckets():
    half_count = BUCKETS // 2
    exact_count = half_count // 2
    table = np.full((2 * LEN,), -1, np.int64)
    for k in range(2 * LEN):
        if k == LEN:
            continue
        relative = -k if k < LEN else 2 * LEN - k
        distance = abs(relative)
        larger = exact_count + int(
            np.log(np.maximum(distance, 1) / exact_count)
            / np.log(128.0 / exact_count)
            * (half_count - exact_count)
        )
        larger = min(larger, half_count - 1)
        table[k] = (half_count if relative > 0 else 0) + (
            distance if distance < exact_count else larger
        )
    return table


def diagonal_onehot(width):
    spread = np.arange(width) // (width // BUCKETS)
    return (diagonal_buckets()[:, None] == spread[None, :]).astype(np.float32)


def bucket_spread():
    return (np.arange(BUCKETS)[:, None] == (np.arange(FLAT) // HEADS)[None, :]).astype(np.float32)


def head_mask():
    return (np.arange(16)[:, None] == (np.arange(FLAT) % HEADS)[None, :]).astype(np.float32)


def nn(left, right):
    return lax.dot_general(
        left, right, (((1,), (0,)), ((), ())), preferred_element_type=F32
    )


def nt(left, right):
    return lax.dot_general(
        left, right, (((1,), (1,)), ((), ())), preferred_element_type=F32
    )


def tn(left, right):
    return lax.dot_general(
        left, right, (((0,), (0,)), ((), ())), preferred_element_type=F32
    )


def parts_of(x):
    high = x.astype(BF16).astype(F32)
    rest = x - high
    middle = rest.astype(BF16).astype(F32)
    return high, middle, rest - middle


def stacked_parts(x):
    high, middle, low = parts_of(x)
    return jnp.concatenate([high, middle, low, jnp.zeros_like(x)], axis=0).astype(BF16)


def folded(y, rows):
    return y[0:rows] + y[rows : 2 * rows] + y[2 * rows : 3 * rows]


def looped(count, body, carry):
    if count == 1:
        return body(0, carry)
    return lax.fori_loop(0, count, body, carry)


def step_kernel(
    n_wide,
    n_narrow,
    proj_hbm,
    resid_hbm,
    weight_hbm,
    error_hbm,
    momentum_hbm,
    seg_hbm,
    pad_hbm,
    roles_hbm,
    label_hbm,
    factor_hbm,
    gain_hbm,
    gain_mom_hbm,
    bias_hbm,
    bias_mom_hbm,
    scale_hbm,
    scale_mom_hbm,
    onehot_hbm,
    spread_hbm,
    diagonal_hbm,
    head_mask_hbm,
    small_ref,
    matrix_hbm,
    weight_keep,
    momentum_keep,
    seg_ref,
    pad_ref,
    roles_ref,
    label_ref,
    factor_ref,
    gain_ref,
    gain_mom_ref,
    bias_ref,
    bias_mom_ref,
    scale_ref,
    scale_mom_ref,
    onehot_ref,
    spread_ref,
    diagonal_ref,
    head_mask_ref,
    small_sem,
    proj,
    resid,
    weight,
    error,
    weight_low,
    bias_table,
    key_extra,
    query_extra,
    member,
    member_t,
    probs,
    score_even,
    score_odd,
    prob_even,
    prob_odd,
    mixed_t,
    wide_rows,
    zed,
    zed_high,
    zed_low,
    rms_inv,
    levels,
    matrix,
    matrix_high,
    matrix_low,
    matrix_rest,
    gather,
    anchors_all,
    own_scores,
    diagonals,
    plane1,
    line1,
    plane2,
    line2,
    row_sem,
    resid_sem,
    load_sem,
    out_sem,
    gather_send,
    gather_recv,
    sibling_recv,
    plane_send,
    plane_recv,
    line_send,
    line_recv,
):
    count = n_wide * n_narrow
    lines = n_wide // 2
    spots = 2 * n_narrow
    wide = lax.axis_index("wide")
    narrow = lax.axis_index("narrow")
    me = wide * n_narrow + narrow
    line = wide // 2
    side = wide % 2
    spot = side * n_narrow + narrow

    y_size = n_narrow // 2
    row_at, core = narrow // 2, narrow % 2
    offsets = sorted(
        (
            (dx, dy, dc)
            for dx in range(2)
            for dy in range(y_size)
            for dc in range(2)
            if dx or dy or dc
        ),
        key=lambda d: (-(d[0] > 0) - (d[1] > 0), -d[2]),
    )
    far_lines = sorted(range(1, lines), key=lambda k: -min(k, lines - k))

    def spot_device(d):
        dx, dy, dc = d
        other_side = (side + dx) % 2
        other_narrow = (row_at + dy) % y_size * 2 + (core + dc) % 2
        return other_side * n_narrow + other_narrow, (line * 2 + other_side, other_narrow)

    def line_device(k):
        other = (line + k) % lines
        return other, (other * 2 + side, narrow)

    def other_line(k):
        return k + (k - line + lines) // lines

    cells = sorted((d for d in offsets if not d[2]), key=lambda d: (-(d[0] > 0) - (d[1] > 0), d[0]))

    sibling = (wide, narrow + 1 - 2 * (narrow % 2))

    def load(source, target, sem):
        copy = pltpu.make_async_copy(source, target, sem)
        copy.start()
        return copy

    mask_loads = [load(seg_hbm, seg_ref, small_sem.at[0]), load(pad_hbm, pad_ref, small_sem.at[1])]
    first_row = load(
        proj_hbm.at[:, pl.ds(0, LEN), :], proj.at[:, pl.ds(0, LEN), :], row_sem.at[0]
    )
    bias_loads = [
        load(bias_hbm, bias_ref, small_sem.at[2]),
        load(diagonal_hbm, diagonal_ref, small_sem.at[3]),
    ]
    later = pl.ds(LEN, TOK - LEN)
    later_rows = load(proj_hbm.at[:, later, :], proj.at[:, later, :], row_sem.at[1])
    rest_loads = [
        load(source, target, small_sem.at[4 + k])
        for k, (source, target) in enumerate(
            (
                (roles_hbm, roles_ref),
                (label_hbm, label_ref),
                (factor_hbm, factor_ref),
                (gain_hbm, gain_ref),
                (gain_mom_hbm, gain_mom_ref),
                (bias_mom_hbm, bias_mom_ref),
                (scale_hbm, scale_ref),
                (scale_mom_hbm, scale_mom_ref),
                (onehot_hbm, onehot_ref),
                (spread_hbm, spread_ref),
                (head_mask_hbm, head_mask_ref),
            )
        )
    ]
    barrier = pltpu.get_barrier_semaphore()
    for d in offsets:
        pl.semaphore_signal(barrier, inc=1, device_id=spot_device(d)[1], device_id_type=MESH)
    for k in far_lines:
        pl.semaphore_signal(barrier, inc=1, device_id=line_device(k)[1], device_id_type=MESH)

    for copy in mask_loads:
        copy.wait()
    code = jnp.where(pad_ref[...] == 1, seg_ref[...], 3).astype(F32)
    seg_f = seg_ref[...].astype(F32)
    fill = jnp.zeros((LEN - 16, LEN), F32)
    code_t = jnp.concatenate([code, seg_f, fill], axis=0).T
    lane = lax.broadcasted_iota(jnp.int32, (1, LEN), 1)
    sentence = lane.astype(F32)
    for r in range(ROWS_DEV):
        code_col = code_t[:, r : r + 1]
        seg_col = code_t[:, 8 + r : 9 + r]
        key_extra[r] = jnp.where(
            (sentence < 3.0) & (sentence != code_col), MASKED, 0.0
        ).astype(BF16)
        query_extra[r] = jnp.where(sentence == seg_col, 1.0, 0.0).astype(BF16)

    first = jnp.where(lane < HEAD_DIM, 1.0, 0.0).astype(BF16)
    second = jnp.where(lane < HEAD_DIM, 0.0, 1.0).astype(BF16)
    nothing = jnp.zeros((HEAD_DIM, LEN), BF16)

    score_rows = (score_even, score_odd)
    prob_rows = (prob_even, prob_odd)

    def rows_of(r):
        return slice(r * LEN, (r + 1) * LEN)

    def score(r, p):
        rows = rows_of(r)
        cols = slice(p * LEN, (p + 1) * LEN)
        query = proj[0, rows, cols]
        query_more = query_extra[r]
        left = jnp.concatenate([proj[1, rows, cols], key_extra[r]], axis=1)
        right = jnp.concatenate(
            [
                jnp.concatenate([query * first, query_more], axis=1),
                jnp.concatenate([query * second, query_more], axis=1),
            ],
            axis=0,
        )
        score_rows[r % 2][p] = nt(left, right)

    def soften(r, p):
        for half in range(2):
            head = 2 * p + half
            part = score_rows[r % 2][p, :, half * LEN : (half + 1) * LEN] + bias_table[head]
            part = jnp.exp(part - jnp.max(part, axis=0, keepdims=True))
            part = part * (1.0 / jnp.sum(part, axis=0, keepdims=True))
            probs[r * HEADS + head] = part
            prob_rows[r % 2][p, half * LEN : (half + 1) * LEN, :] = part.astype(BF16)

    def mix(r, p):
        rows = rows_of(r)
        cols = slice(p * LEN, (p + 1) * LEN)
        value_t = proj[2, rows, cols].T
        left = jnp.concatenate(
            [
                jnp.concatenate([value_t[:HEAD_DIM], nothing], axis=1),
                jnp.concatenate([nothing, value_t[HEAD_DIM:]], axis=1),
            ],
            axis=0,
        )
        mixed_t[cols, rows] = nn(left, prob_rows[r % 2][p]).astype(BF16)

    first_row.wait()
    for p in range(PAIRS):
        score(0, p)

    for copy in bias_loads:
        copy.wait()
    high, middle, low = parts_of(bias_ref[...])
    gap = jnp.zeros((4, BUCKETS), F32)
    diag_bias = folded(
        nt(
            jnp.concatenate([high, gap, middle, gap, low, gap], axis=0).astype(BF16),
            diagonal_ref[...],
        ),
        16,
    )
    row8 = lax.broadcasted_iota(jnp.int32, (8, 1), 0)
    for h in range(HEADS):
        sheared = jnp.broadcast_to(diag_bias[h : h + 1, :], (8, 2 * LEN))
        for bit in (1, 2, 4):
            sheared = jnp.where((row8 & bit) != 0, pltpu.roll(sheared, bit, 1), sheared)
        bias_table[h, 0:8, :] = sheared[:, :LEN]
        for a in range(1, LEN // 8):
            bias_table[h, 8 * a : 8 * a + 8, :] = pltpu.roll(sheared, 8 * a, 1)[:, :LEN]

    for copy in rest_loads:
        copy.wait()
    roles_f = roles_ref[...].astype(F32)
    slot = lane % 32
    row_of = lax.broadcasted_iota(jnp.int32, (32, 1), 0)
    same = lax.broadcasted_iota(jnp.int32, (8, 8), 0) == lax.broadcasted_iota(jnp.int32, (8, 8), 1)

    def column_of(row):
        return jnp.sum(jnp.where(same, row, 0.0), axis=1, keepdims=True)

    role_col = jnp.concatenate(
        [column_of(roles_f[k : k + 1, :]) for k in range(3)] + [jnp.full((8, 1), 9.0, F32)], axis=0
    )
    for r in range(ROWS_DEV):
        role_lane = jnp.where(
            slot < 8,
            roles_f[0:1, r : r + 1],
            jnp.where(slot < 16, roles_f[1:2, r : r + 1], roles_f[2:3, r : r + 1]),
        )
        role_lane = jnp.where((slot < 24) & (slot % 8 == r), role_lane, 9.0)
        member_t[r * LEN : (r + 1) * LEN, :] = jnp.where(
            role_lane == code_t[:, r : r + 1], 1.0, 0.0
        ).astype(BF16)
        member[:, r * LEN : (r + 1) * LEN] = jnp.where(
            (role_col == code[r : r + 1, :]) & (row_of % 8 == r), 1.0, 0.0
        ).astype(BF16)

    def project(c):
        rows = slice(c * 256, (c + 1) * 256)
        zed[rows, :] = resid[rows, :].astype(F32) + tn(mixed_t[:, rows], weight_low[...])

    def normalise():
        for b in range(TOK // 32):
            rows = slice(b * 32, (b + 1) * 32)
            hidden = zed[rows, :]
            inv = lax.rsqrt(jnp.sum(hidden * hidden, axis=1, keepdims=True) * (1.0 / D) + EPSILON)
            hidden = hidden * inv
            zed[rows, :] = hidden
            rms_inv[rows, :] = inv
            high = hidden.astype(BF16)
            zed_high[rows, :] = high
            zed_low[rows, :] = (hidden - high.astype(F32)).astype(BF16)
        return nn(member[...], zed_high[...]) + nn(member[...], zed_low[...])

    later_rows.wait()
    weight_copy = load(weight_hbm, weight, load_sem.at[0])
    resid_copy = load(resid_hbm, resid, resid_sem)
    for step in range(1, ROWS_DEV + 2):
        for p in range(PAIRS):
            if step < ROWS_DEV:
                score(step, p)
            if step > 1:
                mix(step - 2, p)
            if step <= ROWS_DEV:
                soften(step - 1, p)
    weight_copy.wait()
    resid_copy.wait()
    weight_low[...] = weight[...].astype(BF16)
    for c in range(4):
        project(c)
    sums = normalise()
    error_copy = load(error_hbm.at[0], error, load_sem.at[1])
    keep_copies = [
        load(momentum_hbm, momentum_keep, load_sem.at[2]),
        load(weight, weight_keep, load_sem.at[3]),
    ]
    counts = jnp.sum(member[...].astype(F32), axis=1, keepdims=True)[0:24]
    gain_rows = gain_ref[...]
    gain = jnp.concatenate([gain_rows[k : k + 1, :] for k in range(6)], axis=1)
    zed_mean = sums[0:24] / counts
    means = zed_mean * gain
    inverse = lax.rsqrt(jnp.sum(means * means, axis=1, keepdims=True) + EPSILON)
    unit = means * inverse

    live_own = column_of(label_ref[...].astype(F32))
    wide_lane = lax.broadcasted_iota(jnp.int32, (8, D), 1)
    marked = jnp.where(
        live_own > 0.5, unit[0:8], jnp.where(wide_lane == 0, UNLABELLED, 0.0)
    )
    own_cands = unit[8:24].astype(BF16)
    gather[me, :, 0:D] = own_cands
    gather[me, :, D:PACK] = jnp.concatenate([marked[:, :HALF], marked[:, HALF:]], axis=0).astype(
        BF16
    )
    own_anchors = jnp.concatenate([marked, jnp.zeros_like(marked)], axis=0).astype(BF16)

    pl.semaphore_wait(barrier, spots + lines - 2)
    sends = []

    def send_block(block, device, arrival=None):
        pltpu.make_async_remote_copy(
            src_ref=gather.at[block],
            dst_ref=gather.at[block],
            send_sem=gather_send,
            recv_sem=gather_recv.at[block // 2] if arrival is None else arrival,
            device_id=device,
            device_id_type=MESH,
        ).start()
        sends.append(block)

    def await_block(block):
        part = gather.at[block]
        pltpu.make_async_copy(part, part, gather_recv.at[block // 2]).wait()

    def bytes_of(buffers, blocks, sem):
        part = buffers.at[pl.ds(0, blocks)]
        return pltpu.make_async_copy(part, part, sem)

    line_order = [line] + [other_line(k) for k in range(lines - 1)]
    for k in far_lines:
        send_block(me, line_device(k)[1])
    for k in range(lines):
        block = (line_order[k] * 2 + side) * n_narrow + narrow
        if k:
            await_block(block)
        for d in cells:
            send_block(block, spot_device(d)[1])
        send_block(block, sibling, sibling_recv)

    error_copy.wait()
    factor_parts = stacked_parts(factor_ref[...])
    error_rows = error[...]
    error_high = error_rows.astype(BF16)
    error_low = (error_rows - error_high.astype(F32)).astype(BF16)
    row_part = folded(nt(factor_parts, error_high) + nt(factor_parts, error_low), RANK)

    def flat_bias(x):
        high, middle, low = parts_of(x)
        spread = folded(
            nn(
                jnp.concatenate([high, gap, middle, gap, low, gap], axis=0).astype(BF16),
                spread_ref[...],
            ),
            16,
        )
        return jnp.sum(spread * head_mask_ref[...], axis=0, keepdims=True)

    def packed(gain_part, bias_part, scale_part):
        return jnp.concatenate(
            [gain_part]
            + [bias_part[:, k * LEN : (k + 1) * LEN] for k in range(3)]
            + [jnp.where(lane == 0, scale_part, 0.0), jnp.zeros((6, LEN), F32)],
            axis=0,
        )

    small_ref[16:32, LEN : 2 * LEN] = packed(gain_rows, flat_bias(bias_ref[...]), scale_ref[...])
    small_ref[16:32, 2 * LEN : 3 * LEN] = packed(gain_mom_ref[...], flat_bias(bias_mom_ref[...]), scale_mom_ref[...])

    for k in range(lines):
        for d in cells[::-1]:
            _, (other_wide, other_narrow) = spot_device(d)
            block = (line_order[k] * 2 + other_wide % 2) * n_narrow + other_narrow
            await_block(block)
            send_block(block, sibling, sibling_recv)
    bytes_of(gather, count // 2, sibling_recv).wait()

    blocks = count // GROUP
    temper = jnp.exp(scale_ref[...])

    def unpack(b, total):
        picked = gather[pl.ds(b * GROUP, GROUP), :, D:PACK].astype(F32)
        left = picked[:, 0:8, :].reshape(GROUP * 8, HALF)
        right = picked[:, 8:16, :].reshape(GROUP * 8, HALF)
        anchors_all[b] = jnp.concatenate([left, right], axis=1).astype(BF16)
        live = jnp.where(left[:, 0:1] < 1.5, 1.0, 0.0)
        return total + jnp.sum(live, axis=0, keepdims=True)

    live_total = looped(blocks, unpack, jnp.zeros((1, 1), F32))

    def cands_of(b):
        return gather[pl.ds(b * GROUP, GROUP), :, 0:D].reshape(GROUP * 16, D)

    first_lane = jnp.where(lax.broadcasted_iota(jnp.int32, (16, D), 1) == 0, 1.0, 0.0).astype(BF16)
    row16 = lax.broadcasted_iota(jnp.int32, (16, GROUP * 8), 0)
    lane16 = lax.broadcasted_iota(jnp.int32, (16, GROUP * 8), 1)
    per_live = 1.0 / live_total

    def columns(b, cand_grad):
        anchors = anchors_all[b]

        def part(c, state):
            top, total = state
            logits = temper * nt(cands_of(c), anchors)
            new_top = jnp.maximum(top, jnp.max(logits, axis=0, keepdims=True))
            total = total * jnp.exp(top - new_top) + jnp.sum(
                jnp.exp(logits - new_top), axis=0, keepdims=True
            )
            return new_top, total

        start = (jnp.full((1, GROUP * 8), -1e30, F32), jnp.zeros((1, GROUP * 8), F32))
        top, total = looped(blocks, part, start)
        log_total = top + jnp.log(total)
        live = jnp.where(nt(first_lane, anchors) < 1.5, per_live, 0.0)
        logits = temper * nt(own_cands, anchors)
        target = jnp.where(
            (row16 < 8) & (lane16 + b * (GROUP * 8) == row16 + me * ROWS_DEV), 1.0, 0.0
        )
        grad = (jnp.exp(logits - log_total) - target) * live
        return cand_grad + nn((temper * grad).astype(BF16), anchors)

    cand_grad = looped(blocks, columns, jnp.zeros((16, D), F32))

    def own_part(b, state):
        top, total = state
        logits = temper * nt(own_anchors, cands_of(b))
        own_scores[b] = logits
        new_top = jnp.maximum(top, jnp.max(logits, axis=1, keepdims=True))
        total = total * jnp.exp(top - new_top) + jnp.sum(
            jnp.exp(logits - new_top), axis=1, keepdims=True
        )
        return new_top, total

    start = (jnp.full((16, 1), -1e30, F32), jnp.zeros((16, 1), F32))
    top, total = looped(blocks, own_part, start)
    log_total = top + jnp.log(total)
    live16 = jnp.concatenate([live_own, jnp.zeros_like(live_own)], axis=0)
    row32 = lax.broadcasted_iota(jnp.int32, (16, GROUP * 16), 0)
    lane32 = lax.broadcasted_iota(jnp.int32, (16, GROUP * 16), 1)

    def own_grad(b, state):
        anchor_grad, positive, scale_grad = state
        logits = own_scores[b]
        target = jnp.where(
            (row32 < 8) & (lane32 + b * (GROUP * 16) == row32 + me * 2 * ROWS_DEV), 1.0, 0.0
        )
        positive = positive + jnp.sum(logits * target, axis=1, keepdims=True)
        grad = (jnp.exp(logits - log_total) - target) * (live16 * per_live)
        scale_grad = scale_grad + jnp.sum(grad * logits, axis=1, keepdims=True)
        anchor_grad = anchor_grad + nn((temper * grad).astype(BF16), cands_of(b))
        return anchor_grad, positive, scale_grad

    column = jnp.zeros((16, 1), F32)
    anchor_grad, positive, scale_grad = looped(
        blocks, own_grad, (jnp.zeros((16, D), F32), column, column)
    )
    loss_own = jnp.sum(live16 * (log_total - positive), axis=0, keepdims=True)
    scale_grad = jnp.sum(scale_grad, axis=0, keepdims=True)

    branch, mixed_grad = resid, zed_low
    unit_grad = jnp.concatenate([anchor_grad[0:8], cand_grad], axis=0)
    mean_grad = inverse * (unit_grad - unit * jnp.sum(unit * unit_grad, axis=1, keepdims=True))
    gain_grad = jnp.sum(mean_grad * zed_mean, axis=0, keepdims=True)
    high, middle, low = parts_of(mean_grad / counts * gain)
    wide_gap = jnp.zeros((8, D), F32)
    shares = jnp.concatenate(
        [high, wide_gap, middle, wide_gap, low, wide_gap, jnp.zeros((32, D), F32)], axis=0
    ).astype(BF16)
    wide_rows[...] = nn(member_t[...], shares)
    for b in range(TOK // 32):
        rows = slice(b * 32, (b + 1) * 32)
        zed_grad = wide_rows[rows, :]
        zed_rows = zed[rows, :]
        level = jnp.sum(zed_grad * zed_rows, axis=1, keepdims=True) * (1.0 / D)
        branch[rows, :] = (rms_inv[rows, :] * (zed_grad - zed_rows * level)).astype(BF16)
    by_token = folded(nt(factor_parts, branch[...]), RANK)
    row_part = row_part + folded(nt(stacked_parts(by_token), mixed_t[...]), RANK)

    def exchange(buffers, mine, devices, send_sem, recv_sem):
        for device in devices:
            pltpu.make_async_remote_copy(
                src_ref=buffers.at[mine],
                dst_ref=buffers.at[mine],
                send_sem=send_sem,
                recv_sem=recv_sem,
                device_id=device,
                device_id_type=MESH,
            ).start()

    def start_sum(which, plane):
        devices = [spot_device(d)[1] for d in offsets]
        exchange(plane, spot, devices, plane_send.at[which], plane_recv.at[which])

    def middle_sum(which, plane, along):
        bytes_of(plane, spots - 1, plane_recv.at[which]).wait()
        total = plane[0]
        for k in range(1, spots):
            total = total + plane[k]
        along[line] = total
        devices = [line_device(k)[1] for k in far_lines]
        exchange(along, line, devices, line_send.at[which], line_recv.at[which])

    def finish_sum(which, along):
        bytes_of(along, lines - 1, line_recv.at[which]).wait()
        total = along[0]
        for k in range(1, lines):
            total = total + along[k]
        return total

    scalars = jnp.where(lane == 0, loss_own, jnp.where(lane == 1, scale_grad, 0.0))
    extra = jnp.concatenate(
        [gain_grad[:, k * LEN : (k + 1) * LEN] for k in range(6)]
        + [scalars, jnp.zeros((1, LEN), F32)],
        axis=0,
    )
    plane1[spot, :, 0:D] = row_part
    plane1[spot, :, D:WIDTH] = extra
    start_sum(0, plane1)

    for b in range(3):
        rows = slice(b * 256, (b + 1) * 256)
        full = error[rows, :] + nn(mixed_t[rows, :], branch[...])
        matrix[rows, :] = full
        high = full.astype(BF16)
        matrix_high[rows, :] = high
        rest = full - high.astype(F32)
        low = rest.astype(BF16)
        matrix_low[rows, :] = low
        matrix_rest[rows, :] = (rest - low.astype(F32)).astype(BF16)
    matrix_copy = pltpu.make_async_copy(matrix, matrix_hbm, out_sem)
    matrix_copy.start()

    for c in range(4):
        rows = slice(c * 256, (c + 1) * 256)
        mixed_grad[rows, :] = nt(branch[rows, :], weight_low[...]).astype(BF16)
    middle_sum(0, plane1, line1)
    for p in range(PAIRS):
        cols = slice(p * LEN, (p + 1) * LEN)

        def back(r, acc):
            offset = pl.multiple_of(r * LEN, LEN)
            rows = pl.ds(offset, LEN)
            grad = mixed_grad[rows, cols]
            right = jnp.concatenate([grad * first, grad * second], axis=0)
            prob_grad = nt(proj[2, rows, cols], right)
            prob = jnp.concatenate(
                [probs[r * HEADS + 2 * p], probs[r * HEADS + 2 * p + 1]], axis=1
            )
            product = prob * prob_grad
            return acc + (product - prob * jnp.sum(product, axis=0, keepdims=True))

        acc = lax.fori_loop(0, ROWS_DEV, back, jnp.zeros((LEN, 2 * LEN), F32), unroll=True)
        for half in range(2):
            padded = jnp.concatenate(
                [acc[:, half * LEN : (half + 1) * LEN], jnp.zeros((LEN, LEN), F32)], axis=1
            )
            sheared = padded[0:8]
            for a in range(1, LEN // 8):
                sheared = sheared + pltpu.roll(padded[8 * a : 8 * a + 8], 2 * LEN - 8 * a, 1)
            for bit in (1, 2, 4):
                moved = pltpu.roll(sheared, 2 * LEN - bit, 1)
                sheared = jnp.where((row8 & bit) != 0, moved, sheared)
            head = 2 * p + half
            diagonals[head : head + 1, :] = jnp.sum(sheared, axis=0, keepdims=True)
    diagonals[HEADS:16, :] = jnp.zeros((16 - HEADS, 2 * LEN), F32)
    high, middle, low = parts_of(diagonals[...])
    by_bucket = folded(
        nn(jnp.concatenate([high, middle, low], axis=0).astype(BF16), onehot_ref[...]), 16
    )
    bias_grad = jnp.sum(by_bucket * head_mask_ref[...], axis=0, keepdims=True)

    total = finish_sum(0, line1)
    small_ref[16:24, 0:LEN] = total[:, D:WIDTH]
    ortho = total[:, 0:D]
    row_parts = stacked_parts(ortho)
    product = folded(
        nn(row_parts, matrix_high[...])
        + nn(row_parts, matrix_low[...])
        + nn(row_parts, matrix_rest[...]),
        RANK,
    )
    rank_row = lax.broadcasted_iota(jnp.int32, (RANK, 1), 0)
    weights = []
    for k in range(RANK):
        vector = ortho[k : k + 1, :]
        dots = jnp.sum(ortho * vector, axis=1, keepdims=True)
        norm = lax.rsqrt(dots[k : k + 1, :] + EPSILON)
        vector = vector * norm
        weight_k = jnp.where(rank_row > k, dots * norm, 0.0)
        ortho = jnp.where(rank_row == k, vector, ortho - weight_k * vector)
        weights.append((norm, weight_k))
    for k, (norm, weight_k) in enumerate(weights):
        vector = product[k : k + 1, :] * norm
        product = jnp.where(rank_row == k, vector, product - weight_k * vector)
    small_ref[0:8, :] = ortho
    plane2[spot, :, 0:D] = product
    plane2[spot, :, D:WIDTH] = jnp.concatenate(
        [bias_grad[:, k * LEN : (k + 1) * LEN] for k in range(3)] + [jnp.zeros((5, LEN), F32)],
        axis=0,
    )
    start_sum(1, plane2)
    bytes_of(gather, len(sends), gather_send).wait()
    bytes_of(plane1, spots - 1, plane_send.at[0]).wait()
    bytes_of(line1, lines - 1, line_send.at[0]).wait()
    matrix_copy.wait()
    for copy in keep_copies:
        copy.wait()
    middle_sum(1, plane2, line2)
    total = finish_sum(1, line2)
    small_ref[8:16, :] = total[:, 0:D]
    small_ref[24:32, 0:LEN] = total[:, D:WIDTH]
    small_ref[16:32, 3 * LEN : 4 * LEN] = jnp.broadcast_to(live_total, (16, LEN))
    small_ref[16:32, 4 * LEN : D] = jnp.zeros((16, D - 4 * LEN), F32)
    bytes_of(plane2, spots - 1, plane_send.at[1]).wait()
    bytes_of(line2, lines - 1, line_send.at[1]).wait()


def update_kernel(
    count,
    small_ref,
    matrix_ref,
    weight_ref,
    momentum_ref,
    weight_out,
    momentum_out,
    error_out,
    vector_out,
    vector_mom_out,
    loss_out,
    norm_out,
    fnew_out,
    live_out,
    matrix,
    weight,
    momentum,
    store_sem,
):
    ortho = small_ref[0:8, :]
    fnew = small_ref[8:16, :]
    oh, om, ol = parts_of(ortho)
    fh, fm, fl = parts_of(fnew)
    pad = jnp.zeros((16, D), F32)
    left = jnp.concatenate([oh, oh, om, om, oh, ol, pad], axis=0).astype(BF16)
    right = jnp.concatenate([fh, fm, fh, fm, fl, fh, pad], axis=0).astype(BF16)
    copies = []

    def send_out(source, target, rows, sem):
        copy = pltpu.make_async_copy(source.at[rows, :], target.at[rows, :], sem)
        copy.start()
        copies.append(copy)

    for b in range(6):
        rows = slice(b * LEN, (b + 1) * LEN)
        approx = tn(left[:, rows], right)
        weight[rows, :] = approx
        matrix[rows, :] = matrix_ref[rows, :] - approx * (1.0 / count)
        send_out(matrix, error_out.at[0], rows, store_sem.at[b, 2])

    square = jnp.zeros((RANK, 1), F32)
    for k in range(RANK):
        left = jnp.sum(ortho * ortho[k : k + 1, :], axis=1, keepdims=True)
        right = jnp.sum(fnew * fnew[k : k + 1, :], axis=1, keepdims=True)
        square = square + left * right
    square = jnp.sum(square, axis=0, keepdims=True)
    vec = small_ref[16:32, 0:LEN]
    lane = lax.broadcasted_iota(jnp.int32, (1, LEN), 1)
    scale_row = jnp.where(lane == 0, vec[6:7, 1:2], 0.0)
    grad = jnp.concatenate(
        [vec[0:6], vec[8:11], scale_row, jnp.zeros((6, LEN), F32)], axis=0
    )
    square = square + jnp.sum(
        jnp.sum(grad * grad, axis=1, keepdims=True), axis=0, keepdims=True
    )
    norm = jnp.sqrt(square)
    clip = CLIP_NORM / jnp.maximum(norm, CLIP_NORM)

    for b in range(6):
        rows = slice(b * LEN, (b + 1) * LEN)
        mom = MOMENTUM_DECAY * momentum_ref[rows, :] + clip * weight[rows, :]
        momentum[rows, :] = mom
        send_out(momentum, momentum_out, rows, store_sem.at[b, 0])
        weight[rows, :] = weight_ref[rows, :] - RATE_MATRIX * mom
        send_out(weight, weight_out, rows, store_sem.at[b, 1])

    row = lax.broadcasted_iota(jnp.int32, (16, 1), 0)
    rate = jnp.where(row < 6, RATE_GAIN, jnp.where(row < 9, RATE_BIAS, RATE_SCALE))
    mom = MOMENTUM_DECAY * small_ref[16:32, 2 * LEN : 3 * LEN] + clip * grad
    vector_mom_out[...] = mom
    vector_out[...] = small_ref[16:32, LEN : 2 * LEN] - rate * mom
    loss_out[...] = vec[6:7, 0:1]
    norm_out[...] = norm
    fnew_out[...] = fnew
    live_out[...] = small_ref[16:17, 3 * LEN : 3 * LEN + 1]
    for copy in copies:
        copy.wait()


def local(
    n_wide,
    n_narrow,
    projected,
    layer_input,
    segment_ids,
    pad_mask,
    roles,
    labelled,
    out_weight,
    out_momentum,
    errors,
    factors,
    norm_gain,
    position_bias,
    log_scale,
    gain_momentum,
    bias_momentum,
    scale_momentum,
):
    count = n_wide * n_narrow
    lines = n_wide // 2
    spots = 2 * n_narrow
    blocks = count // GROUP
    anywhere = pl.BlockSpec(memory_space=pl.ANY)
    vmem = pl.BlockSpec(memory_space=pltpu.VMEM)

    def stay(x):
        return pltpu.with_memory_space_constraint(x, pltpu.HBM)

    in_hbm = pl.BlockSpec(memory_space=pltpu.HBM)
    kept = pl.pallas_call(
        functools.partial(step_kernel, n_wide, n_narrow),
        out_shape=(
            jax.ShapeDtypeStruct((32, D), F32),
            jax.ShapeDtypeStruct((D, D), F32),
            jax.ShapeDtypeStruct((D, D), F32),
            jax.ShapeDtypeStruct((D, D), F32),
        ),
        in_specs=[in_hbm] * 20,
        out_specs=(vmem, anywhere, anywhere, anywhere),
        scratch_shapes=[
            pltpu.VMEM((ROWS_DEV, LEN), jnp.int32),
            pltpu.VMEM((ROWS_DEV, LEN), jnp.int32),
            pltpu.VMEM((3, ROWS_DEV), jnp.int32),
            pltpu.VMEM((1, ROWS_DEV), jnp.int32),
            pltpu.VMEM((RANK, D), F32),
            pltpu.VMEM((6, LEN), F32),
            pltpu.VMEM((6, LEN), F32),
            pltpu.VMEM((HEADS, BUCKETS), F32),
            pltpu.VMEM((HEADS, BUCKETS), F32),
            pltpu.VMEM((1, 1), F32),
            pltpu.VMEM((1, 1), F32),
            pltpu.VMEM((2 * LEN, FLAT), BF16),
            pltpu.VMEM((BUCKETS, FLAT), BF16),
            pltpu.VMEM((2 * LEN, BUCKETS), BF16),
            pltpu.VMEM((16, FLAT), F32),
            pltpu.SemaphoreType.DMA((15,)),
            pltpu.VMEM((3, TOK, D), BF16),
            pltpu.VMEM((TOK, D), BF16),
            pltpu.VMEM((D, D), F32),
            pltpu.VMEM((D, D), F32),
            pltpu.VMEM((D, D), BF16),
            pltpu.VMEM((HEADS, LEN, LEN), F32),
            pltpu.VMEM((ROWS_DEV, LEN, LEN), BF16),
            pltpu.VMEM((ROWS_DEV, LEN, LEN), BF16),
            pltpu.VMEM((32, TOK), BF16),
            pltpu.VMEM((TOK, LEN), BF16),
            pltpu.VMEM((ROWS_DEV * HEADS, LEN, LEN), F32),
            pltpu.VMEM((PAIRS, LEN, 2 * LEN), F32),
            pltpu.VMEM((PAIRS, LEN, 2 * LEN), F32),
            pltpu.VMEM((PAIRS, 2 * LEN, LEN), BF16),
            pltpu.VMEM((PAIRS, 2 * LEN, LEN), BF16),
            pltpu.VMEM((D, TOK), BF16),
            pltpu.VMEM((TOK, D), F32),
            pltpu.VMEM((TOK, D), F32),
            pltpu.VMEM((TOK, D), BF16),
            pltpu.VMEM((TOK, D), BF16),
            pltpu.VMEM((TOK, 1), F32),
            pltpu.VMEM((TOK, 1), F32),
            pltpu.VMEM((D, D), F32),
            pltpu.VMEM((D, D), BF16),
            pltpu.VMEM((D, D), BF16),
            pltpu.VMEM((D, D), BF16),
            pltpu.VMEM((count, 16, PACK), BF16),
            pltpu.VMEM((blocks, GROUP * 8, D), BF16),
            pltpu.VMEM((blocks, 16, GROUP * 16), F32),
            pltpu.VMEM((16, 2 * LEN), F32),
            pltpu.VMEM((spots, RANK, WIDTH), F32),
            pltpu.VMEM((lines, RANK, WIDTH), F32),
            pltpu.VMEM((spots, RANK, WIDTH), F32),
            pltpu.VMEM((lines, RANK, WIDTH), F32),
            pltpu.SemaphoreType.DMA((2,)),
            pltpu.SemaphoreType.DMA,
            pltpu.SemaphoreType.DMA((4,)),
            pltpu.SemaphoreType.DMA,
            pltpu.SemaphoreType.DMA,
            pltpu.SemaphoreType.DMA((count // 2,)),
            pltpu.SemaphoreType.DMA,
            pltpu.SemaphoreType.DMA((2,)),
            pltpu.SemaphoreType.DMA((2,)),
            pltpu.SemaphoreType.DMA((2,)),
            pltpu.SemaphoreType.DMA((2,)),
        ],
        compiler_params=pltpu.CompilerParams(
            collective_id=0, has_side_effects=True, vmem_limit_bytes=(45 if blocks == 1 else 60) * 2**20
        ),
        name="step",
    )(
        stay(projected),
        stay(layer_input),
        stay(out_weight),
        stay(errors),
        stay(out_momentum),
        stay(segment_ids.reshape(ROWS_DEV, LEN)),
        stay(pad_mask.reshape(ROWS_DEV, LEN)),
        stay(roles.T),
        stay(labelled.reshape(1, ROWS_DEV)),
        stay(factors),
        stay(norm_gain.reshape(6, LEN)),
        stay(gain_momentum.reshape(6, LEN)),
        stay(position_bias.T),
        stay(bias_momentum.T),
        log_scale.reshape(1, 1),
        scale_momentum.reshape(1, 1),
        stay(jnp.asarray(diagonal_onehot(FLAT), BF16)),
        stay(jnp.asarray(bucket_spread(), BF16)),
        stay(jnp.asarray(diagonal_onehot(BUCKETS), BF16)),
        stay(jnp.asarray(head_mask())),
    )
    outs = pl.pallas_call(
        functools.partial(update_kernel, count),
        out_shape=(
            jax.ShapeDtypeStruct((D, D), F32),
            jax.ShapeDtypeStruct((D, D), F32),
            jax.ShapeDtypeStruct((1, D, D), F32),
            jax.ShapeDtypeStruct((16, LEN), F32),
            jax.ShapeDtypeStruct((16, LEN), F32),
            jax.ShapeDtypeStruct((1, 1), F32),
            jax.ShapeDtypeStruct((1, 1), F32),
            jax.ShapeDtypeStruct((RANK, D), F32),
            jax.ShapeDtypeStruct((1, 1), F32),
        ),
        in_specs=[vmem] * 4,
        out_specs=(anywhere,) * 3 + (vmem,) * 6,
        scratch_shapes=[
            pltpu.VMEM((D, D), F32),
            pltpu.VMEM((D, D), F32),
            pltpu.VMEM((D, D), F32),
            pltpu.SemaphoreType.DMA((6, 3)),
        ],
        compiler_params=pltpu.CompilerParams(vmem_limit_bytes=24 * 2**20),
        name="update",
    )(*kept)
    weight_new, weight_mom, errors_new, vec_new, vec_mom, loss, norm, fnew, live_total = outs
    size = D + FLAT + 1
    return (
        weight_new,
        weight_mom,
        errors_new,
        fnew,
        vec_new.reshape(-1)[:size],
        vec_mom.reshape(-1)[:size],
        loss.reshape(1),
        live_total.reshape(1),
        norm.reshape(1),
    )


def solution(mesh):
    both = ("wide", "narrow")
    in_specs = (
        P(None, both, None),
        P(both, None),
        P(both),
        P(both),
        P(both, None),
        P(both),
        P(),
        P(),
        P(both, None, None),
        P(),
        P(),
        P(),
        P(),
        P(),
        P(),
        P(),
    )
    out_specs = (P(), P(), P(both, None, None), P(), P(), P(), P(), P(), P())
    return jax.shard_map(
        functools.partial(local, mesh.shape["wide"], mesh.shape["narrow"]),
        mesh=mesh,
        in_specs=in_specs,
        out_specs=out_specs,
        check_vma=False,
    )
```

```python
import functools

import jax
import jax.numpy as jnp
import numpy as np
from jax import lax
from jax.experimental import pallas as pl
from jax.experimental.pallas import tpu as pltpu
from jax.sharding import PartitionSpec as P

D = 768
HEADS = 12
HEAD_DIM = 64
BUCKETS = 32
LEN = 128
ROWS_DEV = 8
RANK = 8
TOK = ROWS_DEV * LEN
PAIRS = HEADS // 2
HALF = D // 2
FLAT = BUCKETS * HEADS
PACK = D + HALF
GROUP = 32
WIDTH = D + 128

EPSILON = 1e-06
MOMENTUM_DECAY = 0.9
CLIP_NORM = 0.01
RATE_MATRIX = 50000.0
RATE_GAIN = 4000.0
RATE_BIAS = 2000.0
RATE_SCALE = 10.0
MASKED = -float(2**30)
UNLABELLED = 2.0
F32 = jnp.float32
BF16 = jnp.bfloat16
MESH = pl.DeviceIdType.MESH


def diagonal_buckets():
    half_count = BUCKETS // 2
    exact_count = half_count // 2
    table = np.full((2 * LEN,), -1, np.int64)
    for k in range(2 * LEN):
        if k == LEN:
            continue
        relative = -k if k < LEN else 2 * LEN - k
        distance = abs(relative)
        larger = exact_count + int(
            np.log(np.maximum(distance, 1) / exact_count)
            / np.log(128.0 / exact_count)
            * (half_count - exact_count)
        )
        larger = min(larger, half_count - 1)
        table[k] = (half_count if relative > 0 else 0) + (
            distance if distance < exact_count else larger
        )
    return table


def diagonal_onehot(width):
    spread = np.arange(width) // (width // BUCKETS)
    return (diagonal_buckets()[:, None] == spread[None, :]).astype(np.float32)


def bucket_spread():
    return (np.arange(BUCKETS)[:, None] == (np.arange(FLAT) // HEADS)[None, :]).astype(np.float32)


def head_mask():
    return (np.arange(16)[:, None] == (np.arange(FLAT) % HEADS)[None, :]).astype(np.float32)


def nn(left, right):
    return lax.dot_general(
        left, right, (((1,), (0,)), ((), ())), preferred_element_type=F32
    )


def nt(left, right):
    return lax.dot_general(
        left, right, (((1,), (1,)), ((), ())), preferred_element_type=F32
    )


def tn(left, right):
    return lax.dot_general(
        left, right, (((0,), (0,)), ((), ())), preferred_element_type=F32
    )


def parts_of(x):
    high = x.astype(BF16).astype(F32)
    rest = x - high
    middle = rest.astype(BF16).astype(F32)
    return high, middle, rest - middle


def stacked_parts(x):
    high, middle, low = parts_of(x)
    return jnp.concatenate([high, middle, low, jnp.zeros_like(x)], axis=0).astype(BF16)


def folded(y, rows):
    return y[0:rows] + y[rows : 2 * rows] + y[2 * rows : 3 * rows]


def looped(count, body, carry):
    if count == 1:
        return body(0, carry)
    return lax.fori_loop(0, count, body, carry)


def step_kernel(
    n_wide,
    n_narrow,
    proj_hbm,
    resid_hbm,
    weight_hbm,
    error_hbm,
    momentum_hbm,
    seg_hbm,
    pad_hbm,
    roles_hbm,
    label_hbm,
    factor_hbm,
    gain_hbm,
    gain_mom_hbm,
    bias_hbm,
    bias_mom_hbm,
    scale_hbm,
    scale_mom_hbm,
    onehot_hbm,
    spread_hbm,
    diagonal_hbm,
    head_mask_hbm,
    small_ref,
    matrix_hbm,
    weight_keep,
    momentum_keep,
    seg_ref,
    pad_ref,
    roles_ref,
    label_ref,
    factor_ref,
    gain_ref,
    gain_mom_ref,
    bias_ref,
    bias_mom_ref,
    scale_ref,
    scale_mom_ref,
    onehot_ref,
    spread_ref,
    diagonal_ref,
    head_mask_ref,
    small_sem,
    proj,
    resid,
    weight,
    error,
    weight_low,
    bias_table,
    key_extra,
    query_extra,
    member,
    member_t,
    probs,
    score_even,
    score_odd,
    prob_even,
    prob_odd,
    mixed_t,
    wide_rows,
    zed,
    zed_high,
    zed_low,
    rms_inv,
    levels,
    matrix,
    matrix_high,
    matrix_low,
    matrix_rest,
    gather,
    anchors_all,
    own_scores,
    diagonals,
    plane1,
    line1,
    plane2,
    line2,
    row_sem,
    resid_sem,
    load_sem,
    out_sem,
    gather_send,
    gather_recv,
    sibling_recv,
    plane_send,
    plane_recv,
    line_send,
    line_recv,
):
    count = n_wide * n_narrow
    lines = n_wide // 2
    spots = 2 * n_narrow
    wide = lax.axis_index("wide")
    narrow = lax.axis_index("narrow")
    me = wide * n_narrow + narrow
    line = wide // 2
    side = wide % 2
    spot = side * n_narrow + narrow

    y_size = n_narrow // 2
    row_at, core = narrow // 2, narrow % 2
    offsets = sorted(
        (
            (dx, dy, dc)
            for dx in range(2)
            for dy in range(y_size)
            for dc in range(2)
            if dx or dy or dc
        ),
        key=lambda d: (-(d[0] > 0) - (d[1] > 0), -d[2]),
    )
    far_lines = sorted(range(1, lines), key=lambda k: -min(k, lines - k))

    def spot_device(d):
        dx, dy, dc = d
        other_side = (side + dx) % 2
        other_narrow = (row_at + dy) % y_size * 2 + (core + dc) % 2
        return other_side * n_narrow + other_narrow, (line * 2 + other_side, other_narrow)

    def line_device(k):
        other = (line + k) % lines
        return other, (other * 2 + side, narrow)

    def other_line(k):
        return k + (k - line + lines) // lines

    cells = sorted((d for d in offsets if not d[2]), key=lambda d: (-(d[0] > 0) - (d[1] > 0), d[0]))

    sibling = (wide, narrow + 1 - 2 * (narrow % 2))

    def load(source, target, sem):
        copy = pltpu.make_async_copy(source, target, sem)
        copy.start()
        return copy

    mask_loads = [load(seg_hbm, seg_ref, small_sem.at[0]), load(pad_hbm, pad_ref, small_sem.at[1])]
    first_row = load(
        proj_hbm.at[:, pl.ds(0, LEN), :], proj.at[:, pl.ds(0, LEN), :], row_sem.at[0]
    )
    bias_loads = [
        load(bias_hbm, bias_ref, small_sem.at[2]),
        load(diagonal_hbm, diagonal_ref, small_sem.at[3]),
    ]
    later = pl.ds(LEN, TOK - LEN)
    later_rows = load(proj_hbm.at[:, later, :], proj.at[:, later, :], row_sem.at[1])
    rest_loads = [
        load(source, target, small_sem.at[4 + k])
        for k, (source, target) in enumerate(
            (
                (roles_hbm, roles_ref),
                (label_hbm, label_ref),
                (factor_hbm, factor_ref),
                (gain_hbm, gain_ref),
                (gain_mom_hbm, gain_mom_ref),
                (bias_mom_hbm, bias_mom_ref),
                (scale_hbm, scale_ref),
                (scale_mom_hbm, scale_mom_ref),
                (onehot_hbm, onehot_ref),
                (spread_hbm, spread_ref),
                (head_mask_hbm, head_mask_ref),
            )
        )
    ]
    barrier = pltpu.get_barrier_semaphore()
    for d in offsets:
        pl.semaphore_signal(barrier, inc=1, device_id=spot_device(d)[1], device_id_type=MESH)
    for k in far_lines:
        pl.semaphore_signal(barrier, inc=1, device_id=line_device(k)[1], device_id_type=MESH)

    for copy in mask_loads:
        copy.wait()
    code = jnp.where(pad_ref[...] == 1, seg_ref[...], 3).astype(F32)
    seg_f = seg_ref[...].astype(F32)
    fill = jnp.zeros((LEN - 16, LEN), F32)
    code_t = jnp.concatenate([code, seg_f, fill], axis=0).T
    lane = lax.broadcasted_iota(jnp.int32, (1, LEN), 1)
    sentence = lane.astype(F32)
    for r in range(ROWS_DEV):
        code_col = code_t[:, r : r + 1]
        seg_col = code_t[:, 8 + r : 9 + r]
        key_extra[r] = jnp.where(
            (sentence < 3.0) & (sentence != code_col), MASKED, 0.0
        ).astype(BF16)
        query_extra[r] = jnp.where(sentence == seg_col, 1.0, 0.0).astype(BF16)

    first = jnp.where(lane < HEAD_DIM, 1.0, 0.0).astype(BF16)
    second = jnp.where(lane < HEAD_DIM, 0.0, 1.0).astype(BF16)
    nothing = jnp.zeros((HEAD_DIM, LEN), BF16)

    score_rows = (score_even, score_odd)
    prob_rows = (prob_even, prob_odd)

    def rows_of(r):
        return slice(r * LEN, (r + 1) * LEN)

    def score(r, p):
        rows = rows_of(r)
        cols = slice(p * LEN, (p + 1) * LEN)
        query = proj[0, rows, cols]
        query_more = query_extra[r]
        left = jnp.concatenate([proj[1, rows, cols], key_extra[r]], axis=1)
        right = jnp.concatenate(
            [
                jnp.concatenate([query * first, query_more], axis=1),
                jnp.concatenate([query * second, query_more], axis=1),
            ],
            axis=0,
        )
        score_rows[r % 2][p] = nt(left, right)

    def soften(r, p):
        for half in range(2):
            head = 2 * p + half
            part = score_rows[r % 2][p, :, half * LEN : (half + 1) * LEN] + bias_table[head]
            part = jnp.exp(part - jnp.max(part, axis=0, keepdims=True))
            part = part * (1.0 / jnp.sum(part, axis=0, keepdims=True))
            probs[r * HEADS + head] = part
            prob_rows[r % 2][p, half * LEN : (half + 1) * LEN, :] = part.astype(BF16)

    def mix(r, p):
        rows = rows_of(r)
        cols = slice(p * LEN, (p + 1) * LEN)
        value_t = proj[2, rows, cols].T
        left = jnp.concatenate(
            [
                jnp.concatenate([value_t[:HEAD_DIM], nothing], axis=1),
                jnp.concatenate([nothing, value_t[HEAD_DIM:]], axis=1),
            ],
            axis=0,
        )
        mixed_t[cols, rows] = nn(left, prob_rows[r % 2][p]).astype(BF16)

    first_row.wait()
    for p in range(PAIRS):
        score(0, p)

    for copy in bias_loads:
        copy.wait()
    high, middle, low = parts_of(bias_ref[...])
    gap = jnp.zeros((4, BUCKETS), F32)
    diag_bias = folded(
        nt(
            jnp.concatenate([high, gap, middle, gap, low, gap], axis=0).astype(BF16),
            diagonal_ref[...],
        ),
        16,
    )
    row8 = lax.broadcasted_iota(jnp.int32, (8, 1), 0)
    for h in range(HEADS):
        sheared = jnp.broadcast_to(diag_bias[h : h + 1, :], (8, 2 * LEN))
        for bit in (1, 2, 4):
            sheared = jnp.where((row8 & bit) != 0, pltpu.roll(sheared, bit, 1), sheared)
        bias_table[h, 0:8, :] = sheared[:, :LEN]
        for a in range(1, LEN // 8):
            bias_table[h, 8 * a : 8 * a + 8, :] = pltpu.roll(sheared, 8 * a, 1)[:, :LEN]

    for copy in rest_loads:
        copy.wait()
    roles_f = roles_ref[...].astype(F32)
    slot = lane % 32
    row_of = lax.broadcasted_iota(jnp.int32, (32, 1), 0)
    same = lax.broadcasted_iota(jnp.int32, (8, 8), 0) == lax.broadcasted_iota(jnp.int32, (8, 8), 1)

    def column_of(row):
        return jnp.sum(jnp.where(same, row, 0.0), axis=1, keepdims=True)

    role_col = jnp.concatenate(
        [column_of(roles_f[k : k + 1, :]) for k in range(3)] + [jnp.full((8, 1), 9.0, F32)], axis=0
    )
    for r in range(ROWS_DEV):
        role_lane = jnp.where(
            slot < 8,
            roles_f[0:1, r : r + 1],
            jnp.where(slot < 16, roles_f[1:2, r : r + 1], roles_f[2:3, r : r + 1]),
        )
        role_lane = jnp.where((slot < 24) & (slot % 8 == r), role_lane, 9.0)
        member_t[r * LEN : (r + 1) * LEN, :] = jnp.where(
            role_lane == code_t[:, r : r + 1], 1.0, 0.0
        ).astype(BF16)
        member[:, r * LEN : (r + 1) * LEN] = jnp.where(
            (role_col == code[r : r + 1, :]) & (row_of % 8 == r), 1.0, 0.0
        ).astype(BF16)

    def project(c):
        rows = slice(c * 512, (c + 1) * 512)
        zed[rows, :] = resid[rows, :].astype(F32) + tn(mixed_t[:, rows], weight_low[...])

    def normalise():
        for b in range(TOK // 32):
            rows = slice(b * 32, (b + 1) * 32)
            hidden = zed[rows, :]
            inv = lax.rsqrt(jnp.sum(hidden * hidden, axis=1, keepdims=True) * (1.0 / D) + EPSILON)
            hidden = hidden * inv
            zed[rows, :] = hidden
            rms_inv[rows, :] = inv
            high = hidden.astype(BF16)
            zed_high[rows, :] = high
            zed_low[rows, :] = (hidden - high.astype(F32)).astype(BF16)
        return nn(member[...], zed_high[...]) + nn(member[...], zed_low[...])

    later_rows.wait()
    weight_copy = load(weight_hbm, weight, load_sem.at[0])
    resid_copy = load(resid_hbm, resid, resid_sem)
    for step in range(1, ROWS_DEV + 2):
        for p in range(PAIRS):
            if step < ROWS_DEV:
                score(step, p)
            if step > 1:
                mix(step - 2, p)
            if step <= ROWS_DEV:
                soften(step - 1, p)
    weight_copy.wait()
    resid_copy.wait()
    weight_low[...] = weight[...].astype(BF16)
    for c in range(2):
        project(c)
    sums = normalise()
    error_copy = load(error_hbm.at[0], error, load_sem.at[1])
    keep_copies = [
        load(momentum_hbm, momentum_keep, load_sem.at[2]),
        load(weight, weight_keep, load_sem.at[3]),
    ]
    counts = jnp.sum(member[...].astype(F32), axis=1, keepdims=True)[0:24]
    gain_rows = gain_ref[...]
    gain = jnp.concatenate([gain_rows[k : k + 1, :] for k in range(6)], axis=1)
    zed_mean = sums[0:24] / counts
    means = zed_mean * gain
    inverse = lax.rsqrt(jnp.sum(means * means, axis=1, keepdims=True) + EPSILON)
    unit = means * inverse

    live_own = column_of(label_ref[...].astype(F32))
    wide_lane = lax.broadcasted_iota(jnp.int32, (8, D), 1)
    marked = jnp.where(
        live_own > 0.5, unit[0:8], jnp.where(wide_lane == 0, UNLABELLED, 0.0)
    )
    own_cands = unit[8:24].astype(BF16)
    gather[me, :, 0:D] = own_cands
    gather[me, :, D:PACK] = jnp.concatenate([marked[:, :HALF], marked[:, HALF:]], axis=0).astype(
        BF16
    )
    own_anchors = jnp.concatenate([marked, jnp.zeros_like(marked)], axis=0).astype(BF16)

    pl.semaphore_wait(barrier, spots + lines - 2)
    sends = []

    def send_block(block, device, arrival=None):
        pltpu.make_async_remote_copy(
            src_ref=gather.at[block],
            dst_ref=gather.at[block],
            send_sem=gather_send,
            recv_sem=gather_recv.at[block // 2] if arrival is None else arrival,
            device_id=device,
            device_id_type=MESH,
        ).start()
        sends.append(block)

    def await_block(block):
        part = gather.at[block]
        pltpu.make_async_copy(part, part, gather_recv.at[block // 2]).wait()

    def bytes_of(buffers, blocks, sem):
        part = buffers.at[pl.ds(0, blocks)]
        return pltpu.make_async_copy(part, part, sem)

    line_order = [line] + [other_line(k) for k in range(lines - 1)]
    for k in far_lines:
        send_block(me, line_device(k)[1])
    for k in range(lines):
        block = (line_order[k] * 2 + side) * n_narrow + narrow
        if k:
            await_block(block)
        for d in cells:
            send_block(block, spot_device(d)[1])
        send_block(block, sibling, sibling_recv)

    error_copy.wait()
    factor_parts = stacked_parts(factor_ref[...])
    error_rows = error[...]
    error_high = error_rows.astype(BF16)
    error_low = (error_rows - error_high.astype(F32)).astype(BF16)
    row_part = folded(nt(factor_parts, error_high) + nt(factor_parts, error_low), RANK)

    def flat_bias(x):
        high, middle, low = parts_of(x)
        spread = folded(
            nn(
                jnp.concatenate([high, gap, middle, gap, low, gap], axis=0).astype(BF16),
                spread_ref[...],
            ),
            16,
        )
        return jnp.sum(spread * head_mask_ref[...], axis=0, keepdims=True)

    def packed(gain_part, bias_part, scale_part):
        return jnp.concatenate(
            [gain_part]
            + [bias_part[:, k * LEN : (k + 1) * LEN] for k in range(3)]
            + [jnp.where(lane == 0, scale_part, 0.0), jnp.zeros((6, LEN), F32)],
            axis=0,
        )

    small_ref[16:32, LEN : 2 * LEN] = packed(gain_rows, flat_bias(bias_ref[...]), scale_ref[...])
    small_ref[16:32, 2 * LEN : 3 * LEN] = packed(gain_mom_ref[...], flat_bias(bias_mom_ref[...]), scale_mom_ref[...])

    for k in range(lines):
        for d in cells[::-1]:
            _, (other_wide, other_narrow) = spot_device(d)
            block = (line_order[k] * 2 + other_wide % 2) * n_narrow + other_narrow
            await_block(block)
            send_block(block, sibling, sibling_recv)
    bytes_of(gather, count // 2, sibling_recv).wait()

    blocks = count // GROUP
    temper = jnp.exp(scale_ref[...])

    def unpack(b, total):
        picked = gather[pl.ds(b * GROUP, GROUP), :, D:PACK].astype(F32)
        left = picked[:, 0:8, :].reshape(GROUP * 8, HALF)
        right = picked[:, 8:16, :].reshape(GROUP * 8, HALF)
        anchors_all[b] = jnp.concatenate([left, right], axis=1).astype(BF16)
        live = jnp.where(left[:, 0:1] < 1.5, 1.0, 0.0)
        return total + jnp.sum(live, axis=0, keepdims=True)

    live_total = looped(blocks, unpack, jnp.zeros((1, 1), F32))

    def cands_of(b):
        return gather[pl.ds(b * GROUP, GROUP), :, 0:D].reshape(GROUP * 16, D)

    first_lane = jnp.where(lax.broadcasted_iota(jnp.int32, (16, D), 1) == 0, 1.0, 0.0).astype(BF16)
    row16 = lax.broadcasted_iota(jnp.int32, (16, GROUP * 8), 0)
    lane16 = lax.broadcasted_iota(jnp.int32, (16, GROUP * 8), 1)
    per_live = 1.0 / live_total

    def columns(b, cand_grad):
        anchors = anchors_all[b]

        def part(c, state):
            top, total = state
            logits = temper * nt(cands_of(c), anchors)
            new_top = jnp.maximum(top, jnp.max(logits, axis=0, keepdims=True))
            total = total * jnp.exp(top - new_top) + jnp.sum(
                jnp.exp(logits - new_top), axis=0, keepdims=True
            )
            return new_top, total

        start = (jnp.full((1, GROUP * 8), -1e30, F32), jnp.zeros((1, GROUP * 8), F32))
        top, total = looped(blocks, part, start)
        log_total = top + jnp.log(total)
        live = jnp.where(nt(first_lane, anchors) < 1.5, per_live, 0.0)
        logits = temper * nt(own_cands, anchors)
        target = jnp.where(
            (row16 < 8) & (lane16 + b * (GROUP * 8) == row16 + me * ROWS_DEV), 1.0, 0.0
        )
        grad = (jnp.exp(logits - log_total) - target) * live
        return cand_grad + nn((temper * grad).astype(BF16), anchors)

    cand_grad = looped(blocks, columns, jnp.zeros((16, D), F32))

    def own_part(b, state):
        top, total = state
        logits = temper * nt(own_anchors, cands_of(b))
        own_scores[b] = logits
        new_top = jnp.maximum(top, jnp.max(logits, axis=1, keepdims=True))
        total = total * jnp.exp(top - new_top) + jnp.sum(
            jnp.exp(logits - new_top), axis=1, keepdims=True
        )
        return new_top, total

    start = (jnp.full((16, 1), -1e30, F32), jnp.zeros((16, 1), F32))
    top, total = looped(blocks, own_part, start)
    log_total = top + jnp.log(total)
    live16 = jnp.concatenate([live_own, jnp.zeros_like(live_own)], axis=0)
    row32 = lax.broadcasted_iota(jnp.int32, (16, GROUP * 16), 0)
    lane32 = lax.broadcasted_iota(jnp.int32, (16, GROUP * 16), 1)

    def own_grad(b, state):
        anchor_grad, positive, scale_grad = state
        logits = own_scores[b]
        target = jnp.where(
            (row32 < 8) & (lane32 + b * (GROUP * 16) == row32 + me * 2 * ROWS_DEV), 1.0, 0.0
        )
        positive = positive + jnp.sum(logits * target, axis=1, keepdims=True)
        grad = (jnp.exp(logits - log_total) - target) * (live16 * per_live)
        scale_grad = scale_grad + jnp.sum(grad * logits, axis=1, keepdims=True)
        anchor_grad = anchor_grad + nn((temper * grad).astype(BF16), cands_of(b))
        return anchor_grad, positive, scale_grad

    column = jnp.zeros((16, 1), F32)
    anchor_grad, positive, scale_grad = looped(
        blocks, own_grad, (jnp.zeros((16, D), F32), column, column)
    )
    loss_own = jnp.sum(live16 * (log_total - positive), axis=0, keepdims=True)
    scale_grad = jnp.sum(scale_grad, axis=0, keepdims=True)

    branch, mixed_grad = resid, zed_low
    unit_grad = jnp.concatenate([anchor_grad[0:8], cand_grad], axis=0)
    mean_grad = inverse * (unit_grad - unit * jnp.sum(unit * unit_grad, axis=1, keepdims=True))
    gain_grad = jnp.sum(mean_grad * zed_mean, axis=0, keepdims=True)
    high, middle, low = parts_of(mean_grad / counts * gain)
    wide_gap = jnp.zeros((8, D), F32)
    shares = jnp.concatenate(
        [high, wide_gap, middle, wide_gap, low, wide_gap, jnp.zeros((32, D), F32)], axis=0
    ).astype(BF16)
    wide_rows[...] = nn(member_t[...], shares)
    for b in range(TOK // 32):
        rows = slice(b * 32, (b + 1) * 32)
        zed_grad = wide_rows[rows, :]
        zed_rows = zed[rows, :]
        level = jnp.sum(zed_grad * zed_rows, axis=1, keepdims=True) * (1.0 / D)
        branch[rows, :] = (rms_inv[rows, :] * (zed_grad - zed_rows * level)).astype(BF16)
    by_token = folded(nt(factor_parts, branch[...]), RANK)
    row_part = row_part + folded(nt(stacked_parts(by_token), mixed_t[...]), RANK)

    def exchange(buffers, mine, devices, send_sem, recv_sem):
        for device in devices:
            pltpu.make_async_remote_copy(
                src_ref=buffers.at[mine],
                dst_ref=buffers.at[mine],
                send_sem=send_sem,
                recv_sem=recv_sem,
                device_id=device,
                device_id_type=MESH,
            ).start()

    def start_sum(which, plane):
        devices = [spot_device(d)[1] for d in offsets]
        exchange(plane, spot, devices, plane_send.at[which], plane_recv.at[which])

    def middle_sum(which, plane, along):
        bytes_of(plane, spots - 1, plane_recv.at[which]).wait()
        total = plane[0]
        for k in range(1, spots):
            total = total + plane[k]
        along[line] = total
        devices = [line_device(k)[1] for k in far_lines]
        exchange(along, line, devices, line_send.at[which], line_recv.at[which])

    def finish_sum(which, along):
        bytes_of(along, lines - 1, line_recv.at[which]).wait()
        total = along[0]
        for k in range(1, lines):
            total = total + along[k]
        return total

    scalars = jnp.where(lane == 0, loss_own, jnp.where(lane == 1, scale_grad, 0.0))
    extra = jnp.concatenate(
        [gain_grad[:, k * LEN : (k + 1) * LEN] for k in range(6)]
        + [scalars, jnp.zeros((1, LEN), F32)],
        axis=0,
    )
    plane1[spot, :, 0:D] = row_part
    plane1[spot, :, D:WIDTH] = extra
    start_sum(0, plane1)

    for b in range(3):
        rows = slice(b * 256, (b + 1) * 256)
        full = error[rows, :] + nn(mixed_t[rows, :], branch[...])
        matrix[rows, :] = full
        high = full.astype(BF16)
        matrix_high[rows, :] = high
        rest = full - high.astype(F32)
        low = rest.astype(BF16)
        matrix_low[rows, :] = low
        matrix_rest[rows, :] = (rest - low.astype(F32)).astype(BF16)
    matrix_copy = pltpu.make_async_copy(matrix, matrix_hbm, out_sem)
    matrix_copy.start()

    for c in range(4):
        rows = slice(c * 256, (c + 1) * 256)
        mixed_grad[rows, :] = nt(branch[rows, :], weight_low[...]).astype(BF16)
    middle_sum(0, plane1, line1)
    for p in range(PAIRS):
        cols = slice(p * LEN, (p + 1) * LEN)

        def back(r, acc):
            offset = pl.multiple_of(r * LEN, LEN)
            rows = pl.ds(offset, LEN)
            grad = mixed_grad[rows, cols]
            right = jnp.concatenate([grad * first, grad * second], axis=0)
            prob_grad = nt(proj[2, rows, cols], right)
            prob = jnp.concatenate(
                [probs[r * HEADS + 2 * p], probs[r * HEADS + 2 * p + 1]], axis=1
            )
            product = prob * prob_grad
            return acc + (product - prob * jnp.sum(product, axis=0, keepdims=True))

        acc = lax.fori_loop(0, ROWS_DEV, back, jnp.zeros((LEN, 2 * LEN), F32), unroll=True)
        for half in range(2):
            padded = jnp.concatenate(
                [acc[:, half * LEN : (half + 1) * LEN], jnp.zeros((LEN, LEN), F32)], axis=1
            )
            sheared = padded[0:8]
            for a in range(1, LEN // 8):
                sheared = sheared + pltpu.roll(padded[8 * a : 8 * a + 8], 2 * LEN - 8 * a, 1)
            for bit in (1, 2, 4):
                moved = pltpu.roll(sheared, 2 * LEN - bit, 1)
                sheared = jnp.where((row8 & bit) != 0, moved, sheared)
            head = 2 * p + half
            diagonals[head : head + 1, :] = jnp.sum(sheared, axis=0, keepdims=True)
    diagonals[HEADS:16, :] = jnp.zeros((16 - HEADS, 2 * LEN), F32)
    high, middle, low = parts_of(diagonals[...])
    by_bucket = folded(
        nn(jnp.concatenate([high, middle, low], axis=0).astype(BF16), onehot_ref[...]), 16
    )
    bias_grad = jnp.sum(by_bucket * head_mask_ref[...], axis=0, keepdims=True)

    total = finish_sum(0, line1)
    small_ref[16:24, 0:LEN] = total[:, D:WIDTH]
    ortho = total[:, 0:D]
    row_parts = stacked_parts(ortho)
    product = folded(
        nn(row_parts, matrix_high[...])
        + nn(row_parts, matrix_low[...])
        + nn(row_parts, matrix_rest[...]),
        RANK,
    )
    rank_row = lax.broadcasted_iota(jnp.int32, (RANK, 1), 0)
    weights = []
    for k in range(RANK):
        vector = ortho[k : k + 1, :]
        dots = jnp.sum(ortho * vector, axis=1, keepdims=True)
        norm = lax.rsqrt(dots[k : k + 1, :] + EPSILON)
        vector = vector * norm
        weight_k = jnp.where(rank_row > k, dots * norm, 0.0)
        ortho = jnp.where(rank_row == k, vector, ortho - weight_k * vector)
        weights.append((norm, weight_k))
    for k, (norm, weight_k) in enumerate(weights):
        vector = product[k : k + 1, :] * norm
        product = jnp.where(rank_row == k, vector, product - weight_k * vector)
    small_ref[0:8, :] = ortho
    plane2[spot, :, 0:D] = product
    plane2[spot, :, D:WIDTH] = jnp.concatenate(
        [bias_grad[:, k * LEN : (k + 1) * LEN] for k in range(3)] + [jnp.zeros((5, LEN), F32)],
        axis=0,
    )
    start_sum(1, plane2)
    bytes_of(gather, len(sends), gather_send).wait()
    bytes_of(plane1, spots - 1, plane_send.at[0]).wait()
    bytes_of(line1, lines - 1, line_send.at[0]).wait()
    matrix_copy.wait()
    for copy in keep_copies:
        copy.wait()
    middle_sum(1, plane2, line2)
    total = finish_sum(1, line2)
    small_ref[8:16, :] = total[:, 0:D]
    small_ref[24:32, 0:LEN] = total[:, D:WIDTH]
    small_ref[16:32, 3 * LEN : 4 * LEN] = jnp.broadcast_to(live_total, (16, LEN))
    small_ref[16:32, 4 * LEN : D] = jnp.zeros((16, D - 4 * LEN), F32)
    bytes_of(plane2, spots - 1, plane_send.at[1]).wait()
    bytes_of(line2, lines - 1, line_send.at[1]).wait()


def update_kernel(
    count,
    small_ref,
    matrix_ref,
    weight_ref,
    momentum_ref,
    weight_out,
    momentum_out,
    error_out,
    vector_out,
    vector_mom_out,
    loss_out,
    norm_out,
    fnew_out,
    live_out,
    matrix,
    weight,
    momentum,
    store_sem,
):
    ortho = small_ref[0:8, :]
    fnew = small_ref[8:16, :]
    oh, om, ol = parts_of(ortho)
    fh, fm, fl = parts_of(fnew)
    pad = jnp.zeros((16, D), F32)
    left = jnp.concatenate([oh, oh, om, om, oh, ol, pad], axis=0).astype(BF16)
    right = jnp.concatenate([fh, fm, fh, fm, fl, fh, pad], axis=0).astype(BF16)
    copies = []

    def send_out(source, target, rows, sem):
        copy = pltpu.make_async_copy(source.at[rows, :], target.at[rows, :], sem)
        copy.start()
        copies.append(copy)

    for b in range(6):
        rows = slice(b * LEN, (b + 1) * LEN)
        approx = tn(left[:, rows], right)
        weight[rows, :] = approx
        matrix[rows, :] = matrix_ref[rows, :] - approx * (1.0 / count)
        send_out(matrix, error_out.at[0], rows, store_sem.at[b, 2])

    square = jnp.zeros((RANK, 1), F32)
    for k in range(RANK):
        left = jnp.sum(ortho * ortho[k : k + 1, :], axis=1, keepdims=True)
        right = jnp.sum(fnew * fnew[k : k + 1, :], axis=1, keepdims=True)
        square = square + left * right
    square = jnp.sum(square, axis=0, keepdims=True)
    vec = small_ref[16:32, 0:LEN]
    lane = lax.broadcasted_iota(jnp.int32, (1, LEN), 1)
    scale_row = jnp.where(lane == 0, vec[6:7, 1:2], 0.0)
    grad = jnp.concatenate(
        [vec[0:6], vec[8:11], scale_row, jnp.zeros((6, LEN), F32)], axis=0
    )
    square = square + jnp.sum(
        jnp.sum(grad * grad, axis=1, keepdims=True), axis=0, keepdims=True
    )
    norm = jnp.sqrt(square)
    clip = CLIP_NORM / jnp.maximum(norm, CLIP_NORM)

    for b in range(6):
        rows = slice(b * LEN, (b + 1) * LEN)
        mom = MOMENTUM_DECAY * momentum_ref[rows, :] + clip * weight[rows, :]
        momentum[rows, :] = mom
        send_out(momentum, momentum_out, rows, store_sem.at[b, 0])
        weight[rows, :] = weight_ref[rows, :] - RATE_MATRIX * mom
        send_out(weight, weight_out, rows, store_sem.at[b, 1])

    row = lax.broadcasted_iota(jnp.int32, (16, 1), 0)
    rate = jnp.where(row < 6, RATE_GAIN, jnp.where(row < 9, RATE_BIAS, RATE_SCALE))
    mom = MOMENTUM_DECAY * small_ref[16:32, 2 * LEN : 3 * LEN] + clip * grad
    vector_mom_out[...] = mom
    vector_out[...] = small_ref[16:32, LEN : 2 * LEN] - rate * mom
    loss_out[...] = vec[6:7, 0:1]
    norm_out[...] = norm
    fnew_out[...] = fnew
    live_out[...] = small_ref[16:17, 3 * LEN : 3 * LEN + 1]
    for copy in copies:
        copy.wait()


def local(
    n_wide,
    n_narrow,
    projected,
    layer_input,
    segment_ids,
    pad_mask,
    roles,
    labelled,
    out_weight,
    out_momentum,
    errors,
    factors,
    norm_gain,
    position_bias,
    log_scale,
    gain_momentum,
    bias_momentum,
    scale_momentum,
):
    count = n_wide * n_narrow
    lines = n_wide // 2
    spots = 2 * n_narrow
    blocks = count // GROUP
    anywhere = pl.BlockSpec(memory_space=pl.ANY)
    vmem = pl.BlockSpec(memory_space=pltpu.VMEM)

    def stay(x):
        return pltpu.with_memory_space_constraint(x, pltpu.HBM)

    in_hbm = pl.BlockSpec(memory_space=pltpu.HBM)
    kept = pl.pallas_call(
        functools.partial(step_kernel, n_wide, n_narrow),
        out_shape=(
            jax.ShapeDtypeStruct((32, D), F32),
            jax.ShapeDtypeStruct((D, D), F32),
            jax.ShapeDtypeStruct((D, D), F32),
            jax.ShapeDtypeStruct((D, D), F32),
        ),
        in_specs=[in_hbm] * 20,
        out_specs=(vmem, anywhere, anywhere, anywhere),
        scratch_shapes=[
            pltpu.VMEM((ROWS_DEV, LEN), jnp.int32),
            pltpu.VMEM((ROWS_DEV, LEN), jnp.int32),
            pltpu.VMEM((3, ROWS_DEV), jnp.int32),
            pltpu.VMEM((1, ROWS_DEV), jnp.int32),
            pltpu.VMEM((RANK, D), F32),
            pltpu.VMEM((6, LEN), F32),
            pltpu.VMEM((6, LEN), F32),
            pltpu.VMEM((HEADS, BUCKETS), F32),
            pltpu.VMEM((HEADS, BUCKETS), F32),
            pltpu.VMEM((1, 1), F32),
            pltpu.VMEM((1, 1), F32),
            pltpu.VMEM((2 * LEN, FLAT), BF16),
            pltpu.VMEM((BUCKETS, FLAT), BF16),
            pltpu.VMEM((2 * LEN, BUCKETS), BF16),
            pltpu.VMEM((16, FLAT), F32),
            pltpu.SemaphoreType.DMA((15,)),
            pltpu.VMEM((3, TOK, D), BF16),
            pltpu.VMEM((TOK, D), BF16),
            pltpu.VMEM((D, D), F32),
            pltpu.VMEM((D, D), F32),
            pltpu.VMEM((D, D), BF16),
            pltpu.VMEM((HEADS, LEN, LEN), F32),
            pltpu.VMEM((ROWS_DEV, LEN, LEN), BF16),
            pltpu.VMEM((ROWS_DEV, LEN, LEN), BF16),
            pltpu.VMEM((32, TOK), BF16),
            pltpu.VMEM((TOK, LEN), BF16),
            pltpu.VMEM((ROWS_DEV * HEADS, LEN, LEN), F32),
            pltpu.VMEM((PAIRS, LEN, 2 * LEN), F32),
            pltpu.VMEM((PAIRS, LEN, 2 * LEN), F32),
            pltpu.VMEM((PAIRS, 2 * LEN, LEN), BF16),
            pltpu.VMEM((PAIRS, 2 * LEN, LEN), BF16),
            pltpu.VMEM((D, TOK), BF16),
            pltpu.VMEM((TOK, D), F32),
            pltpu.VMEM((TOK, D), F32),
            pltpu.VMEM((TOK, D), BF16),
            pltpu.VMEM((TOK, D), BF16),
            pltpu.VMEM((TOK, 1), F32),
            pltpu.VMEM((TOK, 1), F32),
            pltpu.VMEM((D, D), F32),
            pltpu.VMEM((D, D), BF16),
            pltpu.VMEM((D, D), BF16),
            pltpu.VMEM((D, D), BF16),
            pltpu.VMEM((count, 16, PACK), BF16),
            pltpu.VMEM((blocks, GROUP * 8, D), BF16),
            pltpu.VMEM((blocks, 16, GROUP * 16), F32),
            pltpu.VMEM((16, 2 * LEN), F32),
            pltpu.VMEM((spots, RANK, WIDTH), F32),
            pltpu.VMEM((lines, RANK, WIDTH), F32),
            pltpu.VMEM((spots, RANK, WIDTH), F32),
            pltpu.VMEM((lines, RANK, WIDTH), F32),
            pltpu.SemaphoreType.DMA((2,)),
            pltpu.SemaphoreType.DMA,
            pltpu.SemaphoreType.DMA((4,)),
            pltpu.SemaphoreType.DMA,
            pltpu.SemaphoreType.DMA,
            pltpu.SemaphoreType.DMA((count // 2,)),
            pltpu.SemaphoreType.DMA,
            pltpu.SemaphoreType.DMA((2,)),
            pltpu.SemaphoreType.DMA((2,)),
            pltpu.SemaphoreType.DMA((2,)),
            pltpu.SemaphoreType.DMA((2,)),
        ],
        compiler_params=pltpu.CompilerParams(
            collective_id=0, has_side_effects=True, vmem_limit_bytes=(45 if blocks == 1 else 60) * 2**20
        ),
        name="step",
    )(
        stay(projected),
        stay(layer_input),
        stay(out_weight),
        stay(errors),
        stay(out_momentum),
        stay(segment_ids.reshape(ROWS_DEV, LEN)),
        stay(pad_mask.reshape(ROWS_DEV, LEN)),
        stay(roles.T),
        stay(labelled.reshape(1, ROWS_DEV)),
        stay(factors),
        stay(norm_gain.reshape(6, LEN)),
        stay(gain_momentum.reshape(6, LEN)),
        stay(position_bias.T),
        stay(bias_momentum.T),
        log_scale.reshape(1, 1),
        scale_momentum.reshape(1, 1),
        stay(jnp.asarray(diagonal_onehot(FLAT), BF16)),
        stay(jnp.asarray(bucket_spread(), BF16)),
        stay(jnp.asarray(diagonal_onehot(BUCKETS), BF16)),
        stay(jnp.asarray(head_mask())),
    )
    outs = pl.pallas_call(
        functools.partial(update_kernel, count),
        out_shape=(
            jax.ShapeDtypeStruct((D, D), F32),
            jax.ShapeDtypeStruct((D, D), F32),
            jax.ShapeDtypeStruct((1, D, D), F32),
            jax.ShapeDtypeStruct((16, LEN), F32),
            jax.ShapeDtypeStruct((16, LEN), F32),
            jax.ShapeDtypeStruct((1, 1), F32),
            jax.ShapeDtypeStruct((1, 1), F32),
            jax.ShapeDtypeStruct((RANK, D), F32),
            jax.ShapeDtypeStruct((1, 1), F32),
        ),
        in_specs=[vmem] * 4,
        out_specs=(anywhere,) * 3 + (vmem,) * 6,
        scratch_shapes=[
            pltpu.VMEM((D, D), F32),
            pltpu.VMEM((D, D), F32),
            pltpu.VMEM((D, D), F32),
            pltpu.SemaphoreType.DMA((6, 3)),
        ],
        compiler_params=pltpu.CompilerParams(vmem_limit_bytes=24 * 2**20),
        name="update",
    )(*kept)
    weight_new, weight_mom, errors_new, vec_new, vec_mom, loss, norm, fnew, live_total = outs
    size = D + FLAT + 1
    return (
        weight_new,
        weight_mom,
        errors_new,
        fnew,
        vec_new.reshape(-1)[:size],
        vec_mom.reshape(-1)[:size],
        loss.reshape(1),
        live_total.reshape(1),
        norm.reshape(1),
    )


def solution(mesh):
    both = ("wide", "narrow")
    in_specs = (
        P(None, both, None),
        P(both, None),
        P(both),
        P(both),
        P(both, None),
        P(both),
        P(),
        P(),
        P(both, None, None),
        P(),
        P(),
        P(),
        P(),
        P(),
        P(),
        P(),
    )
    out_specs = (P(), P(), P(both, None, None), P(), P(), P(), P(), P(), P())
    return jax.shard_map(
        functools.partial(local, mesh.shape["wide"], mesh.shape["narrow"]),
        mesh=mesh,
        in_specs=in_specs,
        out_specs=out_specs,
        check_vma=False,
    )
```
